32 devices in a mesh: dp: 8 (over z, x), seq: 4 (over y, core).
Axes of the slice: x: 2, y: 2, z: 4, core: 2. Of those that a mesh axis runs over, the one named last changes fastest.
Arguments:
- latents: bfloat16 [2, 8, 1024, 1024], P(None, 'dp', 'seq'), may hold values from -6 to 6
- conditioning: bfloat16 [2, 8, 1024], P(None, 'dp'), may hold values from -6 to 6
- w_mod: bfloat16 [1, 1024, 6144], P(None, ('dp', 'seq')), may hold values from -0.1875 to 0.1875
- b_mod: bfloat16 [1, 6144], P(None, ('dp', 'seq')), may hold values from -3 to 3
- w_qkv: bfloat16 [1, 1024, 3072], P(None, ('dp', 'seq')), may hold values from -0.1875 to 0.1875
- b_qv: bfloat16 [1, 2048], P(None, ('dp', 'seq')), may hold values from -3 to 3
- w_out: bfloat16 [1, 1024, 1024], P(None, ('dp', 'seq')), may hold values from -3.5 to 3.5
- b_out: bfloat16 [1, 1024], P(None, ('dp', 'seq')), may hold values from -3 to 3
- w_up: bfloat16 [1, 1024, 4096], P(None, ('dp', 'seq')), may hold values from -0.1875 to 0.1875
- b_up: bfloat16 [1, 4096], P(None, ('dp', 'seq')), may hold values from -3 to 3
- w_down: bfloat16 [1, 4096, 1024], P(None, ('dp', 'seq')), may hold values from -0.09375 to 0.09375
- b_down: bfloat16 [1, 1024], P(None, ('dp', 'seq')), may hold values from -3 to 3
- cotangent: bfloat16 [2, 8, 1024, 1024], P(None, 'dp', 'seq'), may hold values from -6 to 6
Outputs:
- output: bfloat16 [2, 8, 1024, 1024], P(None, 'dp', 'seq')
- grad_latents: float32 [2, 8, 1024, 1024], P(None, 'dp', 'seq')
- grad_cond: float32 [2, 8, 1024], P(None, 'dp')
- grad_w_mod: float32 [1, 1024, 6144], P(None, ('dp', 'seq'))
- grad_b_mod: float32 [1, 6144], P(None, ('dp', 'seq'))
- grad_w_qkv: float32 [1, 1024, 3072], P(None, ('dp', 'seq'))
- grad_b_qv: float32 [1, 2048], P(None, ('dp', 'seq'))
- grad_w_out: float32 [1, 1024, 1024], P(None, ('dp', 'seq'))
- grad_b_out: float32 [1, 1024], P(None, ('dp', 'seq'))
- grad_w_up: float32 [1, 1024, 4096], P(None, ('dp', 'seq'))
- grad_b_up: float32 [1, 4096], P(None, ('dp', 'seq'))
- grad_w_down: float32 [1, 4096, 1024], P(None, ('dp', 'seq'))
- grad_b_down: float32 [1, 1024], P(None, ('dp', 'seq'))
The draws below stay inside these ranges and needn't reach their ends.
All inputs are finite; a program needn't handle non-finite values.
Results may differ from the reference program's by a relative error of at most 0.013.
The reference program's roundings to bfloat16 on the way count: a program that leaves them out, or rounds other values in their place, can miss the bound.
Values may be sent and summed in bfloat16 or wider, within the bound.
A program may use at most 320 MiB of HBM per device.

```python
import math
import jax
import jax.numpy as jnp
from jax import lax

D = 1024
HEADS = 16
FF = 4096
TOK_DEV = 256
LAYERS = 1
MICRO = 2
COND = 1024
LENGTH = 1024
LATENTS = 8
N_SEQ = 4


def levels(rng, dims, shards, low, high):
    factor_of, own = 1.0, jax.random.fold_in(rng, 6)
    for position, parts in shards:
        heights = jnp.exp(jax.random.uniform(jax.random.fold_in(own, position), (parts,), jnp.float32, low / len(shards), high / len(shards)))
        factor_of = factor_of * jnp.repeat(heights, dims[position] // parts).reshape([-1 if axis == position else 1 for axis in range(len(dims))])
    return factor_of


def noise(rng, extent, spread, bound, cuts=(), kind=jnp.bfloat16):
    gain = levels(rng, extent, cuts, -0.22, 0.18) if cuts else 1.0
    values = jax.random.normal(rng, extent, jnp.float32) * spread * gain
    return jnp.minimum(jnp.maximum(values, -bound), bound).astype(kind)


def setup_inputs(seed: int = 0) -> dict:
    streams_of = jax.random.split(jax.random.key(seed), 14)
    return {
        "latents": noise(streams_of[0], (MICRO, LATENTS, LENGTH, D), 1.0, 6.0, ((1, 8), (2, 4))),
        "conditioning": noise(streams_of[1], (MICRO, LATENTS, COND), 1.0, 6.0, ((1, 8),)),
        "w_mod": noise(streams_of[2], (LAYERS, COND, 6 * D), COND ** -0.5, 0.1875, ((1, 32),)),
        "b_mod": noise(streams_of[3], (LAYERS, 6 * D), 0.5, 3.0, ((1, 32),)),
        "w_qkv": noise(streams_of[4], (LAYERS, D, 3 * D), D ** -0.5, 0.1875, ((1, 32),)),
        "b_qv": noise(streams_of[5], (LAYERS, 2 * D), 0.5, 3.0, ((1, 32),)),
        "w_out": noise(streams_of[6], (LAYERS, D, D), (max(1, 3 * D // (TOK_DEV * N_SEQ))) ** -0.5, 3.5, ((1, 32),)),
        "b_out": noise(streams_of[7], (LAYERS, D), 0.5, 3.0, ((1, 32),)),
        "w_up": noise(streams_of[8], (LAYERS, D, FF), D ** -0.5, 0.1875, ((1, 32),)),
        "b_up": noise(streams_of[9], (LAYERS, FF), 0.5, 3.0, ((1, 32),)),
        "w_down": noise(streams_of[10], (LAYERS, FF, D), FF ** -0.5, 0.09375, ((1, 32),)),
        "b_down": noise(streams_of[11], (LAYERS, D), 0.5, 3.0, ((1, 32),)),
        "cotangent": noise(streams_of[12], (MICRO, LATENTS, LENGTH, D), 1.0, 6.0, ((1, 8), (2, 4))),
    }


EPS = 1e-06
HIGH = lax.Precision.HIGHEST

@jax.custom_vjp
def low(v):
    return lax.optimization_barrier(v.astype(jnp.bfloat16)).astype(jnp.float32)

@jax.custom_vjp
def low_back(v):
    return v

def low_keep(v):
    return (low(v), None)

def low_pass(kept, grad):
    return (grad,)

def back_keep(v):
    return (v, None)

def back_low(kept, grad):
    return (low(grad),)
low.defvjp(low_keep, low_pass)
low_back.defvjp(back_keep, back_low)

def matmul(left, right):
    return jnp.dot(left, right, precision=HIGH)

def modulate(stream, shift_vec, scale_vec):
    row_mean = lax.optimization_barrier(jnp.mean(stream, -1, keepdims=True))
    centred = stream - row_mean
    row_var = lax.optimization_barrier(jnp.mean(centred * centred, -1, keepdims=True))
    return centred * lax.rsqrt(row_var + EPS) * (1.0 + scale_vec) + shift_vec

def attention(query, keys, values):
    block_rows = math.gcd(LENGTH, 512)
    head_size = D // HEADS
    query_blocks = query.reshape(LENGTH // block_rows, block_rows, HEADS, head_size)
    key_rows = keys.reshape(LENGTH, HEADS, head_size)
    value_rows = values.reshape(LENGTH, HEADS, head_size)

    def one_block(query_rows):
        scores = low_back(jnp.einsum('qhd,khd->hqk', query_rows, key_rows, precision=HIGH) * head_size ** (-0.5))
        probs = low(jax.nn.softmax(scores, axis=-1))
        return jnp.einsum('hqk,khd->qhd', probs, value_rows, precision=HIGH)
    attended = lax.map(jax.checkpoint(one_block), query_blocks)
    return attended.reshape(LENGTH, D)

def layer(stream, cond_act, params):
    w_mod, b_mod, w_qkv, b_qv, w_out, b_out, w_up, b_up, w_down, b_down = params
    modulation = low_back(matmul(cond_act[None], w_mod)[0] + b_mod)
    shift_attn, scale_attn, gate_attn, shift_mlp, scale_mlp, gate_mlp = jnp.split(modulation, 6)
    mixed1 = low(modulate(stream, shift_attn, scale_attn))
    qkv = matmul(mixed1, w_qkv)
    query = low(low_back(qkv[:, :D] + b_qv[:D]))
    keys = low(low_back(qkv[:, D:2 * D]))
    values = low(low_back(qkv[:, 2 * D:] + b_qv[D:]))
    attended = low(low_back(attention(query, keys, values)))
    attn_out = low_back(matmul(attended, w_out) + b_out)
    resid = stream + gate_attn * attn_out
    mixed2 = low(modulate(resid, shift_mlp, scale_mlp))
    preact = low_back(matmul(mixed2, w_up) + b_up)
    activation = low(jax.nn.gelu(preact, approximate=True))
    branch = low_back(matmul(activation, w_down) + b_down)
    return resid + gate_mlp * branch

def forward(stream, cond_row, params):
    cond_act = low(jax.nn.silu(cond_row))
    for layer_index in range(LAYERS):
        stream = layer(stream, cond_act, tuple((weight[layer_index] for weight in params)))
    return stream

def reference(latents, conditioning, w_mod, b_mod, w_qkv, b_qv, w_out, b_out, w_up, b_up, w_down, b_down, cotangent):
    params = tuple((weight.astype(jnp.float32) for weight in (w_mod, b_mod, w_qkv, b_qv, w_out, b_out, w_up, b_up, w_down, b_down)))
    streams = latents.reshape(MICRO * LATENTS, LENGTH, D)
    cond_rows = conditioning.reshape(MICRO * LATENTS, COND)
    targets = cotangent.reshape(MICRO * LATENTS, LENGTH, D)

    def one_latent(totals, sample):
        stream, cond_row, target = sample
        result, pullback = jax.vjp(forward, stream.astype(jnp.float32), cond_row.astype(jnp.float32), params)
        grad_stream, grad_row, grad_params = pullback(target.astype(jnp.float32))
        totals = jax.tree.map(jnp.add, totals, grad_params)
        return (totals, (result.astype(jnp.bfloat16), grad_stream, grad_row))
    zeros = tuple((jnp.zeros_like(weight) for weight in params))
    totals, (results, grads_in, grads_cond) = lax.scan(one_latent, zeros, (streams, cond_rows, targets))
    return (results.reshape(latents.shape), grads_in.reshape(latents.shape), grads_cond.reshape(conditioning.shape), totals[0], totals[1], totals[2], totals[3], totals[4], totals[5], totals[6], totals[7], totals[8], totals[9])
```

```python
import jax
import jax.numpy as jnp
from jax import lax
from jax.sharding import PartitionSpec as P
from jax.experimental import pallas as pl
from jax.experimental.pallas import tpu as pltpu

EPS = 1e-06
HEADS = 16


def modulate(stream, shift_vec, scale_vec):
    row_mean = jnp.mean(stream, -1, keepdims=True)
    centred = stream - row_mean
    row_var = jnp.mean(centred * centred, -1, keepdims=True)
    return centred * lax.rsqrt(row_var + EPS) * (1.0 + scale_vec) + shift_vec


def gelu_tanh(values):
    return jax.nn.gelu(values, approximate=True)


def matmul(left, right):
    return jnp.dot(left, right, preferred_element_type=jnp.float32)


def weight_grad(inputs, upstream):
    return jnp.einsum("ti,to->io", inputs, upstream, preferred_element_type=jnp.float32)


def input_grad(upstream, weight):
    return jnp.einsum("to,io->ti", upstream, weight, preferred_element_type=jnp.float32)


def column_sums(values):
    return jnp.sum(values.astype(jnp.float32), 0)


def gather_once(params, layer_index):
    return (
        lax.all_gather(params[0][layer_index], ("dp", "seq"), axis=0, tiled=True),
        lax.all_gather(params[1][layer_index], ("dp", "seq"), axis=0, tiled=True),
        lax.all_gather(params[2][layer_index], ("dp", "seq"), axis=0, tiled=True),
        lax.all_gather(params[3][layer_index], ("dp", "seq"), axis=0, tiled=True),
        lax.all_gather(params[4][layer_index], ("dp", "seq"), axis=0, tiled=True),
        lax.all_gather(params[5][layer_index], ("dp", "seq"), axis=0, tiled=True),
        lax.all_gather(params[6][layer_index], ("dp", "seq"), axis=0, tiled=True),
        lax.all_gather(params[7][layer_index], ("dp", "seq"), axis=0, tiled=True),
        lax.all_gather(params[8][layer_index], ("dp", "seq"), axis=0, tiled=True),
        lax.all_gather(params[9][layer_index], ("dp", "seq"), axis=0, tiled=True),
    )


def owner_layout(grad, dp_count, seq_count):
    per_owner = grad.shape[1] // (dp_count * seq_count)
    shaped = grad.reshape((grad.shape[0], dp_count, seq_count, per_owner) + grad.shape[2:])
    return jnp.moveaxis(shaped, 0, 2)


def attend(query, keys, values):
    head_size = query.shape[1] // HEADS
    query_rows = query.reshape(query.shape[0], HEADS, head_size)
    key_rows = keys.reshape(keys.shape[0], HEADS, head_size)
    value_rows = values.reshape(values.shape[0], HEADS, head_size)
    scores = jnp.einsum(
        "qhd,khd->hqk", query_rows, key_rows, preferred_element_type=jnp.float32
    ) * head_size ** (-0.5)
    row_max = jnp.max(scores, -1, keepdims=True)
    expon = jnp.exp(scores - row_max)
    row_sum = jnp.sum(expon, -1, keepdims=True)
    probs_low = (expon / row_sum).astype(jnp.bfloat16)
    attended = jnp.einsum("hqk,khd->qhd", probs_low, value_rows, preferred_element_type=jnp.float32)
    return (attended.reshape(query.shape[0], -1).astype(jnp.bfloat16), row_max + jnp.log(row_sum))


def attend_back(query, keys, values, log_total, grad_attended):
    head_size = query.shape[1] // HEADS
    inv_root = head_size ** (-0.5)
    query_rows = query.reshape(query.shape[0], HEADS, head_size)
    key_rows = keys.reshape(keys.shape[0], HEADS, head_size)
    value_rows = values.reshape(values.shape[0], HEADS, head_size)
    grad_rows = grad_attended.reshape(query.shape[0], HEADS, head_size)
    scores = (
        jnp.einsum("qhd,khd->hqk", query_rows, key_rows, preferred_element_type=jnp.float32)
        * inv_root
    )
    probs = jnp.exp(scores - log_total)
    grad_probs = jnp.einsum(
        "qhd,khd->hqk", grad_rows, value_rows, preferred_element_type=jnp.float32
    )
    row_dot = jnp.sum(probs * grad_probs, -1, keepdims=True)
    grad_scores = (probs * (grad_probs - row_dot)).astype(jnp.bfloat16)
    grad_query = (
        jnp.einsum("hqk,khd->qhd", grad_scores, key_rows, preferred_element_type=jnp.float32)
        * inv_root
    )
    grad_keys = (
        jnp.einsum("hqk,qhd->khd", grad_scores, query_rows, preferred_element_type=jnp.float32)
        * inv_root
    )
    grad_values = jnp.einsum(
        "hqk,qhd->khd", probs.astype(jnp.bfloat16), grad_rows, preferred_element_type=jnp.float32
    )
    return (
        grad_query.reshape(query.shape[0], -1),
        grad_keys.reshape(keys.shape[0], -1),
        grad_values.reshape(values.shape[0], -1),
    )


def forward_layer(stream, cond_act, gathered):
    w_mod, b_mod, w_qkv, b_qv, w_out, b_out, w_up, b_up, w_down, b_down = gathered
    model_width = stream.shape[1]
    modulation = matmul(cond_act, w_mod)[0] + b_mod.astype(jnp.float32)
    shift_attn, scale_attn, gate_attn, shift_mlp, scale_mlp, gate_mlp = jnp.split(modulation, 6)
    mixed1 = modulate(stream, shift_attn, scale_attn).astype(jnp.bfloat16)
    qkv = matmul(mixed1, w_qkv)
    qv_bias = b_qv.astype(jnp.float32)
    query = (qkv[:, :model_width] + qv_bias[:model_width]).astype(jnp.bfloat16)
    keys = qkv[:, model_width : 2 * model_width].astype(jnp.bfloat16)
    values = (qkv[:, 2 * model_width :] + qv_bias[model_width:]).astype(jnp.bfloat16)
    all_keys, all_values = (
        lax.all_gather(keys, "seq", axis=0, tiled=True),
        lax.all_gather(values, "seq", axis=0, tiled=True),
    )
    attended, log_total = attend(query, all_keys, all_values)
    attn_out = matmul(attended, w_out) + b_out.astype(jnp.float32)
    resid = stream + gate_attn * attn_out
    mixed2 = modulate(resid, shift_mlp, scale_mlp).astype(jnp.bfloat16)
    preact = matmul(mixed2, w_up) + b_up.astype(jnp.float32)
    activation = gelu_tanh(preact).astype(jnp.bfloat16)
    branch = matmul(activation, w_down) + b_down.astype(jnp.float32)
    saved_acts = (
        stream,
        modulation,
        query,
        all_keys,
        all_values,
        log_total,
        attended,
        attn_out,
        resid,
        preact,
        branch,
    )
    return (resid + gate_mlp * branch, saved_acts)


def backward_layer(gradient, saved_acts, gathered, cond_act):
    w_mod, b_mod, w_qkv, b_qv, w_out, b_out, w_up, b_up, w_down, b_down = gathered
    (
        stream,
        modulation,
        query,
        all_keys,
        all_values,
        log_total,
        attended,
        attn_out,
        resid,
        preact,
        branch,
    ) = saved_acts
    model_width = stream.shape[1]
    shift_attn, scale_attn, gate_attn, shift_mlp, scale_mlp, gate_mlp = jnp.split(modulation, 6)
    grad_branch = (gradient * gate_mlp).astype(jnp.bfloat16)
    grad_gate_mlp = jnp.sum(gradient * branch, 0)
    activation_f, gelu_pull = jax.vjp(gelu_tanh, preact)
    activation = activation_f.astype(jnp.bfloat16)
    grad_b_down = column_sums(grad_branch)
    grad_preact = gelu_pull(input_grad(grad_branch, w_down))[0].astype(jnp.bfloat16)
    mixed2_f, norm_pull_mlp = jax.vjp(modulate, resid, shift_mlp, scale_mlp)
    mixed2 = mixed2_f.astype(jnp.bfloat16)
    grad_b_up = column_sums(grad_preact)
    grad_resid_norm, grad_shift_mlp, grad_scale_mlp = norm_pull_mlp(input_grad(grad_preact, w_up))
    grad_resid = gradient + grad_resid_norm
    grad_attn = (grad_resid * gate_attn).astype(jnp.bfloat16)
    grad_gate_attn = jnp.sum(grad_resid * attn_out, 0)
    grad_b_out = column_sums(grad_attn)
    grad_attended = input_grad(grad_attn, w_out).astype(jnp.bfloat16)
    grad_query, grad_keys_all, grad_values_all = attend_back(
        query, all_keys, all_values, log_total, grad_attended
    )
    grad_keys, grad_values = (
        lax.psum_scatter(
            grad_keys_all.astype(jnp.bfloat16), "seq", scatter_dimension=0, tiled=True
        ).astype(jnp.float32),
        lax.psum_scatter(
            grad_values_all.astype(jnp.bfloat16), "seq", scatter_dimension=0, tiled=True
        ).astype(jnp.float32),
    )
    grad_qkv = jnp.concatenate(
        [
            grad_query.astype(jnp.bfloat16),
            grad_keys.astype(jnp.bfloat16),
            grad_values.astype(jnp.bfloat16),
        ],
        1,
    )
    mixed1_f, norm_pull_attn = jax.vjp(modulate, stream, shift_attn, scale_attn)
    mixed1 = mixed1_f.astype(jnp.bfloat16)
    qkv_sums = column_sums(grad_qkv)
    grad_b_qv = jnp.concatenate([qkv_sums[:model_width], qkv_sums[2 * model_width :]])
    grad_stream_norm, grad_shift_attn, grad_scale_attn = norm_pull_attn(input_grad(grad_qkv, w_qkv))
    grad_stream = grad_resid + grad_stream_norm
    grad_mod_part = jnp.concatenate(
        [
            grad_shift_attn,
            grad_scale_attn,
            grad_gate_attn,
            grad_shift_mlp,
            grad_scale_mlp,
            grad_gate_mlp,
        ]
    )
    grad_mod = lax.psum(grad_mod_part, "seq").astype(jnp.bfloat16)
    seq_share = 1.0 / lax.axis_size("seq")
    grad_b_mod = grad_mod.astype(jnp.float32) * seq_share
    grad_cond_act = input_grad(grad_mod[None], w_mod)
    operands = (
        activation,
        grad_branch,
        mixed2,
        grad_preact,
        attended,
        grad_attn,
        mixed1,
        grad_qkv,
        cond_act,
        grad_mod[None],
    )
    bias_terms = (grad_b_mod, grad_b_qv, grad_b_out, grad_b_up, grad_b_down)
    return (grad_stream, grad_cond_act, operands, bias_terms)


def per_device(
    latents,
    conditioning,
    w_mod,
    b_mod,
    w_qkv,
    b_qv,
    w_out,
    b_out,
    w_up,
    b_up,
    w_down,
    b_down,
    cotangent,
):
    params = (w_mod, b_mod, w_qkv, b_qv, w_out, b_out, w_up, b_up, w_down, b_down)
    layer_count = w_mod.shape[0]
    micro_count = latents.shape[0]
    seq_share = 1.0 / lax.axis_size("seq")
    stored = [gather_once(params, 0)]
    kept_operands = [[]]
    bias_totals = [None] * layer_count
    outputs = []
    grads_in = []
    grads_cond = []
    for micro_step in range(micro_count):
        stream = latents[micro_step, 0].astype(jnp.float32)
        cond_row = conditioning[micro_step, 0:1].astype(jnp.float32)
        cond_act = jax.nn.silu(cond_row).astype(jnp.bfloat16)
        layer_index = 0
        gathered = stored[layer_index]
        stream, saved_acts = forward_layer(stream, cond_act, gathered)
        saved_list = [saved_acts]
        outputs.append(stream.astype(jnp.bfloat16))
        gradient = cotangent[micro_step, 0].astype(jnp.float32)
        grad_cond_act = jnp.zeros(cond_row.shape, jnp.float32)
        for layer_index in reversed(range(layer_count)):
            gathered = stored[layer_index]
            gradient, grad_cond_part, operands, bias_terms = backward_layer(
                gradient, saved_list[layer_index], gathered, cond_act
            )
            grad_cond_act = grad_cond_part
            kept_operands[layer_index].append(operands)
            if bias_totals[layer_index] is None:
                bias_totals[layer_index] = bias_terms
            else:
                bias_totals[layer_index] = tuple(
                    (first + second for first, second in zip(bias_totals[layer_index], bias_terms))
                )
        grads_in.append(gradient)
        silu_pull = jax.vjp(jax.nn.silu, cond_row)[1]
        grads_cond.append(silu_pull(grad_cond_act)[0])
    layer_index = 0
    joined = [
        jnp.concatenate(
            [kept_operands[layer_index][step][member] for step in range(micro_count)], 0
        )
        for member in range(10)
    ]
    grad_w_down = weight_grad(joined[0], joined[1])
    grad_w_up = weight_grad(joined[2], joined[3])
    grad_w_out = weight_grad(joined[4], joined[5])
    grad_w_qkv = weight_grad(joined[6], joined[7])
    grad_w_mod = weight_grad(joined[8], joined[9]) * seq_share
    grad_b_mod, grad_b_qv, grad_b_out, grad_b_up, grad_b_down = bias_totals[layer_index]
    totals = (
        grad_w_mod,
        grad_b_mod,
        grad_w_qkv,
        grad_b_qv,
        grad_w_out,
        grad_b_out,
        grad_w_up,
        grad_b_up,
        grad_w_down,
        grad_b_down,
    )
    dp_count = lax.axis_size("dp")
    seq_count = lax.axis_size("seq")
    stacked = [
        owner_layout(jnp.stack([totals[member]]), dp_count, seq_count) for member in range(10)
    ]
    flat = [member.reshape((dp_count * seq_count,) + member.shape[2:]) for member in stacked]
    owned = (
        lax.psum_scatter(flat[0], ("dp", "seq"), scatter_dimension=0, tiled=True),
        lax.psum_scatter(flat[1], ("dp", "seq"), scatter_dimension=0, tiled=True),
        lax.psum_scatter(flat[2], ("dp", "seq"), scatter_dimension=0, tiled=True),
        lax.psum_scatter(flat[3], ("dp", "seq"), scatter_dimension=0, tiled=True),
        lax.psum_scatter(flat[4], ("dp", "seq"), scatter_dimension=0, tiled=True),
        lax.psum_scatter(flat[5], ("dp", "seq"), scatter_dimension=0, tiled=True),
        lax.psum_scatter(flat[6], ("dp", "seq"), scatter_dimension=0, tiled=True),
        lax.psum_scatter(flat[7], ("dp", "seq"), scatter_dimension=0, tiled=True),
        lax.psum_scatter(flat[8], ("dp", "seq"), scatter_dimension=0, tiled=True),
        lax.psum_scatter(flat[9], ("dp", "seq"), scatter_dimension=0, tiled=True),
    )
    shards = [
        member.reshape(member.shape[member.ndim - stacked_member.ndim + 2 :])
        for member, stacked_member in zip(owned, stacked)
    ]
    output = jnp.stack(outputs)[:, None]
    grad_latents = jnp.stack(grads_in)[:, None]
    grad_cond = jnp.stack(grads_cond)
    return (
        output,
        grad_latents,
        grad_cond,
        shards[0],
        shards[1],
        shards[2],
        shards[3],
        shards[4],
        shards[5],
        shards[6],
        shards[7],
        shards[8],
        shards[9],
    )


MESH_IDS = pl.DeviceIdType.MESH
ANY = pl.BlockSpec(memory_space=pl.ANY)
VM = pl.BlockSpec(memory_space=pltpu.VMEM)
F32, BF = jnp.float32, jnp.bfloat16
ALL = slice(None)
ZN, XN, YN, CN = 4, 2, 2, 2
TOK = 512
ROOT_2_PI = 0.7978845608028654


def dot_nn(left, right):
    return lax.dot_general(left, right, (((1,), (0,)), ((), ())), preferred_element_type=F32)


def dot_nt(left, right):
    return lax.dot_general(left, right, (((1,), (1,)), ((), ())), preferred_element_type=F32)


def dot_tn(left, right):
    return lax.dot_general(left, right, (((0,), (0,)), ((), ())), preferred_element_type=F32)


class Place:
    def __init__(self):
        dp, sq = lax.axis_index("dp"), lax.axis_index("seq")
        self.dp, self.sq = dp, sq
        self.z, self.x = dp // XN, dp % XN
        self.y, self.c = sq // CN, sq % CN
        self.xp = (self.z * XN + 1 - self.x, sq)
        self.yp = (dp, (1 - self.y) * CN + self.c)
        self.cp = (dp, self.y * CN + 1 - self.c)

    def z_to(self, k):
        return (lax.rem(self.z + k, ZN) * XN + self.x, self.sq)

    def z_from(self, k):
        return lax.rem(self.z + ZN - k, ZN)

    def barrier(self):
        sem = pltpu.get_barrier_semaphore()
        peers = [self.z_to(1), self.z_to(2), self.z_to(3), self.xp, self.yp, self.cp]
        for peer in peers:
            pl.semaphore_signal(sem, inc=1, device_id=peer, device_id_type=MESH_IDS)
        pl.semaphore_wait(sem, len(peers))


class Links:
    def __init__(self):
        self.sent = []

    def copy(self, src, dst, send_sem, recv_sem, peer):
        return pltpu.make_async_remote_copy(
            src_ref=src, dst_ref=dst, send_sem=send_sem, recv_sem=recv_sem, device_id=peer, device_id_type=MESH_IDS
        )

    def send(self, src, dst, send_sem, recv_sem, peer):
        copy = self.copy(src, dst, send_sem, recv_sem, peer)
        copy.start()
        self.sent.append(copy)

    def drain(self):
        for copy in self.sent:
            copy.wait_send()
        self.sent = []


def pieces_of(rows, cols):
    if rows == 32:
        return (("d", pl.ds(0, 16), pl.ds(0, cols)), ("a", pl.ds(16, 16), pl.ds(0, 640)), ("b", pl.ds(16, 16), pl.ds(640, cols - 640)))
    return (("d", pl.ds(0, 64), pl.ds(0, cols)), ("a", pl.ds(64, 48), pl.ds(0, cols)), ("b", pl.ds(112, 16), pl.ds(0, cols)))


def gather_steps(at, kind):
    z, x, y, c = at.z, at.x, at.y, at.c
    own = (z, x, y, c)
    if kind == "d":
        return (
            [(own, at.z_to(k), (at.z_from(k), x, y, c), k - 1) for k in (1, 2, 3)],
            [((ALL, x, y, c), at.yp, (ALL, x, 1 - y, c), 3)],
            [((ALL, x, ALL, c), at.xp, (ALL, 1 - x, ALL, c), 4)],
        )
    if kind == "a":
        return (
            [(own, at.z_to(k), (at.z_from(k), x, y, c), 4 + k) for k in (1, 2, 3)],
            [((ALL, x, y, c), at.xp, (ALL, 1 - x, y, c), 8)],
            [((ALL, ALL, y, c), at.yp, (ALL, ALL, 1 - y, c), 9)],
        )
    return (
        [(own, at.yp, (z, x, 1 - y, c), 10)],
        [((z, x, ALL, c), at.xp, (z, 1 - x, ALL, c), 11)],
        [((z, ALL, ALL, c), at.z_to(k), (at.z_from(k), ALL, ALL, c), 11 + k) for k in (1, 2, 3)],
    )


def norm_rows(values):
    centred = values - jnp.mean(values, -1, keepdims=True)
    inv = lax.rsqrt(jnp.mean(centred * centred, -1, keepdims=True) + EPS)
    return centred * inv, inv


def forward_kernel(
    lat, cot, small, w_mod, w_qkv, w_out, w_up, w_down,
    o_out, o_w8, o_wd, o_x, o_cot, o_m1, o_q, o_k, o_v, o_att, o_lse, o_ao, o_res, o_m2, o_gp, o_gb, o_rd, o_vec, o_ca,
    W8, WD, xs, cs, m1, m2, qs, ks, vs, att, lse, aob, res, act, gp, gb, outs, DD, CR, SM, PM, PY, PX, PZ, FM, PC, wm4, cact, vec, bias,
    rs, ss, rsm, ssm, rx, sx, rcd, scd, lw, lo,
):
    at = Place()
    z, x, y, c = at.z, at.x, at.y, at.c
    links = Links()
    lane = lax.broadcasted_iota(jnp.int32, (1, 128), 1)

    def block(unit, idx, rows=ALL, cols=ALL):
        ref = W8.at[unit] if unit < 8 else WD.at[unit - 8]
        return ref.at[idx + (rows, cols)]

    def shard(unit):
        if unit < 3:
            first = (1024, 2048, 0)[unit]
            return w_qkv.at[:, pl.ds(first, 1024)]
        if unit == 3:
            return w_out
        if unit < 8:
            return w_up.at[:, pl.ds((unit - 4) * 1024, 1024)]
        return w_down.at[:, pl.ds((unit - 8) * 256, 256)]

    local_w = [pltpu.make_async_copy(shard(u), block(u, (z, x, y, c)), lw.at[u]) for u in range(12)]
    local_m = [pltpu.make_async_copy(w_mod, wm4.at[pl.ds(32 * k, 32)], lw.at[12 + k]) for k in range(4)]
    local_x = pltpu.make_async_copy(lat.at[y], xs.at[y], lw.at[16])
    local_c = pltpu.make_async_copy(cot.at[y], cs.at[y], lw.at[17])
    for copy in local_w[:3] + local_m + [local_x] + local_w[3:] + [local_c]:
        copy.start()
    SM[z, x, y, c] = small[...]
    at.barrier()

    def pieces(unit):
        return pieces_of(32, 1024) if unit < 8 else pieces_of(128, 256)

    def step(unit, number):
        for kind, rows, cols in pieces(unit):
            for idx, peer, _, sem in gather_steps(at, kind)[number - 1]:
                ref = block(unit, idx, rows, cols)
                links.send(ref, ref, ss.at[unit, sem], rs.at[unit, sem], peer)

    def arrived(unit, number):
        for kind, rows, cols in pieces(unit):
            for _, peer, idx, sem in gather_steps(at, kind)[number - 1]:
                ref = block(unit, idx, rows, cols)
                links.copy(ref, ref, ss.at[unit, sem], rs.at[unit, sem], peer).wait_recv()

    def s1(unit):
        local_w[unit].wait()
        step(unit, 1)

    def s2(unit):
        arrived(unit, 1)
        step(unit, 2)

    def s3(unit):
        arrived(unit, 2)
        step(unit, 3)

    def s4(unit):
        arrived(unit, 3)
        ref = block(unit, (ALL, ALL, ALL, c))
        links.send(ref, ref, ss.at[unit, 15], rs.at[unit, 15], at.cp)

    outgoing = []

    def save(src, dst):
        copy = pltpu.make_async_copy(src, dst, lo.at[len(outgoing)])
        copy.start()
        outgoing.append(copy)

    def ready(unit):
        ref = block(unit, (ALL, ALL, ALL, 1 - c))
        links.copy(ref, ref, ss.at[unit, 15], rs.at[unit, 15], at.cp).wait_recv()
        if unit < 8:
            save(W8.at[unit], o_w8.at[unit])
        else:
            save(WD.at[unit - 8], o_wd.at[unit - 8])

    def tick(t):
        if 0 <= t < 12:
            s2(t)
        if 0 <= t - 1 < 12:
            s3(t - 1)
        if t + 3 < 12:
            s1(t + 3)
        if 0 <= t - 2 < 12:
            s4(t - 2)

    def small_send(idx, peer, n):
        links.send(SM.at[idx], SM.at[idx], ssm.at[n], rsm.at[n], peer)

    def small_wait(idx, n):
        links.copy(SM.at[idx], SM.at[idx], ssm.at[n], rsm.at[n], at.xp).wait_recv()

    for k in (1, 2, 3):
        small_send((z, x, y, c), at.z_to(k), k - 1)
    local_x_out = lat.at[1 - y]
    links.send(local_x_out, xs.at[y], sx.at[0], rx.at[0], at.yp)
    s1(0)
    for k in (1, 2, 3):
        small_wait((at.z_from(k), x, y, c), k - 1)
    small_send((ALL, x, y, c), at.xp, 3)
    s1(1)
    small_wait((ALL, 1 - x, y, c), 3)
    small_send((ALL, ALL, y, c), at.yp, 4)

    row = lax.broadcasted_iota(jnp.int32, (8, 128), 0)
    for m in range(2):
        for p in range(8):
            tile = SM[p // 2, p % 2, y, c, 8 * m : 8 * m + 8, :]
            cact[8 * m + p : 8 * m + p + 1, :] = jnp.sum(jnp.where(row == at.dp, tile, 0.0), 0, keepdims=True)
    cond = cact[...]
    cond = jnp.where(lane // 32 == at.sq, cond / (1.0 + jnp.exp(-cond)), 0.0)
    cact[...] = cond
    cond_low = cond.astype(BF)
    for copy in local_m:
        copy.wait()
    for i in range(6):
        part = dot_nn(cond_low, wm4[:, 1024 * i : 1024 * i + 1024])
        for m in range(2):
            for p in range(8):
                for j in range(8):
                    PM[m, p // 2, p % 2, 8 * i + j : 8 * i + j + 1, :] = part[8 * m + p : 8 * m + p + 1, 128 * j : 128 * j + 128]
    links.send(PM.at[1 - y], PY, sx.at[1], rx.at[1], at.yp)
    s1(2)
    s2(0)
    links.copy(PM.at[1 - y], PY, sx.at[1], rx.at[1], at.yp).wait_recv()
    PM[y] = PM[y] + PY[...]
    links.send(PM.at[y, :, 1 - x], PX, sx.at[2], rx.at[2], at.xp)
    s1(3)
    s2(1)
    links.copy(PM.at[y, :, 1 - x], PX, sx.at[2], rx.at[2], at.xp).wait_recv()
    PM[y, :, x] = PM[y, :, x] + PX[...]
    for k in (1, 2, 3):
        to = lax.rem(z + k, ZN)
        links.send(PM.at[y, to, x], PZ.at[k - 1], sx.at[2 + k], rx.at[2 + k], at.z_to(k))
    small_wait((ALL, ALL, 1 - y, c), 4)
    small_send((ALL, ALL, ALL, c), at.cp, 5)
    s3(0)
    for k in (1, 2, 3):
        links.copy(PM.at[y, z, x], PZ.at[k - 1], sx.at[2 + k], rx.at[2 + k], at.z_to(k)).wait_recv()
    FM[...] = PM[y, z, x] + PZ[0] + PZ[1] + PZ[2]
    links.send(FM, PC, sx.at[6], rx.at[6], at.cp)
    s1(4)
    small_wait((ALL, ALL, ALL, 1 - c), 5)

    def entry(device, line):
        return SM[device // 8, (device // 4) % 2, (device // 2) % 2, device % 2, line : line + 1, :]

    for t in range(16):
        bias[0:1, 128 * t : 128 * t + 128] = entry(2 * t, 16) + entry(2 * t + 1, 16)
    for t in range(8):
        bias[0:1, 2048 + 128 * t : 2176 + 128 * t] = (entry(4 * t, 17) + entry(4 * t + 1, 17)) + (entry(4 * t + 2, 17) + entry(4 * t + 3, 17))
        bias[0:1, 7168 + 128 * t : 7296 + 128 * t] = (entry(4 * t, 19) + entry(4 * t + 1, 19)) + (entry(4 * t + 2, 19) + entry(4 * t + 3, 19))
    for t in range(32):
        bias[0:1, 3072 + 128 * t : 3200 + 128 * t] = entry(t, 18)
    links.copy(FM, PC, sx.at[6], rx.at[6], at.cp).wait_recv()
    for j in range(48):
        k, part = j // 3, j % 3
        if part == 0:
            b_row = entry(2 * k, 20)
        elif part == 1:
            b_row = entry(2 * k, 21) + entry(2 * k + 1, 20)
        else:
            b_row = entry(2 * k + 1, 21)
        vec[j // 8 : j // 8 + 1, 128 * (j % 8) : 128 * (j % 8) + 128] = FM[j : j + 1, :] + PC[j : j + 1, :] + b_row
    shift_attn, scale_attn, gate_attn = vec[0:1, :], 1.0 + vec[1:2, :], vec[2:3, :]
    shift_mlp, scale_mlp, gate_mlp = vec[3:4, :], 1.0 + vec[4:5, :], vec[5:6, :]
    links.send(cot.at[1 - y], cs.at[y], sx.at[7], rx.at[7], at.yp)

    local_x.wait()
    links.copy(lat.at[1 - y], xs.at[1 - y], sx.at[0], rx.at[0], at.yp).wait_recv()
    RB = 32

    def norm1(i, carry):
        half, rows = i // (256 // RB), pl.ds(pl.multiple_of((i % (256 // RB)) * RB, RB), RB)
        n, _ = norm_rows(xs[half, rows, :].astype(F32))
        m1[pl.ds(pl.multiple_of(i * RB, RB), RB), :] = (n * scale_attn + shift_attn).astype(BF)
        return carry

    lax.fori_loop(0, TOK // RB, norm1, 0)
    save(xs, o_x)
    save(m1, o_m1)
    s2(2)
    s3(1)
    s1(5)
    s4(0)

    def weight(unit, cols):
        return W8[unit, :, :, :, :, :, cols].reshape(1024, -1)

    def project(unit, put):
        for t in range(2):
            cols = slice(512 * t, 512 * t + 512)
            put(cols, dot_nn(m1[...], weight(unit, cols)))

    def put_k(cols, value):
        ks[0, :, cols] = value.astype(BF)

    def put_v(cols, value):
        vs[0, :, cols] = (value + bias[0:1, 1024 + cols.start : 1024 + cols.stop]).astype(BF)

    def put_q(cols, value):
        qs[:, cols] = (value + bias[0:1, cols]).astype(BF)

    tick(3)
    ready(0)
    project(0, put_k)
    links.send(ks.at[0], ks.at[1], sx.at[8], rx.at[8], at.cp)
    tick(4)
    ready(1)
    project(1, put_v)
    links.send(vs.at[0], vs.at[1], sx.at[9], rx.at[9], at.cp)
    tick(5)
    ready(2)
    project(2, put_q)
    save(qs, o_q)
    links.copy(ks.at[0], ks.at[1], sx.at[8], rx.at[8], at.cp).wait_recv()
    links.copy(vs.at[0], vs.at[1], sx.at[9], rx.at[9], at.cp).wait_recv()
    save(ks, o_k)
    save(vs, o_v)

    def attend_pair(p, carry):
        cols = pl.ds(pl.multiple_of(p * 128, 128), 128)
        k2, v2 = ks[:, :, cols].reshape(1024, 128), vs[:, :, cols].reshape(1024, 128)
        for t in range(TOK // TQ):
            rows = slice(TQ * t, TQ * t + TQ)
            q2 = qs[rows, cols]
            parts = []
            for e in range(2):
                own = (lane < 64) == (e == 0)
                qe = jnp.where(own, q2, jnp.zeros_like(q2)) * BF(0.125)
                scores = dot_nt(qe, k2)
                top = jnp.max(scores, 1, keepdims=True)
                expon = jnp.exp(scores - top)
                total = jnp.sum(expon, 1, keepdims=True)
                parts.append(dot_nn((expon * (1.0 / total)).astype(BF), v2))
                log_total = jnp.broadcast_to(top + jnp.log(total), (TQ, 128)).T
                lse[p, e : e + 1, rows] = log_total[0:1, :]
            att[rows, cols] = jnp.where(lane < 64, parts[0], parts[1]).astype(BF)
        return carry

    lax.fori_loop(0, 3, attend_pair, 0)
    tick(6)
    lax.fori_loop(3, 7, attend_pair, 0)
    tick(7)
    lax.fori_loop(7, 8, attend_pair, 0)
    save(att, o_att)
    save(lse, o_lse)
    ready(3)
    local_c.wait()
    links.copy(cot.at[1 - y], cs.at[1 - y], sx.at[7], rx.at[7], at.yp).wait_recv()

    for t in range(2):
        cols = slice(512 * t, 512 * t + 512)
        value = dot_nn(att[...], weight(3, cols)) + bias[0:1, 2048 + 512 * t : 2560 + 512 * t]
        aob[:, cols] = value.astype(BF)
        res[:, cols] = xs[:, :, cols].reshape(TOK, 512).astype(F32) + gate_attn[:, cols] * value
    save(aob, o_ao)
    save(res, o_res)

    def norm2(i, carry):
        rows = pl.ds(pl.multiple_of(i * RB, RB), RB)
        half, part = i // (256 // RB), pl.ds(pl.multiple_of((i % (256 // RB)) * RB, RB), RB)
        n, _ = norm_rows(res[rows, :])
        m2[rows, :] = (n * scale_mlp + shift_mlp).astype(BF)
        gb[rows, :] = (cs[half, part, :].astype(F32) * gate_mlp).astype(BF)
        return carry

    lax.fori_loop(0, TOK // RB, norm2, 0)
    save(m2, o_m2)
    save(gb, o_gb)
    save(cs, o_cot)

    ring = [None, None]
    for u in range(4):
        tick(8 + u)
        ready(4 + u)
        for t in range(2):
            cols = slice(512 * t, 512 * t + 512)
            first = 1024 * u + 512 * t
            slot = t
            if ring[slot] is not None:
                ring[slot].wait()
            v = dot_nn(m2[...], weight(4 + u, cols)) + bias[0:1, 3072 + first : 3584 + first]
            sq = v * v
            th = jnp.tanh(ROOT_2_PI * v * (1.0 + 0.044715 * sq))
            up = 0.5 + 0.5 * th
            act[:, first : first + 512] = (v * up).astype(BF)
            gp[slot] = (up + 0.5 * v * (1.0 - th * th) * (ROOT_2_PI + (ROOT_2_PI * 3 * 0.044715) * sq)).astype(BF)
            ring[slot] = pltpu.make_async_copy(gp.at[slot], o_gp.at[u, :, pl.ds(512 * t, 512)], lo.at[40 + slot])
            ring[slot].start()

    def down_grad(u):
        slot = u % 2
        if u >= 2:
            grad_sent[u - 2].wait_send()
        for t in range(2):
            cols = slice(512 * t, 512 * t + 512)
            value = dot_tn(act[:, 1024 * u : 1024 * u + 1024], gb[:, cols])
            DD[slot, :, :, :, :, cols] = value.astype(BF).reshape(2, 2, 2, 128, 512)
        copy = links.copy(DD.at[slot, :, :, 1 - c], CR.at[u], scd.at[u], rcd.at[u], at.cp)
        copy.start()
        grad_sent.append(copy)

    def down_sum(u):
        slot = u % 2
        links.copy(DD.at[slot, :, :, 1 - c], CR.at[u], scd.at[u], rcd.at[u], at.cp).wait_recv()

        def add(i, carry):
            xi, yi = i // 8, (i // 4) % 2
            rows = pl.ds(pl.multiple_of((i % 4) * 32, 32), 32)
            CR[u, xi, yi, rows, :] = (CR[u, xi, yi, rows, :].astype(F32) + DD[slot, xi, yi, c, rows, :].astype(F32)).astype(BF)
            return carry

        lax.fori_loop(0, 16, add, 0)
        copy = pltpu.make_async_copy(CR.at[u], o_rd.at[u], lo.at[42 + u])
        copy.start()
        saved_down.append(copy)

    grad_sent, saved_down = [], []
    down_grad(0)
    tick(12)
    down_grad(1)
    down_sum(0)
    tick(13)
    down_grad(2)
    down_sum(1)

    def finish(u):
        ready(8 + u)
        cols = slice(256 * u, 256 * u + 256)
        branch = dot_nn(act[...], WD[u].reshape(4096, 256)) + bias[0:1, 7168 + 256 * u : 7424 + 256 * u]
        target = cs[:, :, cols].reshape(TOK, 256).astype(F32)
        vec[6:7, cols] = jnp.sum(target * branch, 0, keepdims=True)
        outs[:, :, cols] = (res[:, cols] + gate_mlp[:, cols] * branch).astype(BF).reshape(2, 256, 256)

    finish(0)
    finish(1)
    down_grad(3)
    down_sum(2)
    down_sum(3)
    finish(2)
    finish(3)
    save(vec, o_vec)
    save(cact, o_ca)
    save(outs, o_out)
    links.drain()
    for u in (2, 3):
        grad_sent[u].wait_send()
    for copy in saved_down:
        copy.wait()
    ring[0].wait()
    ring[1].wait()
    for copy in outgoing:
        copy.wait()


TQ = 256


def run_forward(lat, cot, small, w_mod, w_qkv, w_out, w_up, w_down):
    S = jax.ShapeDtypeStruct
    outs = [
        S((2, 256, 1024), BF), S((8, 4, 2, 2, 2, 32, 1024), BF), S((4, 4, 2, 2, 2, 128, 256), BF), S((2, 256, 1024), BF), S((2, 256, 1024), BF),
        S((512, 1024), BF), S((512, 1024), BF), S((2, 512, 1024), BF), S((2, 512, 1024), BF), S((512, 1024), BF), S((8, 8, 512), F32),
        S((512, 1024), BF), S((512, 1024), F32), S((512, 1024), BF), S((4, 512, 1024), BF), S((512, 1024), BF), S((4, 2, 2, 128, 1024), BF),
        S((8, 1024), F32), S((16, 128), F32),
    ]
    V = pltpu.VMEM
    dma = pltpu.SemaphoreType.DMA
    scratch = [
        V((8, 4, 2, 2, 2, 32, 1024), BF), V((4, 4, 2, 2, 2, 128, 256), BF),
        V((2, 256, 1024), BF), V((2, 256, 1024), BF), V((512, 1024), BF), V((512, 1024), BF), V((512, 1024), BF),
        V((2, 512, 1024), BF), V((2, 512, 1024), BF), V((512, 1024), BF), V((8, 8, 512), F32), V((512, 1024), BF), V((512, 1024), F32),
        V((512, 4096), BF), V((2, 512, 512), BF), V((512, 1024), BF), V((2, 256, 1024), BF),
        V((2, 2, 2, 2, 128, 1024), BF), V((4, 2, 2, 128, 1024), BF),
        V((4, 2, 2, 2, 24, 128), F32), V((2, 4, 2, 48, 128), F32), V((4, 2, 48, 128), F32), V((4, 48, 128), F32), V((3, 48, 128), F32),
        V((48, 128), F32), V((48, 128), F32), V((128, 6144), BF), V((16, 128), F32), V((8, 1024), F32), V((1, 8192), F32),
        dma((12, 16)), dma((12, 16)), dma((6,)), dma((6,)), dma((10,)), dma((10,)), dma((4,)), dma((4,)), dma((18,)), dma((48,)),
    ]
    return pl.pallas_call(
        forward_kernel,
        out_shape=outs,
        in_specs=[ANY, ANY, VM, ANY, ANY, ANY, ANY, ANY],
        out_specs=[ANY] * len(outs),
        scratch_shapes=scratch,
        compiler_params=pltpu.CompilerParams(collective_id=0, has_side_effects=True, vmem_limit_bytes=62 * 2**20),
        cost_estimate=pl.CostEstimate(flops=2 * 10**10, bytes_accessed=10**8, transcendentals=10**7),
    )(lat, cot, small, w_mod, w_qkv, w_out, w_up, w_down)


def small_table(conditioning, b_mod, b_qv, b_out, b_up, b_down):
    index = lax.axis_index("dp") * lax.axis_size("seq") + lax.axis_index("seq")
    lane = jnp.arange(128)

    def placed(values):
        size = values.shape[0]
        return jnp.where(lane // size == index % (128 // size), jnp.tile(values.astype(F32), 128 // size), 0.0)[None]

    mod = b_mod[0].astype(F32)
    none = jnp.zeros((64,), F32)
    even = jnp.stack([mod[:128], jnp.concatenate([mod[128:], none])])
    odd = jnp.stack([jnp.concatenate([none, mod[:64]]), mod[64:]])
    return jnp.concatenate(
        [
            conditioning[:, 0, :].astype(F32).reshape(16, 128),
            placed(b_qv[0]), placed(b_out[0]), placed(b_up[0]), placed(b_down[0]),
            jnp.where(index % 2 == 0, even, odd),
            jnp.zeros((2, 128), F32),
        ]
    )


ROW_CUT = 640


def scatter_steps(at):
    z, x, y = at.z, at.x, at.y
    steps = (
        [(0, (ALL, 1 - x, ALL), at.xp, 0, (ALL, x, ALL)), (1, (ALL, ALL, 1 - y), at.yp, 0, (ALL, ALL, y))]
        + [(2, (lax.rem(z + k, ZN), ALL, ALL), at.z_to(k), k - 1, (z, ALL, ALL)) for k in (1, 2, 3)],
        [(0, (ALL, x, 1 - y), at.yp, 0, (ALL, x, y)), (1, (ALL, 1 - x, y), at.xp, 0, (ALL, x, y)), (2, (z, 1 - x, ALL), at.xp, 0, (z, x, ALL))],
        [(0, (lax.rem(z + k, ZN), x, y), at.z_to(k), k - 1, (z, x, y)) for k in (1, 2, 3)]
        + [(1, (lax.rem(z + k, ZN), x, y), at.z_to(k), k - 1, (z, x, y)) for k in (1, 2, 3)]
        + [(2, (z, x, 1 - y), at.yp, 0, (z, x, y))],
    )
    return steps


PIECE_ROWS = (slice(0, 16), slice(16, 32), slice(16, 32))
PIECE_COLS = (slice(0, 1024), slice(0, ROW_CUT), slice(ROW_CUT, 1024))
LANDING = (
    ((12, 4, 2, 16, 1024), (12, 4, 2, 16, ROW_CUT), (12, 3, 2, 2, 16, 1024 - ROW_CUT)),
    ((12, 4, 16, 1024), (12, 4, 16, ROW_CUT), (12, 2, 16, 1024 - ROW_CUT)),
    ((12, 3, 16, 1024), (12, 3, 16, ROW_CUT), (12, 16, 1024 - ROW_CUT)),
)


def backward_kernel(
    h_out, h_w8, h_wd, h_x, h_cot, h_m1, h_q, h_k, h_v, h_att, lse, h_ao, h_res, h_m2, h_gp, h_gb, h_rd, vec, ca, w_mod,
    o_out, o_gl, o_qkv, o_wo, o_up, o_dn, o_mod, o_bmod, o_bias, o_gc,
    RA, RB, D, RC, L00, L01, L02, L10, L11, L12, L20, L21, L22, gp, gb, m2, acc, fr, XR, gl, fin,
    sums, GS, GP, GM, gmv, wmod, modout, bsum, BA, BB, GC, GCX, GCA, brow,
    rs, ss, rc, sc, credit, rx, sx, ld, lo,
):
    at = Place()
    z, x, y, c = at.z, at.x, at.y, at.c
    links = Links()
    lane = lax.broadcasted_iota(jnp.int32, (1, 128), 1)
    landing = ((L00, L01, L02), (L10, L11, L12), (L20, L21, L22))

    loads = {}

    def load(name, src, dst):
        copy = pltpu.make_async_copy(src, dst, ld.at[len(loads)])
        copy.start()
        loads[name] = copy

    def loaded(name):
        loads[name].wait()

    for u in range(4):
        load(f"rd{u}", h_rd.at[:, :, :, pl.ds(32 * u, 32), :], RC.at[4 + u])
    load("gb", h_gb, gb)
    for u in range(4):
        load(f"wd{u}", h_wd.at[u], RB.at[u])
    for u in range(4):
        load(f"gp{u}", h_gp.at[u], gp.at[u])
        if u == 0:
            load("m2", h_m2, m2)
        load(f"wu{u}", h_w8.at[4 + u], RA.at[u])
    load("res", h_res, fr)
    load("wm", w_mod, wmod)
    at.barrier()

    steps = scatter_steps(at)

    def slot_of(n):
        return 4 + n if n < 4 else n - 4

    unit_sent = [[] for _ in range(12)]

    def part(n, idx, piece):
        return RC.at[(slot_of(n),) + idx + (PIECE_ROWS[piece], PIECE_COLS[piece])]

    def landed(n, number, piece, slot):
        ref = landing[number][piece].at[n]
        many = (number == 0 and piece == 2) or (number == 2 and piece < 2)
        return ref.at[slot] if many else ref

    def copies(n, number):
        return [
            (links.copy(part(n, go, piece), landed(n, number, piece, slot), ss.at[n, number, i], rs.at[n, number, i], peer), piece, slot, stay)
            for i, (piece, go, peer, slot, stay) in enumerate(steps[number])
        ]

    def send_step(n, number):
        for copy, _, _, _ in copies(n, number):
            copy.start()
            unit_sent[n].append(copy)

    def add_into(n, number):
        came = copies(n, number)
        for copy, _, _, _ in came:
            copy.wait_recv()
        slot = slot_of(n)
        if number == 0:
            def add(i, carry):
                for e in range(2):
                    RC[slot, i, x, e, 0:16, :] = (RC[slot, i, x, e, 0:16, :].astype(F32) + L00[n, i, e].astype(F32)).astype(BF)
                    RC[slot, i, e, y, 16:32, :ROW_CUT] = (RC[slot, i, e, y, 16:32, :ROW_CUT].astype(F32) + L01[n, i, e].astype(F32)).astype(BF)
                xi, yi = i // 2, i % 2
                RC[slot, z, xi, yi, 16:32, ROW_CUT:] = (
                    (RC[slot, z, xi, yi, 16:32, ROW_CUT:].astype(F32) + L02[n, 0, xi, yi].astype(F32))
                    + (L02[n, 1, xi, yi].astype(F32) + L02[n, 2, xi, yi].astype(F32))
                ).astype(BF)
                return carry

            lax.fori_loop(0, 4, add, 0)
        else:
            def add(i, carry):
                RC[slot, i, x, y, 0:16, :] = (RC[slot, i, x, y, 0:16, :].astype(F32) + L10[n, i].astype(F32)).astype(BF)
                RC[slot, i, x, y, 16:32, :ROW_CUT] = (RC[slot, i, x, y, 16:32, :ROW_CUT].astype(F32) + L11[n, i].astype(F32)).astype(BF)
                return carry

            lax.fori_loop(0, 4, add, 0)
            for e in range(2):
                RC[slot, z, x, e, 16:32, ROW_CUT:] = (RC[slot, z, x, e, 16:32, ROW_CUT:].astype(F32) + L12[n, e].astype(F32)).astype(BF)

    cores_sent = {}

    def exchange(n):
        if n >= 8:
            pl.semaphore_wait(credit.at[n - 8], 1)
        copy = links.copy(D.at[n % 2, :, :, :, 1 - c], RC.at[slot_of(n)], sc.at[n], rc.at[n], at.cp)
        copy.start()
        cores_sent[n] = copy

    def before(n):
        if n - 2 in cores_sent:
            cores_sent[n - 2].wait_send()

    def r1(n):
        if n >= 4:
            links.copy(D.at[n % 2, :, :, :, 1 - c], RC.at[slot_of(n)], sc.at[n], rc.at[n], at.cp).wait_recv()
            slot = slot_of(n)

            def add(i, carry):
                zi, xi, yi = i // 4, (i // 2) % 2, i % 2
                RC[slot, zi, xi, yi] = (RC[slot, zi, xi, yi].astype(F32) + D[n % 2, zi, xi, yi, c].astype(F32)).astype(BF)
                return carry

            lax.fori_loop(0, 16, add, 0)
        else:
            loaded(f"rd{n}")
        send_step(n, 0)

    def r2(n):
        add_into(n, 0)
        send_step(n, 1)

    def r3(n):
        add_into(n, 1)
        send_step(n, 2)

    outgoing = []

    def save(src, dst):
        copy = pltpu.make_async_copy(src, dst, lo.at[len(outgoing)])
        copy.start()
        outgoing.append(copy)

    def r4(n):
        for copy, _, _, _ in copies(n, 2):
            copy.wait_recv()
        slot = slot_of(n)
        fin[n, 0:16, :] = (RC[slot, z, x, y, 0:16, :].astype(F32) + L20[n, 0].astype(F32)) + (L20[n, 1].astype(F32) + L20[n, 2].astype(F32))
        fin[n, 16:32, :ROW_CUT] = (RC[slot, z, x, y, 16:32, :ROW_CUT].astype(F32) + L21[n, 0].astype(F32)) + (L21[n, 1].astype(F32) + L21[n, 2].astype(F32))
        fin[n, 16:32, ROW_CUT:] = RC[slot, z, x, y, 16:32, ROW_CUT:].astype(F32) + L22[n].astype(F32)
        if n < 4:
            save(fin.at[n], o_dn.at[pl.ds(32 * n, 32)])
        elif n < 8:
            save(fin.at[n], o_up.at[:, pl.ds(1024 * (n - 4), 1024)])
        elif n == 8:
            save(fin.at[n], o_wo)
        else:
            save(fin.at[n], o_qkv.at[:, pl.ds(1024 * (n - 9), 1024)])
        for copy in unit_sent[n]:
            copy.wait_send()
        if n < 4:
            pl.semaphore_signal(credit.at[n], inc=1, device_id=at.cp, device_id_type=MESH_IDS)

    def put_grad(n, left, right):
        before(n)
        for t in range(2):
            cols = slice(512 * t, 512 * t + 512)
            D[n % 2, :, :, :, :, :, cols] = dot_tn(left, right(cols)).astype(BF).reshape(4, 2, 2, 2, 32, 512)
        exchange(n)

    def fold(values):
        return jnp.sum(values.reshape(-1, 8, values.shape[-1]), 0)

    for n in range(4):
        r1(n)
    links.send(h_out.at[1 - y], o_out.at[y], sx.at[0], rx.at[0], at.yp)
    save(h_out.at[y], o_out.at[y])
    loaded("gb")
    sums[8] = fold(gb[...].astype(F32))
    for u in range(4):
        loaded(f"wd{u}")

    def mlp_back(u):
        loaded(f"gp{u}")
        for t in range(2):
            rows = slice(1024 * u + 512 * t, 1024 * u + 512 * t + 512)
            cols = slice(512 * t, 512 * t + 512)
            w = jnp.concatenate([RB[j, rows, :] for j in range(4)], 1)
            value = (dot_nt(gb[...], w) * gp[u, :, cols].astype(F32)).astype(BF)
            gp[u, :, cols] = value
            sums[9 + u, :, cols] = fold(value.astype(F32))
        if u == 0:
            loaded("m2")
        put_grad(4 + u, m2[...], lambda cols: gp[u, :, cols])
        loaded(f"wu{u}")
        for t in range(2):
            cols = slice(512 * t, 512 * t + 512)
            value = dot_nt(gp[u], RA[u, cols, :])
            if u == 0:
                acc[:, cols] = value
            else:
                acc[:, cols] = acc[:, cols] + value

    mlp_back(0)
    r2(0)
    mlp_back(1)
    r1(4)
    r3(0)
    r2(1)
    mlp_back(2)
    r1(5)
    r4(0)
    r3(1)
    r2(2)
    mlp_back(3)
    load("cot", h_cot, gb)
    load("ao", h_ao, RA.at[3, pl.ds(512, 512)])
    for j in range(4):
        load(f"wo{j}", h_w8.at[3, :, pl.ds(256 * j, 256)], RB.at[j, pl.ds(3072, 1024)])
    for i, unit in enumerate((2, 0, 1)):
        for j in range(4):
            load(f"wq{i}{j}", h_w8.at[unit, :, pl.ds(256 * j, 256)], RB.at[j, pl.ds(1024 * i, 1024)])
    load("q", h_q, RA.at[0, pl.ds(0, 512)])
    load("att", h_att, RA.at[0, pl.ds(512, 512)])
    load("k", h_k, RA.at[1])
    load("v", h_v, RA.at[2])
    r1(6)
    r4(1)
    r3(2)
    r2(3)

    RB_ = 32
    scale_mlp, gate_attn, scale_attn = 1.0 + vec[4:5, :], vec[2:3, :], 1.0 + vec[1:2, :]
    for i in range(6):
        sums[i] = jnp.zeros((8, 1024), F32)
    loaded("res")
    loaded("cot")
    loaded("ao")
    load("m1", h_m1, m2)

    def norm2_back(i, carry):
        rows = pl.ds(pl.multiple_of(i * RB_, RB_), RB_)
        n, inv = norm_rows(fr[rows, :])
        up = acc[rows, :]
        gn = up * n
        sums[3] = sums[3] + fold(up)
        sums[4] = sums[4] + fold(gn)
        g = up * scale_mlp
        total = gb[rows, :].astype(F32) + (g - jnp.mean(g, -1, keepdims=True) - n * jnp.mean(gn * scale_mlp, -1, keepdims=True)) * inv
        acc[rows, :] = total
        sums[2] = sums[2] + fold(total * RA[3, pl.ds(pl.multiple_of(512 + i * RB_, RB_), RB_), :].astype(F32))
        low = (total * gate_attn).astype(BF)
        gb[rows, :] = low
        sums[5] = sums[5] + fold(low.astype(F32))
        return carry

    lax.fori_loop(0, TOK // RB_, norm2_back, 0)
    r1(7)
    r4(2)
    r3(3)
    r2(4)

    def weight(i, rows):
        return jnp.concatenate([RB[j, 1024 * i + rows.start : 1024 * i + rows.stop, :] for j in range(4)], 1)

    for j in range(4):
        loaded(f"wo{j}")
    for t in range(2):
        rows = slice(512 * t, 512 * t + 512)
        RA[3, 0:512, rows] = dot_nt(gb[...], weight(3, rows)).astype(BF)
    loaded("att")
    r4(3)
    put_grad(8, RA[0, 512:1024, :], lambda cols: gb[:, cols])
    r3(4)
    r2(5)
    for name in ("q", "k", "v"):
        loaded(name)

    def attend_back(p, carry):
        cols = pl.ds(pl.multiple_of(p * 128, 128), 128)
        k2, v2 = RA[1, :, cols], RA[2, :, cols]
        keys_sum, values_sum = None, None
        for t in range(TOK // TQB):
            rows = slice(TQB * t, TQB * t + TQB)
            q2, do2 = RA[0, rows, cols], RA[3, rows, cols]
            prod = (do2.astype(F32) * RA[0, 512 + TQB * t : 512 + TQB * t + TQB, cols].astype(F32)).T
            queries = []
            for e in range(2):
                own = (lane < 64) == (e == 0)
                qe = jnp.where(own, q2, jnp.zeros_like(q2)) * BF(0.125)
                de = jnp.where(own, do2, jnp.zeros_like(do2))
                row_dot = jnp.sum(prod[64 * e : 64 * e + 64, :], 0, keepdims=True)
                probs = jnp.exp(dot_nt(k2, qe) - lse[p, e : e + 1, rows])
                grad_scores = (probs * (dot_nt(v2, de) - row_dot)).astype(BF)
                queries.append(dot_tn(grad_scores, k2))
                a, b = dot_nn(grad_scores, qe), dot_nn(probs.astype(BF), de)
                keys_sum = a if keys_sum is None else keys_sum + a
                values_sum = b if values_sum is None else values_sum + b
            RA[3, 512 + TQB * t : 512 + TQB * t + TQB, cols] = (jnp.where(lane < 64, queries[0], queries[1]) * 0.125).astype(BF)
        gp[0, :, cols] = keys_sum[:512].astype(BF)
        gp[1, :, cols] = keys_sum[512:].astype(BF)
        gp[2, :, cols] = values_sum[:512].astype(BF)
        gp[3, :, cols] = values_sum[512:].astype(BF)
        return carry

    lax.fori_loop(0, 2, attend_back, 0)
    r1(8)
    r4(4)
    r3(5)
    r2(6)
    lax.fori_loop(2, 4, attend_back, 0)
    r4(5)
    r3(6)
    r2(7)
    lax.fori_loop(4, 6, attend_back, 0)
    r4(6)
    r3(7)
    r2(8)
    lax.fori_loop(6, 8, attend_back, 0)
    links.send(gp.at[1], XR.at[0], sx.at[1], rx.at[1], at.cp)
    links.send(gp.at[3], XR.at[1], sx.at[2], rx.at[2], at.cp)
    load("x", h_x, gb)
    loaded("m1")
    put_grad(9, m2[...], lambda cols: RA[3, 512:1024, cols])
    sums[6] = fold(RA[3, 512:1024, :].astype(F32))
    r4(7)
    r3(8)

    def join(n, own, came):
        links.copy(gp.at[own + 1], XR.at[came], sx.at[1 + came], rx.at[1 + came], at.cp).wait_recv()

        def add(i, carry):
            rows = pl.ds(pl.multiple_of(i * 64, 64), 64)
            gp[own, rows, :] = (gp[own, rows, :].astype(F32) + XR[came, rows, :].astype(F32)).astype(BF)
            return carry

        lax.fori_loop(0, 8, add, 0)
        if n == 11:
            sums[7] = fold(gp[own].astype(F32))
        r1(n - 1)
        put_grad(n, m2[...], lambda cols: gp[own, :, cols])

    join(10, 0, 0)
    r2(9)
    join(11, 2, 1)
    r4(8)
    r3(9)
    r2(10)

    for i in range(3):
        for j in range(4):
            loaded(f"wq{i}{j}")
    for t in range(2):
        rows = slice(512 * t, 512 * t + 512)
        fr[:, rows] = dot_nt(RA[3, 512:1024, :], weight(0, rows)) + dot_nt(gp[0], weight(1, rows)) + dot_nt(gp[2], weight(2, rows))
    r1(11)
    loaded("x")

    def norm1_back(i):
        rows = pl.ds(pl.multiple_of(i * RB_, RB_), RB_)
        n, inv = norm_rows(gb[rows, :].astype(F32))
        up = fr[rows, :]
        gn = up * n
        sums[0] = sums[0] + fold(up)
        sums[1] = sums[1] + fold(gn)
        g = up * scale_attn
        return rows, acc[rows, :] + (g - jnp.mean(g, -1, keepdims=True) - n * jnp.mean(gn * scale_attn, -1, keepdims=True)) * inv

    per = 256 // RB_

    def away(i, carry):
        _, value = norm1_back(i + (1 - y) * per)
        gl[0, pl.ds(pl.multiple_of(i * RB_, RB_), RB_), :] = value.astype(BF)
        return carry

    def here(i, carry):
        rows, value = norm1_back(i + y * per)
        fr[rows, :] = value
        return carry

    lax.fori_loop(0, per, away, 0)
    links.send(gl.at[0], gl.at[1], sx.at[3], rx.at[3], at.yp)
    lax.fori_loop(0, per, here, 0)
    save(fr.at[pl.ds(pl.multiple_of(y * 256, 256), 256)], o_gl.at[y])

    for i in range(6):
        value = vec[6:7, :] if i == 5 else jnp.sum(sums[i], 0, keepdims=True)
        for j in range(8):
            GS[8 * i + j : 8 * i + j + 1, :] = value[:, 128 * j : 128 * j + 128]
    links.send(GS, GP, sx.at[4], rx.at[4], at.cp)

    for line, i in enumerate((6, 7, 5, 9, 10, 11, 12, 8)):
        value = jnp.sum(sums[i], 0, keepdims=True)
        for j in range(8):
            BA[8 * line + j : 8 * line + j + 1, :] = value[:, 128 * j : 128 * j + 128]
    links.send(BA, BB.at[0], sx.at[5], rx.at[5], at.cp)
    r4(9)
    r3(10)
    r2(11)
    links.copy(GS, GP, sx.at[4], rx.at[4], at.cp).wait_recv()
    GM[y, z, x] = (GS[...] + GP[...]).astype(BF)
    mine = GM.at[y, z, x]
    for k in (1, 2, 3):
        links.send(mine, mine, sx.at[5 + k], rx.at[5 + k], at.z_to(k))
    links.copy(BA, BB.at[0], sx.at[5], rx.at[5], at.cp).wait_recv()
    BA2 = BB.at[5]
    BA2[...] = BA[...] + BB[0]
    links.send(BA2, BB.at[1], sx.at[9], rx.at[9], at.yp)
    for k in (1, 2, 3):
        ref = GM.at[y, at.z_from(k), x]
        links.copy(ref, ref, sx.at[5 + k], rx.at[5 + k], at.z_to(k)).wait_recv()
    ref = GM.at[y, :, x]
    links.send(ref, ref, sx.at[10], rx.at[10], at.xp)
    links.copy(BA2, BB.at[1], sx.at[9], rx.at[9], at.yp).wait_recv()
    BA3 = BB.at[6]
    BA3[...] = BB[5] + BB[1]
    links.send(BA3, BB.at[2], sx.at[11], rx.at[11], at.xp)
    ref = GM.at[y, :, 1 - x]
    links.copy(ref, ref, sx.at[10], rx.at[10], at.xp).wait_recv()
    links.send(GM.at[y], GM.at[y], sx.at[12], rx.at[12], at.yp)
    links.copy(BA3, BB.at[2], sx.at[11], rx.at[11], at.xp).wait_recv()
    BA4 = BB.at[7]
    BA4[...] = BB[6] + BB[2]
    for k in (1, 2, 3):
        dst = (BB.at[3], BB.at[4], BB.at[8])[k - 1]
        links.send(BA4, dst, sx.at[12 + k], rx.at[12 + k], at.z_to(k))
    r4(10)
    r3(11)
    links.copy(GM.at[1 - y], GM.at[1 - y], sx.at[12], rx.at[12], at.yp).wait_recv()
    for m in range(2):
        for p in range(8):
            tile = GM[m, p // 2, p % 2].astype(F32)
            for j in range(48):
                gmv[8 * m + p : 8 * m + p + 1, 128 * j : 128 * j + 128] = tile[j : j + 1, :]
    loaded("wm")
    cond = ca[...].astype(BF)
    part_sum = None
    for i in range(6):
        cols = slice(1024 * i, 1024 * i + 1024)
        values = gmv[:, cols]
        low = values.astype(BF)
        brow[0:1, cols] = jnp.sum(values, 0, keepdims=True)
        wide = dot_tn(cond, low)
        modout[:, cols] = (wide[0:32] + wide[32:64]) + (wide[64:96] + wide[96:128])
        step = dot_nt(low, wmod[:, cols])
        part_sum = step if part_sum is None else part_sum + step
    save(modout, o_mod)
    save(brow, o_bmod)
    GCX[0] = jnp.where(lane // 32 == at.sq, jnp.concatenate([part_sum] * 4, 1), 0.0)
    links.send(GCX.at[0], GCX.at[1], sx.at[16], rx.at[16], at.cp)
    for k in (1, 2, 3):
        dst = (BB.at[3], BB.at[4], BB.at[8])[k - 1]
        links.copy(BA4, dst, sx.at[12 + k], rx.at[12 + k], at.z_to(k)).wait_recv()
    bsum[...] = (BB[7] + BB[3]) + (BB[4] + BB[8])
    save(bsum, o_bias)
    links.copy(GCX.at[0], GCX.at[1], sx.at[16], rx.at[16], at.cp).wait_recv()
    GCX[2] = GCX[0] + GCX[1]
    links.send(GCX.at[2], GCX.at[3], sx.at[17], rx.at[17], at.yp)
    links.copy(GCX.at[2], GCX.at[3], sx.at[17], rx.at[17], at.yp).wait_recv()
    GC[z, x] = GCX[2] + GCX[3]
    mine = GC.at[z, x]
    for k in (1, 2, 3):
        links.send(mine, mine, sx.at[17 + k], rx.at[17 + k], at.z_to(k))
    for k in (1, 2, 3):
        ref = GC.at[at.z_from(k), x]
        links.copy(ref, ref, sx.at[17 + k], rx.at[17 + k], at.z_to(k)).wait_recv()
    links.send(GC.at[:, x], GC.at[:, x], sx.at[21], rx.at[21], at.xp)
    links.copy(gl.at[0], gl.at[1], sx.at[3], rx.at[3], at.yp).wait_recv()

    def widen(i, carry):
        rows = pl.ds(pl.multiple_of(i * RB_, RB_), RB_)
        fr[pl.ds(pl.multiple_of((1 - y) * 256 + i * RB_, RB_), RB_), :] = gl[1, rows, :].astype(F32)
        return carry

    lax.fori_loop(0, per, widen, 0)
    save(fr.at[pl.ds(pl.multiple_of((1 - y) * 256, 256), 256)], o_gl.at[1 - y])
    links.copy(GC.at[:, 1 - x], GC.at[:, 1 - x], sx.at[21], rx.at[21], at.xp).wait_recv()
    save(GC, o_gc)
    links.copy(h_out.at[1 - y], o_out.at[1 - y], sx.at[0], rx.at[0], at.yp).wait_recv()
    r4(11)
    for n in (10, 11):
        cores_sent[n].wait_send()
    links.drain()
    for copy in outgoing:
        copy.wait()


TQB = 256


def run_backward(fwd, w_mod):
    S = jax.ShapeDtypeStruct
    V = pltpu.VMEM
    dma = pltpu.SemaphoreType.DMA
    (out, w8, wd, xs, cot, m1, q, k, v, att, lse, ao, res, m2, gp, gb, rd, vec, ca) = fwd
    operands = [
        out, w8.reshape(8, 1024, 1024), wd.reshape(4, 4096, 256), xs.reshape(512, 1024), cot.reshape(512, 1024), m1, q,
        k.reshape(1024, 1024), v.reshape(1024, 1024), att, lse, ao, res, m2, gp, gb, rd, vec, ca, w_mod,
    ]
    outs = [
        S((2, 256, 1024), BF), S((2, 256, 1024), F32), S((32, 3072), F32), S((32, 1024), F32), S((32, 4096), F32), S((128, 1024), F32),
        S((32, 6144), F32), S((1, 6144), F32), S((64, 128), F32), S((4, 2, 16, 128), F32),
    ]
    scratch = [
        V((4, 1024, 1024), BF), V((4, 4096, 256), BF), V((2, 4, 2, 2, 2, 32, 1024), BF), V((8, 4, 2, 2, 32, 1024), BF),
        *[V(shape, BF) for step in LANDING for shape in step],
        V((4, 512, 1024), BF), V((512, 1024), BF), V((512, 1024), BF), V((512, 1024), F32), V((512, 1024), F32), V((2, 512, 1024), BF),
        V((2, 256, 1024), BF), V((12, 32, 1024), F32),
        V((13, 8, 1024), F32), V((48, 128), F32), V((48, 128), F32), V((2, 4, 2, 48, 128), BF), V((16, 6144), F32), V((32, 6144), BF),
        V((32, 6144), F32), V((64, 128), F32), V((64, 128), F32), V((9, 64, 128), F32), V((4, 2, 16, 128), F32), V((4, 16, 128), F32),
        V((8, 128), F32), V((1, 6144), F32),
        dma((12, 3, 7)), dma((12, 3, 7)), dma((12,)), dma((12,)), pltpu.SemaphoreType.REGULAR((4,)), dma((22,)), dma((22,)), dma((48,)), dma((24,)),
    ]
    in_specs = [ANY] * len(operands)
    for i in (10, 17, 18):
        in_specs[i] = VM
    return pl.pallas_call(
        backward_kernel,
        out_shape=outs,
        in_specs=in_specs,
        out_specs=[ANY] * len(outs),
        scratch_shapes=scratch,
        compiler_params=pltpu.CompilerParams(collective_id=1, has_side_effects=True, vmem_limit_bytes=62 * 2**20),
        cost_estimate=pl.CostEstimate(flops=4 * 10**10, bytes_accessed=10**8, transcendentals=10**7),
    )(*operands)


def per_device_kernels(latents, conditioning, w_mod, b_mod, w_qkv, b_qv, w_out, b_out, w_up, b_up, w_down, b_down, cotangent):
    small = small_table(conditioning, b_mod, b_qv, b_out, b_up, b_down)
    fwd = run_forward(latents[:, 0], cotangent[:, 0], small, w_mod[0], w_qkv[0], w_out[0], w_up[0], w_down[0])
    output, grad_lat, g_qkv, g_out, g_up, g_down, g_mod, gb_mod, gb_all, g_cond = run_backward(fwd, w_mod[0])
    dp = lax.axis_index("dp")
    index = dp * lax.axis_size("seq") + lax.axis_index("seq")
    flat = gb_all.reshape(-1)

    def share(values, size):
        return lax.dynamic_slice(values, (index * size,), (size,))[None]

    rows = lax.dynamic_slice(g_cond.reshape(8, 2, 8, 128), (0, 0, dp, 0), (8, 2, 1, 128))
    grad_act = jnp.moveaxis(rows[:, :, 0], 0, 1).reshape(2, 1024)
    cond = conditioning[:, 0].astype(F32)
    gate = jax.nn.sigmoid(cond)
    grad_cond = (grad_act * (gate * (1.0 + cond * (1.0 - gate))))[:, None]
    return (
        output[:, None], grad_lat[:, None], grad_cond,
        g_mod[None], share(gb_mod[0], 192), g_qkv[None], share(flat[:2048], 64), g_out[None], share(flat[2048:3072], 32),
        g_up[None], share(flat[3072:7168], 128), g_down[None], share(flat[7168:], 32),
    )


def solution(mesh):
    placed = (
        P(None, "dp", "seq", None),
        P(None, "dp", None),
        P(None, ("dp", "seq"), None),
        P(None, ("dp", "seq")),
        P(None, ("dp", "seq"), None),
        P(None, ("dp", "seq")),
        P(None, ("dp", "seq"), None),
        P(None, ("dp", "seq")),
        P(None, ("dp", "seq"), None),
        P(None, ("dp", "seq")),
        P(None, ("dp", "seq"), None),
        P(None, ("dp", "seq")),
        P(None, "dp", "seq", None),
    )
    return jax.shard_map(
        per_device_kernels if dict(mesh.shape) == {"dp": 8, "seq": 4} else per_device,
        mesh=mesh,
        in_specs=placed,
        out_specs=(
            P(None, "dp", "seq", None),
            P(None, "dp", "seq", None),
            P(None, "dp", None),
            P(None, ("dp", "seq"), None),
            P(None, ("dp", "seq")),
            P(None, ("dp", "seq"), None),
            P(None, ("dp", "seq")),
            P(None, ("dp", "seq"), None),
            P(None, ("dp", "seq")),
            P(None, ("dp", "seq"), None),
            P(None, ("dp", "seq")),
            P(None, ("dp", "seq"), None),
            P(None, ("dp", "seq")),
        ),
        check_vma=False,
    )
```

```python
import jax
import jax.numpy as jnp
from jax import lax
from jax.sharding import PartitionSpec as P
from jax.experimental import pallas as pl
from jax.experimental.pallas import tpu as pltpu

EPS = 1e-06
HEADS = 16


def modulate(stream, shift_vec, scale_vec):
    row_mean = jnp.mean(stream, -1, keepdims=True)
    centred = stream - row_mean
    row_var = jnp.mean(centred * centred, -1, keepdims=True)
    return centred * lax.rsqrt(row_var + EPS) * (1.0 + scale_vec) + shift_vec


def gelu_tanh(values):
    return jax.nn.gelu(values, approximate=True)


def matmul(left, right):
    return jnp.dot(left, right, preferred_element_type=jnp.float32)


def weight_grad(inputs, upstream):
    return jnp.einsum("ti,to->io", inputs, upstream, preferred_element_type=jnp.float32)


def input_grad(upstream, weight):
    return jnp.einsum("to,io->ti", upstream, weight, preferred_element_type=jnp.float32)


def column_sums(values):
    return jnp.sum(values.astype(jnp.float32), 0)


def gather_once(params, layer_index):
    return (
        lax.all_gather(params[0][layer_index], ("dp", "seq"), axis=0, tiled=True),
        lax.all_gather(params[1][layer_index], ("dp", "seq"), axis=0, tiled=True),
        lax.all_gather(params[2][layer_index], ("dp", "seq"), axis=0, tiled=True),
        lax.all_gather(params[3][layer_index], ("dp", "seq"), axis=0, tiled=True),
        lax.all_gather(params[4][layer_index], ("dp", "seq"), axis=0, tiled=True),
        lax.all_gather(params[5][layer_index], ("dp", "seq"), axis=0, tiled=True),
        lax.all_gather(params[6][layer_index], ("dp", "seq"), axis=0, tiled=True),
        lax.all_gather(params[7][layer_index], ("dp", "seq"), axis=0, tiled=True),
        lax.all_gather(params[8][layer_index], ("dp", "seq"), axis=0, tiled=True),
        lax.all_gather(params[9][layer_index], ("dp", "seq"), axis=0, tiled=True),
    )


def owner_layout(grad, dp_count, seq_count):
    per_owner = grad.shape[1] // (dp_count * seq_count)
    shaped = grad.reshape((grad.shape[0], dp_count, seq_count, per_owner) + grad.shape[2:])
    return jnp.moveaxis(shaped, 0, 2)


def attend(query, keys, values):
    head_size = query.shape[1] // HEADS
    query_rows = query.reshape(query.shape[0], HEADS, head_size)
    key_rows = keys.reshape(keys.shape[0], HEADS, head_size)
    value_rows = values.reshape(values.shape[0], HEADS, head_size)
    scores = jnp.einsum(
        "qhd,khd->hqk", query_rows, key_rows, preferred_element_type=jnp.float32
    ) * head_size ** (-0.5)
    row_max = jnp.max(scores, -1, keepdims=True)
    expon = jnp.exp(scores - row_max)
    row_sum = jnp.sum(expon, -1, keepdims=True)
    probs_low = (expon / row_sum).astype(jnp.bfloat16)
    attended = jnp.einsum("hqk,khd->qhd", probs_low, value_rows, preferred_element_type=jnp.float32)
    return (attended.reshape(query.shape[0], -1).astype(jnp.bfloat16), row_max + jnp.log(row_sum))


def attend_back(query, keys, values, log_total, grad_attended):
    head_size = query.shape[1] // HEADS
    inv_root = head_size ** (-0.5)
    query_rows = query.reshape(query.shape[0], HEADS, head_size)
    key_rows = keys.reshape(keys.shape[0], HEADS, head_size)
    value_rows = values.reshape(values.shape[0], HEADS, head_size)
    grad_rows = grad_attended.reshape(query.shape[0], HEADS, head_size)
    scores = (
        jnp.einsum("qhd,khd->hqk", query_rows, key_rows, preferred_element_type=jnp.float32)
        * inv_root
    )
    probs = jnp.exp(scores - log_total)
    grad_probs = jnp.einsum(
        "qhd,khd->hqk", grad_rows, value_rows, preferred_element_type=jnp.float32
    )
    row_dot = jnp.sum(probs * grad_probs, -1, keepdims=True)
    grad_scores = (probs * (grad_probs - row_dot)).astype(jnp.bfloat16)
    grad_query = (
        jnp.einsum("hqk,khd->qhd", grad_scores, key_rows, preferred_element_type=jnp.float32)
        * inv_root
    )
    grad_keys = (
        jnp.einsum("hqk,qhd->khd", grad_scores, query_rows, preferred_element_type=jnp.float32)
        * inv_root
    )
    grad_values = jnp.einsum(
        "hqk,qhd->khd", probs.astype(jnp.bfloat16), grad_rows, preferred_element_type=jnp.float32
    )
    return (
        grad_query.reshape(query.shape[0], -1),
        grad_keys.reshape(keys.shape[0], -1),
        grad_values.reshape(values.shape[0], -1),
    )


def forward_layer(stream, cond_act, gathered):
    w_mod, b_mod, w_qkv, b_qv, w_out, b_out, w_up, b_up, w_down, b_down = gathered
    model_width = stream.shape[1]
    modulation = matmul(cond_act, w_mod)[0] + b_mod.astype(jnp.float32)
    shift_attn, scale_attn, gate_attn, shift_mlp, scale_mlp, gate_mlp = jnp.split(modulation, 6)
    mixed1 = modulate(stream, shift_attn, scale_attn).astype(jnp.bfloat16)
    qkv = matmul(mixed1, w_qkv)
    qv_bias = b_qv.astype(jnp.float32)
    query = (qkv[:, :model_width] + qv_bias[:model_width]).astype(jnp.bfloat16)
    keys = qkv[:, model_width : 2 * model_width].astype(jnp.bfloat16)
    values = (qkv[:, 2 * model_width :] + qv_bias[model_width:]).astype(jnp.bfloat16)
    all_keys, all_values = (
        lax.all_gather(keys, "seq", axis=0, tiled=True),
        lax.all_gather(values, "seq", axis=0, tiled=True),
    )
    attended, log_total = attend(query, all_keys, all_values)
    attn_out = matmul(attended, w_out) + b_out.astype(jnp.float32)
    resid = stream + gate_attn * attn_out
    mixed2 = modulate(resid, shift_mlp, scale_mlp).astype(jnp.bfloat16)
    preact = matmul(mixed2, w_up) + b_up.astype(jnp.float32)
    activation = gelu_tanh(preact).astype(jnp.bfloat16)
    branch = matmul(activation, w_down) + b_down.astype(jnp.float32)
    saved_acts = (
        stream,
        modulation,
        query,
        all_keys,
        all_values,
        log_total,
        attended,
        attn_out,
        resid,
        preact,
        branch,
    )
    return (resid + gate_mlp * branch, saved_acts)


def backward_layer(gradient, saved_acts, gathered, cond_act):
    w_mod, b_mod, w_qkv, b_qv, w_out, b_out, w_up, b_up, w_down, b_down = gathered
    (
        stream,
        modulation,
        query,
        all_keys,
        all_values,
        log_total,
        attended,
        attn_out,
        resid,
        preact,
        branch,
    ) = saved_acts
    model_width = stream.shape[1]
    shift_attn, scale_attn, gate_attn, shift_mlp, scale_mlp, gate_mlp = jnp.split(modulation, 6)
    grad_branch = (gradient * gate_mlp).astype(jnp.bfloat16)
    grad_gate_mlp = jnp.sum(gradient * branch, 0)
    activation_f, gelu_pull = jax.vjp(gelu_tanh, preact)
    activation = activation_f.astype(jnp.bfloat16)
    grad_b_down = column_sums(grad_branch)
    grad_preact = gelu_pull(input_grad(grad_branch, w_down))[0].astype(jnp.bfloat16)
    mixed2_f, norm_pull_mlp = jax.vjp(modulate, resid, shift_mlp, scale_mlp)
    mixed2 = mixed2_f.astype(jnp.bfloat16)
    grad_b_up = column_sums(grad_preact)
    grad_resid_norm, grad_shift_mlp, grad_scale_mlp = norm_pull_mlp(input_grad(grad_preact, w_up))
    grad_resid = gradient + grad_resid_norm
    grad_attn = (grad_resid * gate_attn).astype(jnp.bfloat16)
    grad_gate_attn = jnp.sum(grad_resid * attn_out, 0)
    grad_b_out = column_sums(grad_attn)
    grad_attended = input_grad(grad_attn, w_out).astype(jnp.bfloat16)
    grad_query, grad_keys_all, grad_values_all = attend_back(
        query, all_keys, all_values, log_total, grad_attended
    )
    grad_keys, grad_values = (
        lax.psum_scatter(
            grad_keys_all.astype(jnp.bfloat16), "seq", scatter_dimension=0, tiled=True
        ).astype(jnp.float32),
        lax.psum_scatter(
            grad_values_all.astype(jnp.bfloat16), "seq", scatter_dimension=0, tiled=True
        ).astype(jnp.float32),
    )
    grad_qkv = jnp.concatenate(
        [
            grad_query.astype(jnp.bfloat16),
            grad_keys.astype(jnp.bfloat16),
            grad_values.astype(jnp.bfloat16),
        ],
        1,
    )
    mixed1_f, norm_pull_attn = jax.vjp(modulate, stream, shift_attn, scale_attn)
    mixed1 = mixed1_f.astype(jnp.bfloat16)
    qkv_sums = column_sums(grad_qkv)
    grad_b_qv = jnp.concatenate([qkv_sums[:model_width], qkv_sums[2 * model_width :]])
    grad_stream_norm, grad_shift_attn, grad_scale_attn = norm_pull_attn(input_grad(grad_qkv, w_qkv))
    grad_stream = grad_resid + grad_stream_norm
    grad_mod_part = jnp.concatenate(
        [
            grad_shift_attn,
            grad_scale_attn,
            grad_gate_attn,
            grad_shift_mlp,
            grad_scale_mlp,
            grad_gate_mlp,
        ]
    )
    grad_mod = lax.psum(grad_mod_part, "seq").astype(jnp.bfloat16)
    seq_share = 1.0 / lax.axis_size("seq")
    grad_b_mod = grad_mod.astype(jnp.float32) * seq_share
    grad_cond_act = input_grad(grad_mod[None], w_mod)
    operands = (
        activation,
        grad_branch,
        mixed2,
        grad_preact,
        attended,
        grad_attn,
        mixed1,
        grad_qkv,
        cond_act,
        grad_mod[None],
    )
    bias_terms = (grad_b_mod, grad_b_qv, grad_b_out, grad_b_up, grad_b_down)
    return (grad_stream, grad_cond_act, operands, bias_terms)


def per_device(
    latents,
    conditioning,
    w_mod,
    b_mod,
    w_qkv,
    b_qv,
    w_out,
    b_out,
    w_up,
    b_up,
    w_down,
    b_down,
    cotangent,
):
    params = (w_mod, b_mod, w_qkv, b_qv, w_out, b_out, w_up, b_up, w_down, b_down)
    layer_count = w_mod.shape[0]
    micro_count = latents.shape[0]
    seq_share = 1.0 / lax.axis_size("seq")
    stored = [gather_once(params, 0)]
    kept_operands = [[]]
    bias_totals = [None] * layer_count
    outputs = []
    grads_in = []
    grads_cond = []
    for micro_step in range(micro_count):
        stream = latents[micro_step, 0].astype(jnp.float32)
        cond_row = conditioning[micro_step, 0:1].astype(jnp.float32)
        cond_act = jax.nn.silu(cond_row).astype(jnp.bfloat16)
        layer_index = 0
        gathered = stored[layer_index]
        stream, saved_acts = forward_layer(stream, cond_act, gathered)
        saved_list = [saved_acts]
        outputs.append(stream.astype(jnp.bfloat16))
        gradient = cotangent[micro_step, 0].astype(jnp.float32)
        grad_cond_act = jnp.zeros(cond_row.shape, jnp.float32)
        for layer_index in reversed(range(layer_count)):
            gathered = stored[layer_index]
            gradient, grad_cond_part, operands, bias_terms = backward_layer(
                gradient, saved_list[layer_index], gathered, cond_act
            )
            grad_cond_act = grad_cond_part
            kept_operands[layer_index].append(operands)
            if bias_totals[layer_index] is None:
                bias_totals[layer_index] = bias_terms
            else:
                bias_totals[layer_index] = tuple(
                    (first + second for first, second in zip(bias_totals[layer_index], bias_terms))
                )
        grads_in.append(gradient)
        silu_pull = jax.vjp(jax.nn.silu, cond_row)[1]
        grads_cond.append(silu_pull(grad_cond_act)[0])
    layer_index = 0
    joined = [
        jnp.concatenate(
            [kept_operands[layer_index][step][member] for step in range(micro_count)], 0
        )
        for member in range(10)
    ]
    grad_w_down = weight_grad(joined[0], joined[1])
    grad_w_up = weight_grad(joined[2], joined[3])
    grad_w_out = weight_grad(joined[4], joined[5])
    grad_w_qkv = weight_grad(joined[6], joined[7])
    grad_w_mod = weight_grad(joined[8], joined[9]) * seq_share
    grad_b_mod, grad_b_qv, grad_b_out, grad_b_up, grad_b_down = bias_totals[layer_index]
    totals = (
        grad_w_mod,
        grad_b_mod,
        grad_w_qkv,
        grad_b_qv,
        grad_w_out,
        grad_b_out,
        grad_w_up,
        grad_b_up,
        grad_w_down,
        grad_b_down,
    )
    dp_count = lax.axis_size("dp")
    seq_count = lax.axis_size("seq")
    stacked = [
        owner_layout(jnp.stack([totals[member]]), dp_count, seq_count) for member in range(10)
    ]
    flat = [member.reshape((dp_count * seq_count,) + member.shape[2:]) for member in stacked]
    owned = (
        lax.psum_scatter(flat[0], ("dp", "seq"), scatter_dimension=0, tiled=True),
        lax.psum_scatter(flat[1], ("dp", "seq"), scatter_dimension=0, tiled=True),
        lax.psum_scatter(flat[2], ("dp", "seq"), scatter_dimension=0, tiled=True),
        lax.psum_scatter(flat[3], ("dp", "seq"), scatter_dimension=0, tiled=True),
        lax.psum_scatter(flat[4], ("dp", "seq"), scatter_dimension=0, tiled=True),
        lax.psum_scatter(flat[5], ("dp", "seq"), scatter_dimension=0, tiled=True),
        lax.psum_scatter(flat[6], ("dp", "seq"), scatter_dimension=0, tiled=True),
        lax.psum_scatter(flat[7], ("dp", "seq"), scatter_dimension=0, tiled=True),
        lax.psum_scatter(flat[8], ("dp", "seq"), scatter_dimension=0, tiled=True),
        lax.psum_scatter(flat[9], ("dp", "seq"), scatter_dimension=0, tiled=True),
    )
    shards = [
        member.reshape(member.shape[member.ndim - stacked_member.ndim + 2 :])
        for member, stacked_member in zip(owned, stacked)
    ]
    output = jnp.stack(outputs)[:, None]
    grad_latents = jnp.stack(grads_in)[:, None]
    grad_cond = jnp.stack(grads_cond)
    return (
        output,
        grad_latents,
        grad_cond,
        shards[0],
        shards[1],
        shards[2],
        shards[3],
        shards[4],
        shards[5],
        shards[6],
        shards[7],
        shards[8],
        shards[9],
    )


MESH_IDS = pl.DeviceIdType.MESH
ANY = pl.BlockSpec(memory_space=pl.ANY)
VM = pl.BlockSpec(memory_space=pltpu.VMEM)
F32, BF = jnp.float32, jnp.bfloat16
ALL = slice(None)
ZN, XN, YN, CN = 4, 2, 2, 2
TOK = 512
CUT = 512
ROOT_2_PI = 0.7978845608028654


def dot_nn(left, right):
    return lax.dot_general(left, right, (((1,), (0,)), ((), ())), preferred_element_type=F32)


def dot_nt(left, right):
    return lax.dot_general(left, right, (((1,), (1,)), ((), ())), preferred_element_type=F32)


def dot_tn(left, right):
    return lax.dot_general(left, right, (((0,), (0,)), ((), ())), preferred_element_type=F32)


class Place:
    def __init__(self):
        dp, sq = lax.axis_index("dp"), lax.axis_index("seq")
        self.dp, self.sq = dp, sq
        self.z, self.x = dp // XN, dp % XN
        self.y, self.c = sq // CN, sq % CN
        self.xp = (self.z * XN + 1 - self.x, sq)
        self.yp = (dp, (1 - self.y) * CN + self.c)
        self.cp = (dp, self.y * CN + 1 - self.c)

    def z_to(self, k):
        return (lax.rem(self.z + k, ZN) * XN + self.x, self.sq)

    def z_at(self, z):
        return (z * XN + self.x, self.sq)

    def z_from(self, k):
        return lax.rem(self.z + ZN - k, ZN)

    def barrier(self):
        sem = pltpu.get_barrier_semaphore()
        peers = [self.z_to(1), self.z_to(2), self.z_to(3), self.xp, self.yp, self.cp]
        for peer in peers:
            pl.semaphore_signal(sem, inc=1, device_id=peer, device_id_type=MESH_IDS)
        pl.semaphore_wait(sem, len(peers))


class Links:
    def __init__(self):
        self.sent = []

    def copy(self, src, dst, send_sem, recv_sem, peer):
        return pltpu.make_async_remote_copy(
            src_ref=src, dst_ref=dst, send_sem=send_sem, recv_sem=recv_sem, device_id=peer, device_id_type=MESH_IDS
        )

    def send(self, src, dst, send_sem, recv_sem, peer, when=None):
        copy = self.copy(src, dst, send_sem, recv_sem, peer)
        guarded(when, copy.start)
        self.sent.append((copy, when))

    def drain(self):
        for copy, when in self.sent:
            guarded(when, copy.wait_send)
        self.sent = []


def pieces_of(rows, cols):
    if rows == 32:
        return (
            ("zyx", (pl.ds(0, 16), pl.ds(0, cols))),
            ("zxy", (pl.ds(16, 16), pl.ds(0, CUT))),
            ("yxz", (pl.ds(16, 16), pl.ds(CUT, cols - CUT))),
        )
    return (("zyx", (0,)), ("zxy", (1, 0)), ("yxz", (1, 1)))


def line_gather(at, idx_of):
    z = at.z
    inner, outer = (z == 1) | (z == 2), (z == 0) | (z == 3)
    near = jnp.where(z == 1, 0, 3)
    return (
        [
            (idx_of(z), at.z_at(jnp.minimum(z + 1, 3)), idx_of(jnp.maximum(z - 1, 0)), z < 3, z > 0),
            (idx_of(z), at.z_at(jnp.maximum(z - 1, 0)), idx_of(jnp.minimum(z + 1, 3)), z > 0, z < 3),
        ],
        [
            (idx_of(3 - z), at.z_at(near), idx_of(jnp.where(z == 0, 2, 1)), inner, outer),
            (idx_of(near), at.z_at(jnp.where(z == 1, 2, 1)), idx_of(jnp.where(z == 2, 0, 3)), inner, inner),
            (idx_of(near), at.z_at(3 - near), idx_of(jnp.where(z == 3, 0, 3)), inner, outer),
        ],
    )


def gather_steps(at, kind):
    z, x, y, c = at.z, at.x, at.y, at.c
    if kind == "yxz":
        return (
            [((z, x, y, c), at.yp, (z, x, 1 - y, c), None, None)],
            [((z, x, ALL, c), at.xp, (z, 1 - x, ALL, c), None, None)],
            *line_gather(at, lambda q: (q, ALL, ALL, c)),
        )
    first = line_gather(at, lambda q: (q, x, y, c))
    if kind == "zyx":
        return (
            *first,
            [((ALL, x, y, c), at.yp, (ALL, x, 1 - y, c), None, None)],
            [((ALL, x, ALL, c), at.xp, (ALL, 1 - x, ALL, c), None, None)],
        )
    return (
        *first,
        [((ALL, x, y, c), at.xp, (ALL, 1 - x, y, c), None, None)],
        [((ALL, ALL, y, c), at.yp, (ALL, ALL, 1 - y, c), None, None)],
    )


def line_scatter(at):
    z = at.z
    inner, outer = (z == 1) | (z == 2), (z == 0) | (z == 3)
    return (
        [
            (jnp.where(z == 0, 2, 1), jnp.where(z == 0, 1, 2), 0, outer, inner),
            (jnp.where(z == 2, 0, 3), 3 - z, 1, inner, inner),
            (3 - z, jnp.where(z == 0, 2, 1), 2, outer, inner),
        ],
        [(jnp.minimum(z + 1, 3), jnp.minimum(z + 1, 3), 0, z < 3, z > 0), (jnp.maximum(z - 1, 0), jnp.maximum(z - 1, 0), 1, z > 0, z < 3)],
    )


def guarded(condition, action):
    if condition is None:
        action()
    else:
        pl.when(condition)(action)


def norm_rows(values):
    centred = values - jnp.mean(values, -1, keepdims=True)
    inv = lax.rsqrt(jnp.mean(centred * centred, -1, keepdims=True) + EPS)
    return centred * inv, inv


def scatter_steps(at):
    z, x, y = at.z, at.x, at.y

    def line(piece, number, block):
        return [(piece, block(q), at.z_at(to), slot, sends, receives) for q, to, slot, sends, receives in line_scatter(at)[number]]

    def ends(q):
        return (q, x, y)

    return (
        [(0, (ALL, 1 - x, ALL), at.xp, None, None, None), (1, (ALL, ALL, 1 - y), at.yp, None, None, None)] + line(2, 0, lambda q: (q, ALL, ALL)),
        [(0, (ALL, x, 1 - y), at.yp, None, None, None), (1, (ALL, 1 - x, y), at.xp, None, None, None)] + line(2, 1, lambda q: (q, ALL, ALL)),
        line(0, 0, ends) + line(1, 0, ends) + [(2, (z, 1 - x, ALL), at.xp, None, None, None)],
        line(0, 1, ends) + line(1, 1, ends) + [(2, (z, x, 1 - y), at.yp, None, None, None)],
    )


LR = 5
PIECE_ROWS = (slice(0, 16), slice(16, 32), slice(16, 32))
PIECE_COLS = (slice(0, 1024), slice(0, CUT), slice(CUT, 1024))
LANDING = (
    ((LR, 4, 2, 16, 1024), (LR, 4, 2, 16, CUT), (LR, 3, 2, 2, 16, 1024 - CUT)),
    ((LR, 4, 16, 1024), (LR, 4, 16, CUT), (LR, 2, 2, 2, 16, 1024 - CUT)),
    ((LR, 3, 16, 1024), (LR, 3, 16, CUT), (LR, 2, 16, 1024 - CUT)),
    ((LR, 2, 16, 1024), (LR, 2, 16, CUT), (LR, 16, 1024 - CUT)),
)


RB = 32


def block_kernel(
    lat, cot, cond_in, b_mod, b_qv, b_out, b_up, b_down, w_mod, w_qkv, w_out, w_up, w_down,
    o_out, o_gl, o_qkv, o_wo, o_up, o_dn, o_mod, o_bmod, o_bias, o_gc, t_w, t_x, t_m1, t_q, t_k, t_v, t_att, t_ao,
    W8, WD, CR, RC, L00, L01, L02, L10, L11, L12, L20, L21, L22, L30, L31, L32,
    act, gp, m2, gb, res, acc, br, cs, xs, fin, lse,
    SM, PM, PY, PX, PZ, FM, PC, wm, cact, vec, bias, sums, GS, GP, GM, bsum, BA, BB, GC, GCX, brow,
    gs, gr, gcs, gcr, rss, rsr, rcs, rcr, dcs, dcr, credit, credit_c, ready_c, sx, rx, sy, ry, ssm, rsm, lw, lo, ld, lf,
):
    at = Place()
    z, x, y, c = at.z, at.x, at.y, at.c
    links = Links()
    lane = lax.broadcasted_iota(jnp.int32, (1, 128), 1)
    inner = (z == 1) | (z == 2)
    near = jnp.where(z == 1, 0, 3)

    outgoing = []

    def save(src, dst):
        copy = pltpu.make_async_copy(src, dst, lo.at[len(outgoing)])
        copy.start()
        outgoing.append(copy)
        return copy

    loads = {}

    def load(name, src, dst):
        copy = pltpu.make_async_copy(src, dst, ld.at[len(loads)])
        copy.start()
        loads[name] = copy

    def loaded(name):
        loads[name].wait()

    ORDER = (0, 1, 2, 3, 8, 9, 10, 11, 4, 5, 6, 7)
    plans = {kind: gather_steps(at, kind) for kind in ("zyx", "zxy", "yxz")}

    def block(unit, idx, part=()):
        ref = W8.at[unit] if unit < 8 else WD.at[unit - 8]
        return ref.at[idx + part]

    def shard(unit):
        if unit < 3:
            return w_qkv.at[:, pl.ds((1024, 2048, 0)[unit], 1024)]
        if unit == 3:
            return w_out
        if unit < 8:
            return w_up.at[:, pl.ds((unit - 4) * 1024, 1024)]
        return w_down.at[:, :, :, pl.ds((unit - 8) * 256, 256)]

    def pieces(unit):
        return pieces_of(32, 1024) if unit < 8 else pieces_of(128, 256)

    gather_sent = {unit: [] for unit in range(12)}

    def step(unit, number):
        for i, (kind, part) in enumerate(pieces(unit)):
            for j, (idx, peer, _, sends, _) in enumerate(plans[kind][number]):
                ref = block(unit, idx, part)
                copy = links.copy(ref, ref, gs.at[unit, number, i, j], gr.at[unit, number, i, j], peer)
                guarded(sends, copy.start)
                gather_sent[unit].append((copy, sends))

    def arrived(unit, number):
        for i, (kind, part) in enumerate(pieces(unit)):
            for j, (_, peer, idx, _, receives) in enumerate(plans[kind][number]):
                ref = block(unit, idx, part)
                guarded(receives, links.copy(ref, ref, gs.at[unit, number, i, j], gr.at[unit, number, i, j], peer).wait_recv)

    local_w = [pltpu.make_async_copy(shard(u), block(u, (z, x, y, c)), lw.at[u]) for u in range(12)]

    def gather_stage(unit, number):
        if number == 0:
            local_w[unit].wait()
        else:
            arrived(unit, number - 1)
        if number < 4:
            step(unit, number)
        else:
            ref = block(unit, (ALL, ALL, ALL, c))
            copy = links.copy(ref, ref, gcs.at[unit], gcr.at[unit], at.cp)
            copy.start()
            gather_sent[unit].append((copy, None))

    def ready(unit):
        ref = block(unit, (ALL, ALL, ALL, 1 - c))
        links.copy(ref, ref, gcs.at[unit], gcr.at[unit], at.cp).wait_recv()

    def gather_tick(t):
        for number in (1, 2, 3):
            if 0 <= t + 1 - number < 12:
                gather_stage(ORDER[t + 1 - number], number)
        if t + 3 < 12:
            gather_stage(ORDER[t + 3], 0)
        if 0 <= t - 3 < 12:
            gather_stage(ORDER[t - 3], 4)

    def gather_done(unit):
        for copy, sends in gather_sent.pop(unit):
            guarded(sends, copy.wait_send)

    scatter_plan = scatter_steps(at)
    landing = ((L00, L01, L02), (L10, L11, L12), (L20, L21, L22), (L30, L31, L32))
    unit_sent = [[] for _ in range(12)]
    finished = set()

    def at_block(n, idx):
        if 4 <= n < 8:
            return CR, idx + ((n - 4) // 2, (n - 4) % 2)
        return RC, (n % 4 if n < 4 else n - 8,) + idx

    def part_ref(n, idx, piece):
        ref, full = at_block(n, idx)
        return ref.at[full + (PIECE_ROWS[piece], PIECE_COLS[piece])]

    def copies(n, number):
        result = []
        for i, (piece, go, peer, slot, sends, receives) in enumerate(scatter_plan[number]):
            dst = landing[number][piece].at[n % LR]
            dst = dst if slot is None else dst.at[slot]
            result.append((links.copy(part_ref(n, go, piece), dst, rss.at[n, number, i], rsr.at[n, number, i], peer), sends, receives))
        return result

    def send_step(n, number):
        for copy, sends, _ in copies(n, number):
            guarded(sends, copy.start)
            unit_sent[n].append((copy, sends))

    def add_into(n, number):
        for copy, _, receives in copies(n, number):
            guarded(receives, copy.wait_recv)
        s = n % LR

        def plus(idx, piece, *came):
            ref, full = at_block(n, idx)
            full = full + (PIECE_ROWS[piece], PIECE_COLS[piece])
            total = came[0].astype(F32)
            for more in came[1:]:
                total = total + more.astype(F32)
            ref[full] = (ref[full].astype(F32) + total).astype(BF)

        if number == 0:
            def add(i, carry):
                for e in range(2):
                    plus((i, x, e), 0, L00[s, i, e])
                    plus((i, e, y), 1, L01[s, i, e])
                return carry

            lax.fori_loop(0, 4, add, 0)

            @pl.when(inner)
            def _():
                def add_line(i, carry):
                    xi, yi = i // 2, i % 2
                    plus((3 - z, xi, yi), 2, L02[s, 0, xi, yi])
                    plus((near, xi, yi), 2, L02[s, 1, xi, yi], L02[s, 2, xi, yi])
                    return carry

                lax.fori_loop(0, 4, add_line, 0)
        elif number == 1:
            def add(i, carry):
                plus((i, x, y), 0, L10[s, i])
                plus((i, x, y), 1, L11[s, i])
                return carry

            lax.fori_loop(0, 4, add, 0)
            for slot_in, came in ((0, z > 0), (1, z < 3)):
                @pl.when(came)
                def _():
                    def add_line(i, carry):
                        xi, yi = i // 2, i % 2
                        plus((z, xi, yi), 2, L12[s, slot_in, xi, yi])
                        return carry

                    lax.fori_loop(0, 4, add_line, 0)
        elif number == 2:
            @pl.when(inner)
            def _():
                for piece, ref in ((0, L20), (1, L21)):
                    plus((3 - z, x, y), piece, ref[s, 0])
                    plus((near, x, y), piece, ref[s, 1], ref[s, 2])

            for e in range(2):
                plus((z, x, e), 2, L22[s, e])

    cores_sent = {}

    def core_copy(n, d):
        return links.copy(W8.at[d, :, :, :, 1 - c], RC.at[n % 4 if n < 4 else n - 8], rcs.at[n], rcr.at[n], at.cp)

    def slot_free(d):
        for copy in cores_sent.pop(d, ()):
            copy.wait_send()

    def put_grad(n, d, left, right):
        slot_free(d)
        for t in range(2):
            cols = slice(512 * t, 512 * t + 512)
            W8[d, :, :, :, :, :, cols] = dot_tn(left, right(cols)).astype(BF).reshape(4, 2, 2, 2, 32, 512)
        if n >= 8:
            assert n - 8 in finished
            pl.semaphore_wait(credit_c.at[n - 8], 1)
        copy = core_copy(n, d)
        copy.start()
        cores_sent[d] = (copy,)
        slot_of_unit[n] = d
        if n != 8:
            waiting[n] = 1

    slot_of_unit = {}

    def r1(n):
        if not 4 <= n < 8:
            d = slot_of_unit[n]
            core_copy(n, d).wait_recv()
            slot = n % 4 if n < 4 else n - 8

            def add(i, carry):
                zi, xi, yi = i // 4, (i // 2) % 2, i % 2
                RC[slot, zi, xi, yi] = (RC[slot, zi, xi, yi].astype(F32) + W8[d, zi, xi, yi, c].astype(F32)).astype(BF)
                return carry

            lax.fori_loop(0, 16, add, 0)
        if n >= LR:
            assert n - LR in finished
            pl.semaphore_wait(credit.at[n - LR], 5)
        send_step(n, 0)

    def middle(number):
        def run(n):
            add_into(n, number)
            send_step(n, number + 1)

        return run

    fin_saved = {}

    def r5(n):
        for copy, _, receives in copies(n, 3):
            guarded(receives, copy.wait_recv)
        s, f = n % LR, n % 3
        if n - 3 in fin_saved:
            fin_saved.pop(n - 3).wait()
        ref_, full = at_block(n, (z, x, y))
        for piece, ref in ((0, L30), (1, L31)):
            rows, cols = PIECE_ROWS[piece], PIECE_COLS[piece]
            fin[f, rows, cols] = ref_[full + (rows, cols)].astype(F32)
            for slot_in, came in ((0, z > 0), (1, z < 3)):
                @pl.when(came)
                def _():
                    fin[f, rows, cols] = fin[f, rows, cols] + ref[s, slot_in].astype(F32)
        fin[f, 16:32, CUT:] = ref_[full + (slice(16, 32), slice(CUT, 1024))].astype(F32) + L32[s].astype(F32)
        if n < 4:
            dst = o_up.at[:, pl.ds(1024 * n, 1024)]
        elif n < 8:
            dst = o_dn.at[pl.ds(32 * (n - 4), 32)]
        elif n == 8:
            dst = o_wo
        else:
            dst = o_qkv.at[:, pl.ds(1024 * (n - 9), 1024)]
        fin_saved[n] = pltpu.make_async_copy(fin.at[f], dst, lf.at[n])
        fin_saved[n].start()
        for copy, sends in unit_sent[n]:
            guarded(sends, copy.wait_send)
        if n + LR < 12:
            for peer in (at.z_to(1), at.z_to(2), at.z_to(3), at.xp, at.yp):
                pl.semaphore_signal(credit.at[n], inc=1, device_id=peer, device_id_type=MESH_IDS)
        if n < 4:
            pl.semaphore_signal(credit_c.at[n], inc=1, device_id=at.cp, device_id_type=MESH_IDS)
        finished.add(n)

    stages = {1: r1, 2: middle(0), 3: middle(1), 4: middle(2), 5: r5}
    waiting = {}

    def tick():
        for n in sorted(waiting, reverse=True):
            stages[waiting[n]](n)
            waiting[n] += 1
            if waiting[n] == 6:
                del waiting[n]

    def fold(values):
        return jnp.sum(values.reshape(-1, 8, values.shape[-1]), 0)

    local_m = pltpu.make_async_copy(w_mod, wm, lw.at[12])
    local_x = pltpu.make_async_copy(lat.at[y], xs.at[y], lw.at[13])
    local_c = pltpu.make_async_copy(cot.at[y], cs.at[y], lw.at[14])
    for copy in local_w[:3] + [local_m, local_x] + local_w[3:] + [local_c]:
        copy.start()
    index = at.dp * (YN * CN) + at.sq

    def table(line, value):
        SM[z, x, y, c, line : line + 1, :] = value

    rows_in = cond_in[...].astype(F32)
    for m in range(2):
        for j in range(8):
            table(8 * m + j, rows_in[m : m + 1, 128 * j : 128 * j + 128])
    for line, ref in ((16, b_qv), (17, b_out), (18, b_up), (19, b_down)):
        size = ref.shape[1]
        wide = jnp.concatenate([ref[...].astype(F32)] * (128 // size), 1) if size < 128 else ref[...].astype(F32)
        table(line, jnp.where(lane // size == lax.rem(index, 128 // size), wide, 0.0))
    bm = b_mod[...].astype(F32)
    none = jnp.zeros((1, 64), F32)
    even = lax.rem(index, 2) == 0
    table(20, jnp.where(even, bm[:, :128], jnp.concatenate([none, bm[:, :64]], 1)))
    table(21, jnp.where(even, jnp.concatenate([bm[:, 128:], none], 1), bm[:, 64:]))
    at.barrier()

    def small_send(idx, peer, n):
        links.send(SM.at[idx], SM.at[idx], ssm.at[n], rsm.at[n], peer)

    def small_wait(idx, n):
        links.copy(SM.at[idx], SM.at[idx], ssm.at[n], rsm.at[n], at.xp).wait_recv()

    for k in (1, 2, 3):
        small_send((z, x, y, c), at.z_to(k), k - 1)
    gather_stage(ORDER[0], 0)
    links.send(lat.at[1 - y], xs.at[y], sx.at[0], rx.at[0], at.yp)
    for k in (1, 2, 3):
        small_wait((at.z_from(k), x, y, c), k - 1)
    small_send((ALL, x, y, c), at.xp, 3)
    gather_stage(ORDER[1], 0)
    gather_stage(ORDER[2], 0)
    gather_tick(0)
    small_wait((ALL, 1 - x, y, c), 3)
    small_send((ALL, ALL, y, c), at.yp, 4)

    row = lax.broadcasted_iota(jnp.int32, (8, 128), 0)
    for m in range(2):
        for p in range(8):
            tile = SM[p // 2, p % 2, y, c, 8 * m : 8 * m + 8, :]
            cact[8 * m + p : 8 * m + p + 1, :] = jnp.sum(jnp.where(row == at.dp, tile, 0.0), 0, keepdims=True)
    cond = cact[...]
    cond = jnp.where(lane // 32 == at.sq, cond / (1.0 + jnp.exp(-cond)), 0.0)
    cact[...] = cond
    cond_low = ((cond[:, 0:32] + cond[:, 32:64]) + (cond[:, 64:96] + cond[:, 96:128])).astype(BF)
    local_m.wait()
    for i in range(6):
        part = dot_nn(cond_low, wm[:, 1024 * i : 1024 * i + 1024])
        for m in range(2):
            for p in range(8):
                for j in range(8):
                    PM[m, p // 2, p % 2, 8 * i + j : 8 * i + j + 1, :] = part[8 * m + p : 8 * m + p + 1, 128 * j : 128 * j + 128]
    links.send(PM.at[1 - y], PY, sx.at[1], rx.at[1], at.yp)
    gather_tick(1)
    links.copy(PM.at[1 - y], PY, sx.at[1], rx.at[1], at.yp).wait_recv()
    PM[y] = PM[y] + PY[...]
    links.send(PM.at[y, :, 1 - x], PX, sx.at[2], rx.at[2], at.xp)
    small_wait((ALL, ALL, 1 - y, c), 4)
    small_send((ALL, ALL, ALL, c), at.cp, 5)
    gather_tick(2)
    links.copy(PM.at[y, :, 1 - x], PX, sx.at[2], rx.at[2], at.xp).wait_recv()
    PM[y, :, x] = PM[y, :, x] + PX[...]
    for k in (1, 2, 3):
        to = lax.rem(z + k, ZN)
        links.send(PM.at[y, to, x], PZ.at[k - 1], sx.at[2 + k], rx.at[2 + k], at.z_to(k))
    gather_tick(3)
    for k in (1, 2, 3):
        links.copy(PM.at[y, z, x], PZ.at[k - 1], sx.at[2 + k], rx.at[2 + k], at.z_to(k)).wait_recv()
    FM[...] = PM[y, z, x] + PZ[0] + PZ[1] + PZ[2]
    links.send(FM, PC, sx.at[6], rx.at[6], at.cp)
    small_wait((ALL, ALL, ALL, 1 - c), 5)

    def entry(device, line):
        return SM[device // 8, (device // 4) % 2, (device // 2) % 2, device % 2, line : line + 1, :]

    for t in range(16):
        bias[0:1, 128 * t : 128 * t + 128] = entry(2 * t, 16) + entry(2 * t + 1, 16)
    for t in range(8):
        bias[0:1, 2048 + 128 * t : 2176 + 128 * t] = (entry(4 * t, 17) + entry(4 * t + 1, 17)) + (entry(4 * t + 2, 17) + entry(4 * t + 3, 17))
        bias[0:1, 7168 + 128 * t : 7296 + 128 * t] = (entry(4 * t, 19) + entry(4 * t + 1, 19)) + (entry(4 * t + 2, 19) + entry(4 * t + 3, 19))
    for t in range(32):
        bias[0:1, 3072 + 128 * t : 3200 + 128 * t] = entry(t, 18)
    links.copy(FM, PC, sx.at[6], rx.at[6], at.cp).wait_recv()
    for j in range(48):
        k, third = j // 3, j % 3
        if third == 0:
            b_row = entry(2 * k, 20)
        elif third == 1:
            b_row = entry(2 * k, 21) + entry(2 * k + 1, 20)
        else:
            b_row = entry(2 * k + 1, 21)
        vec[j // 8 : j // 8 + 1, 128 * (j % 8) : 128 * (j % 8) + 128] = FM[j : j + 1, :] + PC[j : j + 1, :] + b_row
    shift_attn, scale_attn, gate_attn = vec[0:1, :], 1.0 + vec[1:2, :], vec[2:3, :]
    shift_mlp, scale_mlp, gate_mlp = vec[3:4, :], 1.0 + vec[4:5, :], vec[5:6, :]
    links.send(cot.at[1 - y], cs.at[y], sx.at[7], rx.at[7], at.yp)

    local_x.wait()
    links.copy(lat.at[1 - y], xs.at[1 - y], sx.at[0], rx.at[0], at.yp).wait_recv()

    def halves(i):
        return i // (256 // RB), pl.ds(pl.multiple_of((i % (256 // RB)) * RB, RB), RB)

    def norm1(i, carry):
        half, rows = halves(i)
        n, _ = norm_rows(xs[half, rows, :].astype(F32))
        gp[0, pl.ds(pl.multiple_of(i * RB, RB), RB), :] = (n * scale_attn + shift_attn).astype(BF)
        return carry

    lax.fori_loop(0, TOK // RB, norm1, 0)
    x_saved = save(xs, t_x)
    m1_saved = save(gp.at[0], t_m1)
    gather_tick(4)

    def weight(unit, cols):
        return W8[unit, :, :, :, :, :, cols].reshape(1024, -1)

    def project(unit, put):
        for t in range(2):
            cols = slice(512 * t, 512 * t + 512)
            put(cols, dot_nn(gp[0], weight(unit, cols)))

    def rows512(value):
        return value.astype(BF).reshape(2, 2, 2, 2, 32, -1)

    def put_k(cols, value):
        CR[0, :, :, :, :, :, cols] = rows512(value)

    def put_v(cols, value):
        CR[2, :, :, :, :, :, cols] = rows512(value + bias[0:1, 1024 + cols.start : 1024 + cols.stop])

    def put_q(cols, value):
        act[0, :, :, :, :, :, cols] = rows512(value + bias[0:1, cols])

    ready(0)
    w_saved = [save(W8.at[0], t_w.at[0])]
    project(0, put_k)
    k_sent = links.copy(CR.at[0], CR.at[1], sx.at[8], rx.at[8], at.cp)
    k_sent.start()
    gather_tick(5)
    ready(1)
    w_saved.append(save(W8.at[1], t_w.at[1]))
    project(1, put_v)
    v_sent = links.copy(CR.at[2], CR.at[3], sx.at[9], rx.at[9], at.cp)
    v_sent.start()
    gather_tick(6)
    ready(2)
    project(2, put_q)
    q_saved = save(act.at[0], t_q)
    k_sent.wait_recv()
    v_sent.wait_recv()
    kv_saved = [save(CR.at[pl.ds(0, 2)], t_k), save(CR.at[pl.ds(2, 2)], t_v)]

    def attend_pair(p, carry):
        cols = pl.ds(pl.multiple_of(p * 128, 128), 128)
        k2, v2 = CR[0:2, :, :, :, :, :, cols].reshape(1024, 128), CR[2:4, :, :, :, :, :, cols].reshape(1024, 128)
        for t in range(2):
            rows = slice(256 * t, 256 * t + 256)
            q2 = act[0, t, :, :, :, :, cols].reshape(256, 128)
            parts = []
            for e in range(2):
                own = (lane < 64) == (e == 0)
                qe = jnp.where(own, q2, jnp.zeros_like(q2)) * BF(0.125)
                scores = dot_nt(qe, k2)
                top = jnp.max(scores, 1, keepdims=True)
                expon = jnp.exp(scores - top)
                total = jnp.sum(expon, 1, keepdims=True)
                parts.append(dot_nn((expon * (1.0 / total)).astype(BF), v2))
                log_total = jnp.broadcast_to(top + jnp.log(total), (256, 128)).T
                lse[p, e : e + 1, rows] = log_total[0:1, :]
            act[1, t, :, :, :, :, cols] = jnp.where(lane < 64, parts[0], parts[1]).astype(BF).reshape(2, 2, 2, 32, 128)
        return carry

    lax.fori_loop(0, 3, attend_pair, 0)
    gather_tick(7)
    lax.fori_loop(3, 6, attend_pair, 0)
    gather_tick(8)
    lax.fori_loop(6, 8, attend_pair, 0)
    att_saved = save(act.at[1], t_att)
    for copy in kv_saved + [q_saved]:
        copy.wait()
    k_sent.wait_send()
    v_sent.wait_send()
    pl.semaphore_signal(ready_c, inc=1, device_id=at.cp, device_id_type=MESH_IDS)
    ready(3)
    local_c.wait()
    links.copy(cot.at[1 - y], cs.at[1 - y], sx.at[7], rx.at[7], at.yp).wait_recv()

    for t in range(2):
        cols = slice(512 * t, 512 * t + 512)
        value = dot_nn(act[1].reshape(512, 1024), weight(3, cols)) + bias[0:1, 2048 + 512 * t : 2560 + 512 * t]
        gp[1, :, cols] = value.astype(BF)
        res[:, cols] = xs[:, :, cols].reshape(TOK, 512).astype(F32) + gate_attn[:, cols] * value
    ao_saved = save(gp.at[1], t_ao)
    for i in range(13):
        sums[i] = jnp.zeros((8, 1024), F32)

    def norm2(i, carry):
        rows = pl.ds(pl.multiple_of(i * RB, RB), RB)
        half, part = halves(i)
        n, _ = norm_rows(res[rows, :])
        m2[rows, :] = (n * scale_mlp + shift_mlp).astype(BF)
        low = (cs[half, part, :].astype(F32) * gate_mlp).astype(BF)
        gb[rows, :] = low
        sums[8] = sums[8] + fold(low.astype(F32))
        return carry

    lax.fori_loop(0, TOK // RB, norm2, 0)
    gather_tick(9)
    for copy in [x_saved, m1_saved, att_saved, ao_saved] + w_saved:
        copy.wait()
    gather_tick(10)
    for unit in (8, 9, 10, 11):
        ready(unit)
    gather_done(0)
    gather_done(1)

    def down_rows(j, u):
        return WD[j, u].reshape(1024, 256)

    def down_copies(u):
        return [
            links.copy(W8.at[1, pl.ds(2 * xi, 2), 1 - c], CR.at[u, xi], dcs.at[u, xi], dcr.at[u, xi], at.cp)
            for xi in range(2)
        ]

    def mlp(u):
        for t in range(2):
            cols = slice(512 * t, 512 * t + 512)
            first = 3072 + 1024 * u + 512 * t
            v = dot_nn(m2[...], weight(4 + u, cols)) + bias[0:1, first : first + 512]
            rows = jnp.concatenate([WD[j, u, t].reshape(512, 256) for j in range(4)], 1)
            slope = dot_nt(gb[...], rows)
            square = v * v
            th = jnp.tanh(ROOT_2_PI * v * (1.0 + 0.044715 * square))
            up = 0.5 + 0.5 * th
            act[0, :, :, :, :, :, cols] = rows512(v * up)
            low = (slope * (up + 0.5 * v * (1.0 - th * th) * (ROOT_2_PI + (ROOT_2_PI * 3 * 0.044715) * square))).astype(BF)
            gp[0, :, cols] = low
            sums[9 + u, :, cols] = fold(low.astype(F32))
        put_grad(u, 0, m2[...], lambda cols: gp[0, :, cols])
        slot_free(1)
        acts = act[0].reshape(512, 1024)
        for t in range(2):
            cols = slice(512 * t, 512 * t + 512)
            W8[1, :, :, :, :, :, cols] = dot_tn(acts, gb[:, cols]).astype(BF).reshape(4, 2, 2, 2, 32, 512)
        if u == 0:
            pl.semaphore_wait(ready_c, 1)
        cores_sent[1] = down_copies(u)
        for copy in cores_sent[1]:
            copy.start()
        for t in range(2):
            cols = slice(512 * t, 512 * t + 512)
            back = dot_nt(gp[0], W8[4 + u, 2 * t : 2 * t + 2].reshape(512, 1024))
            ahead = dot_nn(acts, jnp.concatenate([down_rows(2 * t, u), down_rows(2 * t + 1, u)], 1))
            acc[:, cols] = back if u == 0 else acc[:, cols] + back
            br[:, cols] = ahead if u == 0 else br[:, cols] + ahead

    def down_sum(u):
        for copy in down_copies(u):
            copy.wait_recv()

        def add(i, carry):
            xi, yi, a, b = i // 8, (i // 4) % 2, (i // 2) % 2, i % 2
            CR[u, xi, yi, a, b] = (CR[u, xi, yi, a, b].astype(F32) + W8[1, 2 * xi + yi, c, a, b].astype(F32)).astype(BF)
            return carry

        lax.fori_loop(0, 16, add, 0)

    gather_tick(11)
    for u in range(4):
        ready(4 + u)
        mlp(u)
        if u < 3:
            gather_tick(12 + u)
        tick()
        down_sum(u)
    waiting[4] = 1

    def output(i, carry):
        rows = pl.ds(pl.multiple_of(i * RB, RB), RB)
        half, part = halves(i)
        branch = br[rows, :] + bias[0:1, 7168:8192]
        sums[6] = sums[6] + fold(cs[half, part, :].astype(F32) * branch)
        xs[half, part, :] = (res[rows, :] + gate_mlp * branch).astype(BF)
        return carry

    lax.fori_loop(0, TOK // RB, output, 0)
    vec[6:7, :] = jnp.sum(sums[6], 0, keepdims=True)
    out_saved = save(xs.at[y], o_out.at[y])
    links.send(xs.at[1 - y], o_out.at[y], sx.at[10], rx.at[10], at.yp)
    for unit in (2, 3, 4, 5, 6, 7, 8, 9, 10, 11):
        gather_done(unit)
    load("ao", t_ao, gp.at[1])
    for j in range(4):
        cols = pl.ds(256 * j, 256)
        load(f"k{j}", t_k.at[:, :, :, :, :, :, cols], WD.at[j, 0])
        load(f"v{j}", t_v.at[:, :, :, :, :, :, cols], WD.at[j, 1])
        load(f"q{j}", t_q.at[:, :, :, :, :, cols], WD.at[j, 2, 0])
        load(f"att{j}", t_att.at[:, :, :, :, :, cols], WD.at[j, 2, 1])
    load("m1", t_m1, gp.at[0])
    load("wk", t_w.at[0], W8.at[4])
    load("wv", t_w.at[1], W8.at[5])
    tick()
    waiting[5] = 1

    loaded("ao")

    def norm2_back(i, carry):
        rows = pl.ds(pl.multiple_of(i * RB, RB), RB)
        half, part = halves(i)
        n, inv = norm_rows(res[rows, :])
        up = acc[rows, :]
        gn = up * n
        sums[3] = sums[3] + fold(up)
        sums[4] = sums[4] + fold(gn)
        g = up * scale_mlp
        total = cs[half, part, :].astype(F32) + (g - jnp.mean(g, -1, keepdims=True) - n * jnp.mean(gn * scale_mlp, -1, keepdims=True)) * inv
        acc[rows, :] = total
        sums[2] = sums[2] + fold(total * gp[1, rows, :].astype(F32))
        low = (total * gate_attn).astype(BF)
        gb[rows, :] = low
        sums[5] = sums[5] + fold(low.astype(F32))
        return carry

    lax.fori_loop(0, TOK // RB, norm2_back, 0)
    for half in range(2):
        load(f"x{half}", t_x.at[half], gp.at[1, pl.ds(256 * half, 256)])
    tick()
    waiting[6] = 1
    for t in range(2):
        value = dot_nt(gb[...], W8[3, 2 * t : 2 * t + 2].reshape(512, 1024)).astype(BF)
        for h in range(2):
            WD[2 * t + h, 3, 0] = value[:, 256 * h : 256 * h + 256].reshape(2, 2, 2, 2, 32, 256)
    for j in range(4):
        for name in ("k", "v", "q", "att"):
            loaded(f"{name}{j}")

    def wide(a, b):
        return jnp.concatenate([WD[j, a, b].reshape(512, 256) for j in range(4)], 1)

    put_grad(8, 0, wide(2, 1), lambda cols: gb[:, cols])
    tick()
    waiting[7] = 1

    def attend_back(p, carry):
        j, cols = p // 2, pl.ds(pl.multiple_of((p % 2) * 128, 128), 128)
        full = pl.ds(pl.multiple_of(p * 128, 128), 128)
        k2, v2 = WD[j, 0, :, :, :, :, :, :, cols].reshape(1024, 128), WD[j, 1, :, :, :, :, :, :, cols].reshape(1024, 128)
        keys_sum, values_sum = None, None
        for t in range(2):
            rows = slice(256 * t, 256 * t + 256)
            q2, do2 = WD[j, 2, 0, t, :, :, :, :, cols].reshape(256, 128), WD[j, 3, 0, t, :, :, :, :, cols].reshape(256, 128)
            prod = (do2.astype(F32) * WD[j, 2, 1, t, :, :, :, :, cols].reshape(256, 128).astype(F32)).T
            queries = []
            for e in range(2):
                own = (lane < 64) == (e == 0)
                qe = jnp.where(own, q2, jnp.zeros_like(q2)) * BF(0.125)
                de = jnp.where(own, do2, jnp.zeros_like(do2))
                row_dot = jnp.sum(prod[64 * e : 64 * e + 64, :], 0, keepdims=True)
                probs = jnp.exp(dot_nt(k2, qe) - lse[p, e : e + 1, rows])
                grad_scores = (probs * (dot_nt(v2, de) - row_dot)).astype(BF)
                queries.append(dot_tn(grad_scores, k2))
                a, b = dot_nn(grad_scores, qe), dot_nn(probs.astype(BF), de)
                keys_sum = a if keys_sum is None else keys_sum + a
                values_sum = b if values_sum is None else values_sum + b
            grad_query = (jnp.where(lane < 64, queries[0], queries[1]) * 0.125).astype(BF)
            WD[j, 3, 1, t, :, :, :, :, cols] = grad_query.reshape(2, 2, 2, 32, 128)
        W8[6, :, :, :, :, :, full] = keys_sum.astype(BF).reshape(4, 2, 2, 2, 32, 128)
        W8[7, :, :, :, :, :, full] = values_sum.astype(BF).reshape(4, 2, 2, 2, 32, 128)
        return carry

    lax.fori_loop(0, 2, attend_back, 0)
    tick()
    waiting[8] = 1
    lax.fori_loop(2, 4, attend_back, 0)
    tick()
    lax.fori_loop(4, 6, attend_back, 0)
    tick()
    lax.fori_loop(6, 8, attend_back, 0)
    links.send(W8.at[6, pl.ds(2, 2)], act.at[0], sx.at[11], rx.at[11], at.cp)
    links.send(W8.at[7, pl.ds(2, 2)], act.at[1], sx.at[12], rx.at[12], at.cp)
    loaded("m1")
    grad_q = wide(3, 1)
    put_grad(9, 1, gp[0], lambda cols: grad_q[:, cols])
    sums[6] = fold(grad_q.astype(F32))

    def join(n, own, came, d):
        links.copy(W8.at[own, pl.ds(2, 2)], act.at[came], sx.at[11 + came], rx.at[11 + came], at.cp).wait_recv()

        def add(i, carry):
            a, b = i // 2, i % 2
            W8[own, a, b] = (W8[own, a, b].astype(F32) + act[came, a, b].astype(F32)).astype(BF)
            return carry

        lax.fori_loop(0, 4, add, 0)
        if n == 11:
            sums[7] = fold(W8[own, 0:2].reshape(512, 1024).astype(F32))
        tick()
        put_grad(n, d, gp[0], lambda cols: W8[own, 0:2, :, :, :, :, cols].reshape(512, 512))

    join(10, 6, 0, 0)
    join(11, 7, 1, 1)
    tick()

    loaded("wk")
    loaded("wv")
    grad_q = wide(3, 1)
    grad_k, grad_v = W8[6, 0:2].reshape(512, 1024), W8[7, 0:2].reshape(512, 1024)
    for t in range(2):
        rows = slice(2 * t, 2 * t + 2)
        br[:, 512 * t : 512 * t + 512] = (
            dot_nt(grad_q, W8[2, rows].reshape(512, 1024)) + dot_nt(grad_k, W8[4, rows].reshape(512, 1024)) + dot_nt(grad_v, W8[5, rows].reshape(512, 1024))
        )
    tick()
    loaded("x0")
    loaded("x1")

    def norm1_back(i):
        rows = pl.ds(pl.multiple_of(i * RB, RB), RB)
        n, inv = norm_rows(gp[1, rows, :].astype(F32))
        up = br[rows, :]
        gn = up * n
        sums[0] = sums[0] + fold(up)
        sums[1] = sums[1] + fold(gn)
        g = up * scale_attn
        return rows, acc[rows, :] + (g - jnp.mean(g, -1, keepdims=True) - n * jnp.mean(gn * scale_attn, -1, keepdims=True)) * inv

    per = 256 // RB

    def away(i, carry):
        _, value = norm1_back(i + (1 - y) * per)
        cs[0, pl.ds(pl.multiple_of(i * RB, RB), RB), :] = value.astype(BF)
        return carry

    def here(i, carry):
        rows, value = norm1_back(i + y * per)
        br[rows, :] = value
        return carry

    lax.fori_loop(0, per, away, 0)
    links.send(cs.at[0], cs.at[1], sx.at[13], rx.at[13], at.yp)
    lax.fori_loop(0, per, here, 0)
    save(br.at[pl.ds(pl.multiple_of(y * 256, 256), 256)], o_gl.at[y])

    for i in range(6):
        value = vec[6:7, :] if i == 5 else jnp.sum(sums[i], 0, keepdims=True)
        for j in range(8):
            GS[8 * i + j : 8 * i + j + 1, :] = value[:, 128 * j : 128 * j + 128]
    links.send(GS, GP, sy.at[4], ry.at[4], at.cp)
    for line, i in enumerate((6, 7, 5, 9, 10, 11, 12, 8)):
        value = jnp.sum(sums[i], 0, keepdims=True)
        for j in range(8):
            BA[8 * line + j : 8 * line + j + 1, :] = value[:, 128 * j : 128 * j + 128]
    links.send(BA, BB.at[0], sy.at[5], ry.at[5], at.cp)
    links.copy(GS, GP, sy.at[4], ry.at[4], at.cp).wait_recv()
    GM[y, z, x] = (GS[...] + GP[...]).astype(BF)
    mine = GM.at[y, z, x]
    for k in (1, 2, 3):
        links.send(mine, mine, sy.at[5 + k], ry.at[5 + k], at.z_to(k))
    tick()
    links.copy(BA, BB.at[0], sy.at[5], ry.at[5], at.cp).wait_recv()
    BB[5] = BA[...] + BB[0]
    links.send(BB.at[5], BB.at[1], sy.at[9], ry.at[9], at.yp)
    for k in (1, 2, 3):
        ref = GM.at[y, at.z_from(k), x]
        links.copy(ref, ref, sy.at[5 + k], ry.at[5 + k], at.z_to(k)).wait_recv()
    ref = GM.at[y, :, x]
    links.send(ref, ref, sy.at[10], ry.at[10], at.xp)
    links.copy(BB.at[5], BB.at[1], sy.at[9], ry.at[9], at.yp).wait_recv()
    BB[6] = BB[5] + BB[1]
    links.send(BB.at[6], BB.at[2], sy.at[11], ry.at[11], at.xp)
    ref = GM.at[y, :, 1 - x]
    links.copy(ref, ref, sy.at[10], ry.at[10], at.xp).wait_recv()
    links.send(GM.at[y], GM.at[y], sy.at[12], ry.at[12], at.yp)
    links.copy(BB.at[6], BB.at[2], sy.at[11], ry.at[11], at.xp).wait_recv()
    BB[7] = BB[6] + BB[2]
    bias_in = (BB.at[3], BB.at[4], BB.at[8])
    for k in (1, 2, 3):
        links.send(BB.at[7], bias_in[k - 1], sy.at[12 + k], ry.at[12 + k], at.z_to(k))
    tick()
    links.copy(GM.at[1 - y], GM.at[1 - y], sy.at[12], ry.at[12], at.yp).wait_recv()

    for m in range(2):
        for p in range(8):
            tile = GM[m, p // 2, p % 2].astype(F32)
            for j in range(48):
                first = 256 + 16 * (j // 8) + 8 * m + p
                acc[first : first + 1, 128 * (j % 8) : 128 * (j % 8) + 128] = tile[j : j + 1, :]
    cond = cact[...].astype(BF)
    part_sum = None
    for i in range(6):
        cols = slice(1024 * i, 1024 * i + 1024)
        values = acc[256 + 16 * i : 272 + 16 * i, :]
        low = values.astype(BF)
        brow[0:1, cols] = jnp.sum(values, 0, keepdims=True)
        spread = dot_tn(cond, low)
        acc[32 * i : 32 * i + 32, :] = (spread[0:32] + spread[32:64]) + (spread[64:96] + spread[96:128])
        save(acc.at[pl.ds(32 * i, 32)], o_mod.at[:, pl.ds(1024 * i, 1024)])
        term = dot_nt(low, wm[:, cols])
        part_sum = term if part_sum is None else part_sum + term
    save(brow, o_bmod)
    GCX[0] = jnp.where(lane // 32 == at.sq, jnp.concatenate([part_sum] * 4, 1), 0.0)
    links.send(GCX.at[0], GCX.at[1], sy.at[16], ry.at[16], at.cp)
    for k in (1, 2, 3):
        links.copy(BB.at[7], bias_in[k - 1], sy.at[12 + k], ry.at[12 + k], at.z_to(k)).wait_recv()
    bsum[...] = (BB[7] + BB[3]) + (BB[4] + BB[8])
    save(bsum, o_bias)
    links.copy(GCX.at[0], GCX.at[1], sy.at[16], ry.at[16], at.cp).wait_recv()
    GCX[2] = GCX[0] + GCX[1]
    links.send(GCX.at[2], GCX.at[3], sy.at[17], ry.at[17], at.yp)
    if waiting:
        tick()
    links.copy(GCX.at[2], GCX.at[3], sy.at[17], ry.at[17], at.yp).wait_recv()
    GC[z, x] = GCX[2] + GCX[3]
    mine = GC.at[z, x]
    for k in (1, 2, 3):
        links.send(mine, mine, sy.at[17 + k], ry.at[17 + k], at.z_to(k))
    for k in (1, 2, 3):
        ref = GC.at[at.z_from(k), x]
        links.copy(ref, ref, sy.at[17 + k], ry.at[17 + k], at.z_to(k)).wait_recv()
    links.send(GC.at[:, x], GC.at[:, x], sy.at[21], ry.at[21], at.xp)
    links.copy(cs.at[0], cs.at[1], sx.at[13], rx.at[13], at.yp).wait_recv()

    def widen(i, carry):
        rows = pl.ds(pl.multiple_of(i * RB, RB), RB)
        br[pl.ds(pl.multiple_of((1 - y) * 256 + i * RB, RB), RB), :] = cs[1, rows, :].astype(F32)
        return carry

    lax.fori_loop(0, per, widen, 0)
    save(br.at[pl.ds(pl.multiple_of((1 - y) * 256, 256), 256)], o_gl.at[1 - y])
    while waiting:
        tick()
    links.copy(GC.at[:, 1 - x], GC.at[:, 1 - x], sy.at[21], ry.at[21], at.xp).wait_recv()
    save(GC, o_gc)
    links.copy(xs.at[1 - y], o_out.at[1 - y], sx.at[10], rx.at[10], at.yp).wait_recv()
    slot_free(0)
    slot_free(1)
    for copy in fin_saved.values():
        copy.wait()
    links.drain()
    early = [id(copy) for copy in kv_saved + [q_saved, x_saved, m1_saved, att_saved, ao_saved] + w_saved]
    for copy in outgoing:
        if id(copy) not in early:
            copy.wait()


def run_block(lat, cot, cond, b_mod, b_qv, b_out, b_up, b_down, w_mod, w_qkv, w_out, w_up, w_down):
    S = jax.ShapeDtypeStruct
    V = pltpu.VMEM
    dma = pltpu.SemaphoreType.DMA
    regular = pltpu.SemaphoreType.REGULAR
    half = (2, 2, 2, 2, 32, 1024)
    outs = [
        S((2, 256, 1024), BF), S((2, 256, 1024), F32), S((32, 3072), F32), S((32, 1024), F32), S((32, 4096), F32), S((128, 1024), F32),
        S((32, 6144), F32), S((1, 6144), F32), S((64, 128), F32), S((4, 2, 16, 128), F32),
        S((2, 4, 2, 2, 2, 32, 1024), BF), S((2, 256, 1024), BF), S((512, 1024), BF), S(half, BF), S((2,) + half, BF), S((2,) + half, BF), S(half, BF),
        S((512, 1024), BF),
    ]
    scratch = [
        V((8, 4, 2, 2, 2, 32, 1024), BF), V((4, 4, 2, 2, 2, 2, 2, 32, 256), BF), V((4, 2, 2, 2, 2, 32, 1024), BF), V((4, 4, 2, 2, 32, 1024), BF),
        *[V(shape, BF) for step in LANDING for shape in step],
        V((2,) + half, BF), V((2, 512, 1024), BF), V((512, 1024), BF), V((512, 1024), BF), V((512, 1024), F32), V((512, 1024), F32), V((512, 1024), F32),
        V((2, 256, 1024), BF), V((2, 256, 1024), BF), V((3, 32, 1024), F32), V((8, 8, 512), F32),
        V((4, 2, 2, 2, 24, 128), F32), V((2, 4, 2, 48, 128), F32), V((4, 2, 48, 128), F32), V((4, 48, 128), F32), V((3, 48, 128), F32),
        V((48, 128), F32), V((48, 128), F32), V((32, 6144), BF), V((16, 128), F32), V((8, 1024), F32), V((1, 8192), F32), V((13, 8, 1024), F32),
        V((48, 128), F32), V((48, 128), F32), V((2, 4, 2, 48, 128), BF), V((64, 128), F32), V((64, 128), F32), V((9, 64, 128), F32),
        V((4, 2, 16, 128), F32), V((4, 16, 128), F32), V((1, 6144), F32),
        dma((12, 4, 3, 3)), dma((12, 4, 3, 3)), dma((12,)), dma((12,)), dma((12, 4, 7)), dma((12, 4, 7)), dma((12,)), dma((12,)), dma((4, 2)), dma((4, 2)),
        regular((12,)), regular((4,)), regular, dma((14,)), dma((14,)), dma((22,)), dma((22,)), dma((6,)), dma((6,)),
        dma((15,)), dma((40,)), dma((48,)), dma((12,)),
    ]
    return pl.pallas_call(
        block_kernel,
        out_shape=outs,
        in_specs=[ANY, ANY, VM, VM, VM, VM, VM, VM, ANY, ANY, ANY, ANY, ANY],
        out_specs=[ANY] * len(outs),
        scratch_shapes=scratch,
        compiler_params=pltpu.CompilerParams(collective_id=0, has_side_effects=True, vmem_limit_bytes=63 * 2**20),
        cost_estimate=pl.CostEstimate(flops=6 * 10**10, bytes_accessed=10**8, transcendentals=2 * 10**7),
    )(lat, cot, cond, b_mod, b_qv, b_out, b_up, b_down, w_mod, w_qkv, w_out, w_up, w_down.reshape(2, 2, 32, 1024))[:10]


def finish_kernel(h_out, h_gl, h_qkv, h_wo, h_up, h_dn, h_mod, bmod, bias, gcond, cond, o_out, o_gl, o_cond, o_mod, o_bmod, o_qkv, o_bqv, o_wo, o_bo, o_up, o_bu, o_dn, o_bd, v_out, v_gl, v_qkv, v_wo, v_up, v_dn, v_mod, sem_in, sem_out):
    ways = (
        (h_gl, v_gl, o_gl), (h_out, v_out, o_out), (h_mod, v_mod, o_mod), (h_up, v_up, o_up), (h_dn, v_dn, o_dn), (h_qkv, v_qkv, o_qkv), (h_wo, v_wo, o_wo),
    )
    into = [pltpu.make_async_copy(src, mid, sem_in.at[i]) for i, (src, mid, _) in enumerate(ways)]
    copies = [pltpu.make_async_copy(mid, dst, sem_out.at[i]) for i, (_, mid, dst) in enumerate(ways)]
    for copy in into:
        copy.start()
    for first, then in zip(into, copies):
        first.wait()
        then.start()
    dp, sq = lax.axis_index("dp"), lax.axis_index("seq")
    index = dp * (YN * CN) + sq

    def pick(values, row):
        return jnp.sum(jnp.where(lax.broadcasted_iota(jnp.int32, values.shape, 0) == row, values, 0.0), 0, keepdims=True)

    def lanes(row, size, at_):
        total = jnp.where(at_ == 0, row[:, 0:size], 0.0)
        for k in range(1, 128 // size):
            total = jnp.where(at_ == k, row[:, size * k : size * k + size], total)
        return total

    o_bqv[...] = lanes(pick(bias[0:16, :], index // 2), 64, lax.rem(index, 2))
    o_bo[...] = lanes(pick(bias[16:24, :], index // 4), 32, lax.rem(index, 4))
    o_bu[...] = pick(bias[24:56, :], index)
    o_bd[...] = lanes(pick(bias[56:64, :], index // 4), 32, lax.rem(index, 4))
    wide = bmod[0:1, pl.ds(pl.multiple_of((index // 2) * 384 + lax.rem(index, 2) * 128, 128), 256)]
    o_bmod[...] = jnp.where(lax.rem(index, 2) == 0, wide[:, 0:192], wide[:, 64:256])
    for m in range(2):
        for p in range(8):
            v = cond[m : m + 1, 128 * p : 128 * p + 128].astype(F32)
            gate = 1.0 / (1.0 + jnp.exp(-v))
            o_cond[m : m + 1, 128 * p : 128 * p + 128] = pick(gcond[p, 8 * m : 8 * m + 8, :], dp) * (gate * (1.0 + v * (1.0 - gate)))
    for copy in copies:
        copy.wait()


def per_device_kernels(latents, conditioning, w_mod, b_mod, w_qkv, b_qv, w_out, b_out, w_up, b_up, w_down, b_down, cotangent):
    cond = conditioning[:, 0]
    output, grad_lat, g_qkv, g_out, g_up, g_down, g_mod, gb_mod, gb_all, g_cond = run_block(
        latents[:, 0], cotangent[:, 0], cond, b_mod, b_qv, b_out, b_up, b_down, w_mod[0], w_qkv[0], w_out[0], w_up[0], w_down[0]
    )
    S = jax.ShapeDtypeStruct
    shapes = [
        S((2, 256, 1024), BF), S((2, 256, 1024), F32), S((2, 1024), F32), S((32, 6144), F32), S((1, 192), F32), S((32, 3072), F32), S((1, 64), F32),
        S((32, 1024), F32), S((1, 32), F32), S((32, 4096), F32), S((1, 128), F32), S((128, 1024), F32), S((1, 32), F32),
    ]
    (out, gl, gc, mod, bmod, qkv, bqv, wo, bo, up, bu, dn, bd) = pl.pallas_call(
        finish_kernel,
        out_shape=shapes,
        in_specs=[ANY] * 7 + [VM] * 4,
        out_specs=[ANY, ANY, VM, ANY, VM, ANY, VM, ANY, VM, ANY, VM, ANY, VM],
        scratch_shapes=[pltpu.VMEM(s.shape, s.dtype) for s in (output, grad_lat, g_qkv, g_out, g_up, g_down, g_mod)]
        + [pltpu.SemaphoreType.DMA((7,)), pltpu.SemaphoreType.DMA((7,))],
        cost_estimate=pl.CostEstimate(flops=10**6, bytes_accessed=10**7, transcendentals=2048),
    )(output, grad_lat, g_qkv, g_out, g_up, g_down, g_mod, gb_mod, gb_all, g_cond.reshape(8, 16, 128), cond)
    return (out[:, None], gl[:, None], gc[:, None], mod[None], bmod, qkv[None], bqv, wo[None], bo, up[None], bu, dn[None], bd)


def solution(mesh):
    placed = (
        P(None, "dp", "seq", None),
        P(None, "dp", None),
        P(None, ("dp", "seq"), None),
        P(None, ("dp", "seq")),
        P(None, ("dp", "seq"), None),
        P(None, ("dp", "seq")),
        P(None, ("dp", "seq"), None),
        P(None, ("dp", "seq")),
        P(None, ("dp", "seq"), None),
        P(None, ("dp", "seq")),
        P(None, ("dp", "seq"), None),
        P(None, ("dp", "seq")),
        P(None, "dp", "seq", None),
    )
    return jax.shard_map(
        per_device_kernels if dict(mesh.shape) == {"dp": 8, "seq": 4} else per_device,
        mesh=mesh,
        in_specs=placed,
        out_specs=(
            P(None, "dp", "seq", None),
            P(None, "dp", "seq", None),
            P(None, "dp", None),
            P(None, ("dp", "seq"), None),
            P(None, ("dp", "seq")),
            P(None, ("dp", "seq"), None),
            P(None, ("dp", "seq")),
            P(None, ("dp", "seq"), None),
            P(None, ("dp", "seq")),
            P(None, ("dp", "seq"), None),
            P(None, ("dp", "seq")),
            P(None, ("dp", "seq"), None),
            P(None, ("dp", "seq")),
        ),
        check_vma=False,
    )
```

```python
import jax
import jax.numpy as jnp
from jax import lax
from jax.sharding import PartitionSpec as P
from jax.experimental import pallas as pl
from jax.experimental.pallas import tpu as pltpu

EPS = 1e-06
HEADS = 16


def modulate(stream, shift_vec, scale_vec):
    row_mean = jnp.mean(stream, -1, keepdims=True)
    centred = stream - row_mean
    row_var = jnp.mean(centred * centred, -1, keepdims=True)
    return centred * lax.rsqrt(row_var + EPS) * (1.0 + scale_vec) + shift_vec


def gelu_tanh(values):
    return jax.nn.gelu(values, approximate=True)


def matmul(left, right):
    return jnp.dot(left, right, preferred_element_type=jnp.float32)


def weight_grad(inputs, upstream):
    return jnp.einsum("ti,to->io", inputs, upstream, preferred_element_type=jnp.float32)


def input_grad(upstream, weight):
    return jnp.einsum("to,io->ti", upstream, weight, preferred_element_type=jnp.float32)


def column_sums(values):
    return jnp.sum(values.astype(jnp.float32), 0)


def gather_once(params, layer_index):
    return (
        lax.all_gather(params[0][layer_index], ("dp", "seq"), axis=0, tiled=True),
        lax.all_gather(params[1][layer_index], ("dp", "seq"), axis=0, tiled=True),
        lax.all_gather(params[2][layer_index], ("dp", "seq"), axis=0, tiled=True),
        lax.all_gather(params[3][layer_index], ("dp", "seq"), axis=0, tiled=True),
        lax.all_gather(params[4][layer_index], ("dp", "seq"), axis=0, tiled=True),
        lax.all_gather(params[5][layer_index], ("dp", "seq"), axis=0, tiled=True),
        lax.all_gather(params[6][layer_index], ("dp", "seq"), axis=0, tiled=True),
        lax.all_gather(params[7][layer_index], ("dp", "seq"), axis=0, tiled=True),
        lax.all_gather(params[8][layer_index], ("dp", "seq"), axis=0, tiled=True),
        lax.all_gather(params[9][layer_index], ("dp", "seq"), axis=0, tiled=True),
    )


def owner_layout(grad, dp_count, seq_count):
    per_owner = grad.shape[1] // (dp_count * seq_count)
    shaped = grad.reshape((grad.shape[0], dp_count, seq_count, per_owner) + grad.shape[2:])
    return jnp.moveaxis(shaped, 0, 2)


def attend(query, keys, values):
    head_size = query.shape[1] // HEADS
    query_rows = query.reshape(query.shape[0], HEADS, head_size)
    key_rows = keys.reshape(keys.shape[0], HEADS, head_size)
    value_rows = values.reshape(values.shape[0], HEADS, head_size)
    scores = jnp.einsum(
        "qhd,khd->hqk", query_rows, key_rows, preferred_element_type=jnp.float32
    ) * head_size ** (-0.5)
    row_max = jnp.max(scores, -1, keepdims=True)
    expon = jnp.exp(scores - row_max)
    row_sum = jnp.sum(expon, -1, keepdims=True)
    probs_low = (expon / row_sum).astype(jnp.bfloat16)
    attended = jnp.einsum("hqk,khd->qhd", probs_low, value_rows, preferred_element_type=jnp.float32)
    return (attended.reshape(query.shape[0], -1).astype(jnp.bfloat16), row_max + jnp.log(row_sum))


def attend_back(query, keys, values, log_total, grad_attended):
    head_size = query.shape[1] // HEADS
    inv_root = head_size ** (-0.5)
    query_rows = query.reshape(query.shape[0], HEADS, head_size)
    key_rows = keys.reshape(keys.shape[0], HEADS, head_size)
    value_rows = values.reshape(values.shape[0], HEADS, head_size)
    grad_rows = grad_attended.reshape(query.shape[0], HEADS, head_size)
    scores = (
        jnp.einsum("qhd,khd->hqk", query_rows, key_rows, preferred_element_type=jnp.float32)
        * inv_root
    )
    probs = jnp.exp(scores - log_total)
    grad_probs = jnp.einsum(
        "qhd,khd->hqk", grad_rows, value_rows, preferred_element_type=jnp.float32
    )
    row_dot = jnp.sum(probs * grad_probs, -1, keepdims=True)
    grad_scores = (probs * (grad_probs - row_dot)).astype(jnp.bfloat16)
    grad_query = (
        jnp.einsum("hqk,khd->qhd", grad_scores, key_rows, preferred_element_type=jnp.float32)
        * inv_root
    )
    grad_keys = (
        jnp.einsum("hqk,qhd->khd", grad_scores, query_rows, preferred_element_type=jnp.float32)
        * inv_root
    )
    grad_values = jnp.einsum(
        "hqk,qhd->khd", probs.astype(jnp.bfloat16), grad_rows, preferred_element_type=jnp.float32
    )
    return (
        grad_query.reshape(query.shape[0], -1),
        grad_keys.reshape(keys.shape[0], -1),
        grad_values.reshape(values.shape[0], -1),
    )


def forward_layer(stream, cond_act, gathered):
    w_mod, b_mod, w_qkv, b_qv, w_out, b_out, w_up, b_up, w_down, b_down = gathered
    model_width = stream.shape[1]
    modulation = matmul(cond_act, w_mod)[0] + b_mod.astype(jnp.float32)
    shift_attn, scale_attn, gate_attn, shift_mlp, scale_mlp, gate_mlp = jnp.split(modulation, 6)
    mixed1 = modulate(stream, shift_attn, scale_attn).astype(jnp.bfloat16)
    qkv = matmul(mixed1, w_qkv)
    qv_bias = b_qv.astype(jnp.float32)
    query = (qkv[:, :model_width] + qv_bias[:model_width]).astype(jnp.bfloat16)
    keys = qkv[:, model_width : 2 * model_width].astype(jnp.bfloat16)
    values = (qkv[:, 2 * model_width :] + qv_bias[model_width:]).astype(jnp.bfloat16)
    all_keys, all_values = (
        lax.all_gather(keys, "seq", axis=0, tiled=True),
        lax.all_gather(values, "seq", axis=0, tiled=True),
    )
    attended, log_total = attend(query, all_keys, all_values)
    attn_out = matmul(attended, w_out) + b_out.astype(jnp.float32)
    resid = stream + gate_attn * attn_out
    mixed2 = modulate(resid, shift_mlp, scale_mlp).astype(jnp.bfloat16)
    preact = matmul(mixed2, w_up) + b_up.astype(jnp.float32)
    activation = gelu_tanh(preact).astype(jnp.bfloat16)
    branch = matmul(activation, w_down) + b_down.astype(jnp.float32)
    saved_acts = (
        stream,
        modulation,
        query,
        all_keys,
        all_values,
        log_total,
        attended,
        attn_out,
        resid,
        preact,
        branch,
    )
    return (resid + gate_mlp * branch, saved_acts)


def backward_layer(gradient, saved_acts, gathered, cond_act):
    w_mod, b_mod, w_qkv, b_qv, w_out, b_out, w_up, b_up, w_down, b_down = gathered
    (
        stream,
        modulation,
        query,
        all_keys,
        all_values,
        log_total,
        attended,
        attn_out,
        resid,
        preact,
        branch,
    ) = saved_acts
    model_width = stream.shape[1]
    shift_attn, scale_attn, gate_attn, shift_mlp, scale_mlp, gate_mlp = jnp.split(modulation, 6)
    grad_branch = (gradient * gate_mlp).astype(jnp.bfloat16)
    grad_gate_mlp = jnp.sum(gradient * branch, 0)
    activation_f, gelu_pull = jax.vjp(gelu_tanh, preact)
    activation = activation_f.astype(jnp.bfloat16)
    grad_b_down = column_sums(grad_branch)
    grad_preact = gelu_pull(input_grad(grad_branch, w_down))[0].astype(jnp.bfloat16)
    mixed2_f, norm_pull_mlp = jax.vjp(modulate, resid, shift_mlp, scale_mlp)
    mixed2 = mixed2_f.astype(jnp.bfloat16)
    grad_b_up = column_sums(grad_preact)
    grad_resid_norm, grad_shift_mlp, grad_scale_mlp = norm_pull_mlp(input_grad(grad_preact, w_up))
    grad_resid = gradient + grad_resid_norm
    grad_attn = (grad_resid * gate_attn).astype(jnp.bfloat16)
    grad_gate_attn = jnp.sum(grad_resid * attn_out, 0)
    grad_b_out = column_sums(grad_attn)
    grad_attended = input_grad(grad_attn, w_out).astype(jnp.bfloat16)
    grad_query, grad_keys_all, grad_values_all = attend_back(
        query, all_keys, all_values, log_total, grad_attended
    )
    grad_keys, grad_values = (
        lax.psum_scatter(
            grad_keys_all.astype(jnp.bfloat16), "seq", scatter_dimension=0, tiled=True
        ).astype(jnp.float32),
        lax.psum_scatter(
            grad_values_all.astype(jnp.bfloat16), "seq", scatter_dimension=0, tiled=True
        ).astype(jnp.float32),
    )
    grad_qkv = jnp.concatenate(
        [
            grad_query.astype(jnp.bfloat16),
            grad_keys.astype(jnp.bfloat16),
            grad_values.astype(jnp.bfloat16),
        ],
        1,
    )
    mixed1_f, norm_pull_attn = jax.vjp(modulate, stream, shift_attn, scale_attn)
    mixed1 = mixed1_f.astype(jnp.bfloat16)
    qkv_sums = column_sums(grad_qkv)
    grad_b_qv = jnp.concatenate([qkv_sums[:model_width], qkv_sums[2 * model_width :]])
    grad_stream_norm, grad_shift_attn, grad_scale_attn = norm_pull_attn(input_grad(grad_qkv, w_qkv))
    grad_stream = grad_resid + grad_stream_norm
    grad_mod_part = jnp.concatenate(
        [
            grad_shift_attn,
            grad_scale_attn,
            grad_gate_attn,
            grad_shift_mlp,
            grad_scale_mlp,
            grad_gate_mlp,
        ]
    )
    grad_mod = lax.psum(grad_mod_part, "seq").astype(jnp.bfloat16)
    seq_share = 1.0 / lax.axis_size("seq")
    grad_b_mod = grad_mod.astype(jnp.float32) * seq_share
    grad_cond_act = input_grad(grad_mod[None], w_mod)
    operands = (
        activation,
        grad_branch,
        mixed2,
        grad_preact,
        attended,
        grad_attn,
        mixed1,
        grad_qkv,
        cond_act,
        grad_mod[None],
    )
    bias_terms = (grad_b_mod, grad_b_qv, grad_b_out, grad_b_up, grad_b_down)
    return (grad_stream, grad_cond_act, operands, bias_terms)


def per_device(
    latents,
    conditioning,
    w_mod,
    b_mod,
    w_qkv,
    b_qv,
    w_out,
    b_out,
    w_up,
    b_up,
    w_down,
    b_down,
    cotangent,
):
    params = (w_mod, b_mod, w_qkv, b_qv, w_out, b_out, w_up, b_up, w_down, b_down)
    layer_count = w_mod.shape[0]
    micro_count = latents.shape[0]
    seq_share = 1.0 / lax.axis_size("seq")
    stored = [gather_once(params, 0)]
    kept_operands = [[]]
    bias_totals = [None] * layer_count
    outputs = []
    grads_in = []
    grads_cond = []
    for micro_step in range(micro_count):
        stream = latents[micro_step, 0].astype(jnp.float32)
        cond_row = conditioning[micro_step, 0:1].astype(jnp.float32)
        cond_act = jax.nn.silu(cond_row).astype(jnp.bfloat16)
        layer_index = 0
        gathered = stored[layer_index]
        stream, saved_acts = forward_layer(stream, cond_act, gathered)
        saved_list = [saved_acts]
        outputs.append(stream.astype(jnp.bfloat16))
        gradient = cotangent[micro_step, 0].astype(jnp.float32)
        grad_cond_act = jnp.zeros(cond_row.shape, jnp.float32)
        for layer_index in reversed(range(layer_count)):
            gathered = stored[layer_index]
            gradient, grad_cond_part, operands, bias_terms = backward_layer(
                gradient, saved_list[layer_index], gathered, cond_act
            )
            grad_cond_act = grad_cond_part
            kept_operands[layer_index].append(operands)
            if bias_totals[layer_index] is None:
                bias_totals[layer_index] = bias_terms
            else:
                bias_totals[layer_index] = tuple(
                    (first + second for first, second in zip(bias_totals[layer_index], bias_terms))
                )
        grads_in.append(gradient)
        silu_pull = jax.vjp(jax.nn.silu, cond_row)[1]
        grads_cond.append(silu_pull(grad_cond_act)[0])
    layer_index = 0
    joined = [
        jnp.concatenate(
            [kept_operands[layer_index][step][member] for step in range(micro_count)], 0
        )
        for member in range(10)
    ]
    grad_w_down = weight_grad(joined[0], joined[1])
    grad_w_up = weight_grad(joined[2], joined[3])
    grad_w_out = weight_grad(joined[4], joined[5])
    grad_w_qkv = weight_grad(joined[6], joined[7])
    grad_w_mod = weight_grad(joined[8], joined[9]) * seq_share
    grad_b_mod, grad_b_qv, grad_b_out, grad_b_up, grad_b_down = bias_totals[layer_index]
    totals = (
        grad_w_mod,
        grad_b_mod,
        grad_w_qkv,
        grad_b_qv,
        grad_w_out,
        grad_b_out,
        grad_w_up,
        grad_b_up,
        grad_w_down,
        grad_b_down,
    )
    dp_count = lax.axis_size("dp")
    seq_count = lax.axis_size("seq")
    stacked = [
        owner_layout(jnp.stack([totals[member]]), dp_count, seq_count) for member in range(10)
    ]
    flat = [member.reshape((dp_count * seq_count,) + member.shape[2:]) for member in stacked]
    owned = (
        lax.psum_scatter(flat[0], ("dp", "seq"), scatter_dimension=0, tiled=True),
        lax.psum_scatter(flat[1], ("dp", "seq"), scatter_dimension=0, tiled=True),
        lax.psum_scatter(flat[2], ("dp", "seq"), scatter_dimension=0, tiled=True),
        lax.psum_scatter(flat[3], ("dp", "seq"), scatter_dimension=0, tiled=True),
        lax.psum_scatter(flat[4], ("dp", "seq"), scatter_dimension=0, tiled=True),
        lax.psum_scatter(flat[5], ("dp", "seq"), scatter_dimension=0, tiled=True),
        lax.psum_scatter(flat[6], ("dp", "seq"), scatter_dimension=0, tiled=True),
        lax.psum_scatter(flat[7], ("dp", "seq"), scatter_dimension=0, tiled=True),
        lax.psum_scatter(flat[8], ("dp", "seq"), scatter_dimension=0, tiled=True),
        lax.psum_scatter(flat[9], ("dp", "seq"), scatter_dimension=0, tiled=True),
    )
    shards = [
        member.reshape(member.shape[member.ndim - stacked_member.ndim + 2 :])
        for member, stacked_member in zip(owned, stacked)
    ]
    output = jnp.stack(outputs)[:, None]
    grad_latents = jnp.stack(grads_in)[:, None]
    grad_cond = jnp.stack(grads_cond)
    return (
        output,
        grad_latents,
        grad_cond,
        shards[0],
        shards[1],
        shards[2],
        shards[3],
        shards[4],
        shards[5],
        shards[6],
        shards[7],
        shards[8],
        shards[9],
    )


MESH_IDS = pl.DeviceIdType.MESH
ANY = pl.BlockSpec(memory_space=pl.ANY)
VM = pl.BlockSpec(memory_space=pltpu.VMEM)
F32, BF = jnp.float32, jnp.bfloat16
ALL = slice(None)
ZN, XN, YN, CN = 4, 2, 2, 2
TOK = 512
CUT = 512
ROOT_2_PI = 0.7978845608028654


def dot_nn(left, right):
    return lax.dot_general(left, right, (((1,), (0,)), ((), ())), preferred_element_type=F32)


def dot_nt(left, right):
    return lax.dot_general(left, right, (((1,), (1,)), ((), ())), preferred_element_type=F32)


def dot_tn(left, right):
    return lax.dot_general(left, right, (((0,), (0,)), ((), ())), preferred_element_type=F32)


class Place:
    def __init__(self):
        dp, sq = lax.axis_index("dp"), lax.axis_index("seq")
        self.dp, self.sq = dp, sq
        self.z, self.x = dp // XN, dp % XN
        self.y, self.c = sq // CN, sq % CN
        self.xp = (self.z * XN + 1 - self.x, sq)
        self.yp = (dp, (1 - self.y) * CN + self.c)
        self.cp = (dp, self.y * CN + 1 - self.c)

    def z_to(self, k):
        return (lax.rem(self.z + k, ZN) * XN + self.x, self.sq)

    def z_at(self, z):
        return (z * XN + self.x, self.sq)

    def z_from(self, k):
        return lax.rem(self.z + ZN - k, ZN)

    def barrier(self):
        sem = pltpu.get_barrier_semaphore()
        peers = [self.z_to(1), self.z_to(2), self.z_to(3), self.xp, self.yp, self.cp]
        for peer in peers:
            pl.semaphore_signal(sem, inc=1, device_id=peer, device_id_type=MESH_IDS)
        pl.semaphore_wait(sem, len(peers))


class Links:
    def __init__(self):
        self.sent = []

    def copy(self, src, dst, send_sem, recv_sem, peer):
        return pltpu.make_async_remote_copy(
            src_ref=src, dst_ref=dst, send_sem=send_sem, recv_sem=recv_sem, device_id=peer, device_id_type=MESH_IDS
        )

    def send(self, src, dst, send_sem, recv_sem, peer, when=None):
        copy = self.copy(src, dst, send_sem, recv_sem, peer)
        guarded(when, copy.start)
        self.sent.append((copy, when))

    def drain(self):
        for copy, when in self.sent:
            guarded(when, copy.wait_send)
        self.sent = []


def pieces_of(rows, cols):
    if rows == 32:
        return (
            ("zyx", (pl.ds(0, 16), pl.ds(0, cols))),
            ("zxy", (pl.ds(16, 16), pl.ds(0, CUT))),
            ("yxz", (pl.ds(16, 16), pl.ds(CUT, cols - CUT))),
        )
    return (("zyx", (0,)), ("zxy", (1, 0)), ("yxz", (1, 1)))


def line_gather(at, idx_of):
    z = at.z
    inner, outer = (z == 1) | (z == 2), (z == 0) | (z == 3)
    near = jnp.where(z == 1, 0, 3)
    return (
        [
            (idx_of(z), at.z_at(jnp.minimum(z + 1, 3)), idx_of(jnp.maximum(z - 1, 0)), z < 3, z > 0),
            (idx_of(z), at.z_at(jnp.maximum(z - 1, 0)), idx_of(jnp.minimum(z + 1, 3)), z > 0, z < 3),
        ],
        [
            (idx_of(3 - z), at.z_at(near), idx_of(jnp.where(z == 0, 2, 1)), inner, outer),
            (idx_of(near), at.z_at(jnp.where(z == 1, 2, 1)), idx_of(jnp.where(z == 2, 0, 3)), inner, inner),
            (idx_of(near), at.z_at(3 - near), idx_of(jnp.where(z == 3, 0, 3)), inner, outer),
        ],
    )


def gather_steps(at, kind):
    z, x, y, c = at.z, at.x, at.y, at.c
    if kind == "yxz":
        return (
            [((z, x, y, c), at.yp, (z, x, 1 - y, c), None, None)],
            [((z, x, ALL, c), at.xp, (z, 1 - x, ALL, c), None, None)],
            *line_gather(at, lambda q: (q, ALL, ALL, c)),
        )
    first = line_gather(at, lambda q: (q, x, y, c))
    if kind == "zyx":
        return (
            *first,
            [((ALL, x, y, c), at.yp, (ALL, x, 1 - y, c), None, None)],
            [((ALL, x, ALL, c), at.xp, (ALL, 1 - x, ALL, c), None, None)],
        )
    return (
        *first,
        [((ALL, x, y, c), at.xp, (ALL, 1 - x, y, c), None, None)],
        [((ALL, ALL, y, c), at.yp, (ALL, ALL, 1 - y, c), None, None)],
    )


def line_scatter(at):
    z = at.z
    inner, outer = (z == 1) | (z == 2), (z == 0) | (z == 3)
    return (
        [
            (jnp.where(z == 0, 2, 1), jnp.where(z == 0, 1, 2), 0, outer, inner),
            (jnp.where(z == 2, 0, 3), 3 - z, 1, inner, inner),
            (3 - z, jnp.where(z == 0, 2, 1), 2, outer, inner),
        ],
        [(jnp.minimum(z + 1, 3), jnp.minimum(z + 1, 3), 0, z < 3, z > 0), (jnp.maximum(z - 1, 0), jnp.maximum(z - 1, 0), 1, z > 0, z < 3)],
    )


def guarded(condition, action):
    if condition is None:
        action()
    else:
        pl.when(condition)(action)


def norm_rows(values):
    centred = values - jnp.mean(values, -1, keepdims=True)
    inv = lax.rsqrt(jnp.mean(centred * centred, -1, keepdims=True) + EPS)
    return centred * inv, inv


def scatter_steps(at):
    z, x, y = at.z, at.x, at.y

    def line(piece, number, block):
        return [(piece, block(q), at.z_at(to), slot, sends, receives) for q, to, slot, sends, receives in line_scatter(at)[number]]

    def ends(q):
        return (q, x, y)

    return (
        [(0, (ALL, 1 - x, ALL), at.xp, None, None, None), (1, (ALL, ALL, 1 - y), at.yp, None, None, None)] + line(2, 0, lambda q: (q, ALL, ALL)),
        [(0, (ALL, x, 1 - y), at.yp, None, None, None), (1, (ALL, 1 - x, y), at.xp, None, None, None)] + line(2, 1, lambda q: (q, ALL, ALL)),
        line(0, 0, ends) + line(1, 0, ends) + [(2, (z, 1 - x, ALL), at.xp, None, None, None)],
        line(0, 1, ends) + line(1, 1, ends) + [(2, (z, x, 1 - y), at.yp, None, None, None)],
    )


LR = 5
PIECE_ROWS = (slice(0, 16), slice(16, 32), slice(16, 32))
PIECE_COLS = (slice(0, 1024), slice(0, CUT), slice(CUT, 1024))
LANDING = (
    ((LR, 4, 2, 16, 1024), (LR, 4, 2, 16, CUT), (LR, 3, 2, 2, 16, 1024 - CUT)),
    ((LR, 4, 16, 1024), (LR, 4, 16, CUT), (LR, 2, 2, 2, 16, 1024 - CUT)),
    ((LR, 3, 16, 1024), (LR, 3, 16, CUT), (LR, 2, 16, 1024 - CUT)),
    ((LR, 2, 16, 1024), (LR, 2, 16, CUT), (LR, 16, 1024 - CUT)),
)


RB = 128


def block_kernel(
    lat, cot, cond_in, b_mod, b_qv, b_out, b_up, b_down, w_mod, w_qkv, w_out, w_up, w_down,
    o_out, o_gl, o_qkv, o_wo, o_up, o_dn, o_mod, o_bmod, o_bias, o_gc, t_w, t_x, t_m1, t_q, t_k, t_v, t_att, t_ao,
    W8, WD, CR, RC, L00, L01, L02, L10, L11, L12, L20, L21, L22, L30, L31, L32,
    act, gp, m2, gb, res, acc, br, cs, xs, fin, lse,
    SM, PM, PY, PX, PZ, FM, PC, wm, cact, vec, bias, sums, GS, GP, GM, bsum, BA, BB, GC, GCX, brow,
    gs, gr, gcs, gcr, rss, rsr, rcs, rcr, dcs, dcr, credit, credit_c, ready_c, sx, rx, sy, ry, ssm, rsm, lw, lo, ld, lf,
):
    at = Place()
    z, x, y, c = at.z, at.x, at.y, at.c
    links = Links()
    lane = lax.broadcasted_iota(jnp.int32, (1, 128), 1)
    inner = (z == 1) | (z == 2)
    near = jnp.where(z == 1, 0, 3)

    outgoing = []

    def save(src, dst):
        copy = pltpu.make_async_copy(src, dst, lo.at[len(outgoing)])
        copy.start()
        outgoing.append(copy)
        return copy

    loads = {}

    def load(name, src, dst):
        copy = pltpu.make_async_copy(src, dst, ld.at[len(loads)])
        copy.start()
        loads[name] = copy

    def loaded(name):
        loads[name].wait()

    ORDER = (0, 1, 2, 3, 8, 9, 10, 11, 4, 5, 6, 7)
    plans = {kind: gather_steps(at, kind) for kind in ("zyx", "zxy", "yxz")}

    def block(unit, idx, part=()):
        ref = W8.at[unit] if unit < 8 else WD.at[unit - 8]
        return ref.at[idx + part]

    def shard(unit):
        if unit < 3:
            return w_qkv.at[:, pl.ds((1024, 2048, 0)[unit], 1024)]
        if unit == 3:
            return w_out
        if unit < 8:
            return w_up.at[:, pl.ds((unit - 4) * 1024, 1024)]
        return w_down.at[:, :, :, pl.ds((unit - 8) * 256, 256)]

    def pieces(unit):
        return pieces_of(32, 1024) if unit < 8 else pieces_of(128, 256)

    gather_sent = {unit: [] for unit in range(12)}
    steps_at = {}
    for i, (kind, _) in enumerate(pieces(0)):
        for number in range(4):
            for j in range(len(plans[kind][number])):
                steps_at[number, i, j] = len(steps_at)

    def gather_sems(unit, number, i, j):
        k = steps_at[number, i, j]
        return gs.at[ORDER.index(unit) % 7, k], gr.at[unit, k]

    def step(unit, number):
        for i, (kind, part) in enumerate(pieces(unit)):
            for j, (idx, peer, _, sends, _) in enumerate(plans[kind][number]):
                ref = block(unit, idx, part)
                copy = links.copy(ref, ref, *gather_sems(unit, number, i, j), peer)
                guarded(sends, copy.start)
                gather_sent[unit].append((copy, sends))

    def arrived(unit, number):
        for i, (kind, part) in enumerate(pieces(unit)):
            for j, (_, peer, idx, _, receives) in enumerate(plans[kind][number]):
                ref = block(unit, idx, part)
                guarded(receives, links.copy(ref, ref, *gather_sems(unit, number, i, j), peer).wait_recv)

    local_w = [pltpu.make_async_copy(shard(u), block(u, (z, x, y, c)), lw.at[u]) for u in range(12)]

    def gather_stage(unit, number):
        if number == 0:
            if ORDER.index(unit) >= 7:
                gather_done(ORDER[ORDER.index(unit) - 7])
            local_w[unit].wait()
        else:
            arrived(unit, number - 1)
        if number < 4:
            step(unit, number)
        else:
            ref = block(unit, (ALL, ALL, ALL, c))
            copy = links.copy(ref, ref, gcs.at[unit], gcr.at[unit], at.cp)
            copy.start()
            gather_sent[unit].append((copy, None))

    def ready(unit):
        ref = block(unit, (ALL, ALL, ALL, 1 - c))
        links.copy(ref, ref, gcs.at[unit], gcr.at[unit], at.cp).wait_recv()

    def gather_tick(t):
        for number in (1, 2, 3):
            if 0 <= t + 1 - number < 12:
                gather_stage(ORDER[t + 1 - number], number)
        if t + 3 < 12:
            gather_stage(ORDER[t + 3], 0)
        if 0 <= t - 3 < 12:
            gather_stage(ORDER[t - 3], 4)

    def gather_done(unit):
        for copy, sends in gather_sent.pop(unit, ()):
            guarded(sends, copy.wait_send)

    scatter_plan = scatter_steps(at)
    landing = ((L00, L01, L02), (L10, L11, L12), (L20, L21, L22), (L30, L31, L32))
    unit_sent = [[] for _ in range(12)]
    finished = set()

    def at_block(n, idx):
        if 4 <= n < 8:
            return CR, idx + ((n - 4) // 2, (n - 4) % 2)
        return RC, (n % 4 if n < 4 else n - 8,) + idx

    def part_ref(n, idx, piece):
        ref, full = at_block(n, idx)
        return ref.at[full + (PIECE_ROWS[piece], PIECE_COLS[piece])]

    def copies(n, number):
        result = []
        for i, (piece, go, peer, slot, sends, receives) in enumerate(scatter_plan[number]):
            dst = landing[number][piece].at[n % LR]
            dst = dst if slot is None else dst.at[slot]
            k = (0, 5, 9, 16)[number] + i
            result.append((links.copy(part_ref(n, go, piece), dst, rss.at[n % LR, k], rsr.at[n % LR, k], peer), sends, receives))
        return result

    def send_step(n, number):
        for copy, sends, _ in copies(n, number):
            guarded(sends, copy.start)
            unit_sent[n].append((copy, sends))

    def add_into(n, number):
        for copy, _, receives in copies(n, number):
            guarded(receives, copy.wait_recv)
        s = n % LR

        def plus(idx, piece, *came):
            ref, full = at_block(n, idx)
            full = full + (PIECE_ROWS[piece], PIECE_COLS[piece])
            if len(came) == 1:
                ref[full] = ref[full] + came[0]
            else:
                ref[full] = (ref[full].astype(F32) + (came[0].astype(F32) + came[1].astype(F32))).astype(BF)

        if number == 0:
            def add(i, carry):
                for e in range(2):
                    plus((i, x, e), 0, L00[s, i, e])
                    plus((i, e, y), 1, L01[s, i, e])
                return carry

            lax.fori_loop(0, 4, add, 0)

            @pl.when(inner)
            def _():
                def add_line(i, carry):
                    xi, yi = i // 2, i % 2
                    plus((3 - z, xi, yi), 2, L02[s, 0, xi, yi])
                    plus((near, xi, yi), 2, L02[s, 1, xi, yi], L02[s, 2, xi, yi])
                    return carry

                lax.fori_loop(0, 4, add_line, 0)
        elif number == 1:
            def add(i, carry):
                plus((i, x, y), 0, L10[s, i])
                plus((i, x, y), 1, L11[s, i])
                return carry

            lax.fori_loop(0, 4, add, 0)
            for slot_in, came in ((0, z > 0), (1, z < 3)):
                @pl.when(came)
                def _():
                    def add_line(i, carry):
                        xi, yi = i // 2, i % 2
                        plus((z, xi, yi), 2, L12[s, slot_in, xi, yi])
                        return carry

                    lax.fori_loop(0, 4, add_line, 0)
        elif number == 2:
            @pl.when(inner)
            def _():
                for piece, ref in ((0, L20), (1, L21)):
                    plus((3 - z, x, y), piece, ref[s, 0])
                    plus((near, x, y), piece, ref[s, 1], ref[s, 2])

            for e in range(2):
                plus((z, x, e), 2, L22[s, e])

    cores_sent = {}

    def core_copy(n, d):
        return links.copy(W8.at[d, :, :, :, 1 - c], RC.at[n % 4 if n < 4 else n - 8], rcs.at[n], rcr.at[n], at.cp)

    def slot_free(d):
        for copy in cores_sent.pop(d, ()):
            copy.wait_send()

    def put_grad(n, d, left, right):
        slot_free(d)
        for t in range(2):
            cols = slice(512 * t, 512 * t + 512)
            W8[d, :, :, :, :, :, cols] = dot_tn(left, right(cols)).astype(BF).reshape(4, 2, 2, 2, 32, 512)
        if n >= 8:
            assert n - 8 in finished
            pl.semaphore_wait(credit_c.at[n - 8], 1)
        copy = core_copy(n, d)
        copy.start()
        cores_sent[d] = (copy,)
        slot_of_unit[n] = d
        if n != 8:
            waiting[n] = 1

    slot_of_unit = {}

    def r1(n):
        if not 4 <= n < 8:
            d = slot_of_unit[n]
            core_copy(n, d).wait_recv()
            slot = n % 4 if n < 4 else n - 8

            def add(i, carry):
                zi, xi, yi = i // 4, (i // 2) % 2, i % 2
                RC[slot, zi, xi, yi] = RC[slot, zi, xi, yi] + W8[d, zi, xi, yi, c]
                return carry

            lax.fori_loop(0, 16, add, 0)
        if n >= LR:
            assert n - LR in finished
            pl.semaphore_wait(credit.at[n - LR], 5)
        send_step(n, 0)

    def middle(number):
        def run(n):
            add_into(n, number)
            send_step(n, number + 1)

        return run

    fin_saved = {}

    def r5(n):
        for copy, _, receives in copies(n, 3):
            guarded(receives, copy.wait_recv)
        s, f = n % LR, n % 3
        if n - 3 in fin_saved:
            fin_saved.pop(n - 3).wait()
        ref_, full = at_block(n, (z, x, y))
        for piece, ref in ((0, L30), (1, L31)):
            rows, cols = PIECE_ROWS[piece], PIECE_COLS[piece]
            fin[f, rows, cols] = ref_[full + (rows, cols)].astype(F32)
            for slot_in, came in ((0, z > 0), (1, z < 3)):
                @pl.when(came)
                def _():
                    fin[f, rows, cols] = fin[f, rows, cols] + ref[s, slot_in].astype(F32)
        fin[f, 16:32, CUT:] = ref_[full + (slice(16, 32), slice(CUT, 1024))].astype(F32) + L32[s].astype(F32)
        if n < 4:
            dst = o_up.at[:, pl.ds(1024 * n, 1024)]
        elif n < 8:
            dst = o_dn.at[pl.ds(32 * (n - 4), 32)]
        elif n == 8:
            dst = o_wo
        else:
            dst = o_qkv.at[:, pl.ds(1024 * (n - 9), 1024)]
        fin_saved[n] = pltpu.make_async_copy(fin.at[f], dst, lf.at[f])
        fin_saved[n].start()
        for copy, sends in unit_sent[n]:
            guarded(sends, copy.wait_send)
        if n + LR < 12:
            for peer in (at.z_to(1), at.z_to(2), at.z_to(3), at.xp, at.yp):
                pl.semaphore_signal(credit.at[n], inc=1, device_id=peer, device_id_type=MESH_IDS)
        if n < 4:
            pl.semaphore_signal(credit_c.at[n], inc=1, device_id=at.cp, device_id_type=MESH_IDS)
        finished.add(n)

    stages = {1: r1, 2: middle(0), 3: middle(1), 4: middle(2), 5: r5}
    waiting = {}

    def tick():
        for n in sorted(waiting, reverse=True):
            stages[waiting[n]](n)
            waiting[n] += 1
            if waiting[n] == 6:
                del waiting[n]

    def fold(values):
        return jnp.sum(values.reshape(-1, 8, values.shape[-1]), 0)

    local_m = pltpu.make_async_copy(w_mod, wm, lw.at[12])
    local_x = pltpu.make_async_copy(lat.at[y], xs.at[y], lw.at[13])
    local_c = pltpu.make_async_copy(cot.at[y], cs.at[y], lw.at[14])
    for copy in local_w[:3] + [local_m, local_x] + local_w[3:] + [local_c]:
        copy.start()
    index = at.dp * (YN * CN) + at.sq

    def table(line, value):
        SM[z, x, y, c, line : line + 1, :] = value

    rows_in = cond_in[...].astype(F32)
    for m in range(2):
        for j in range(8):
            table(8 * m + j, rows_in[m : m + 1, 128 * j : 128 * j + 128])
    for line, ref in ((16, b_qv), (17, b_out), (18, b_up), (19, b_down)):
        size = ref.shape[1]
        wide = jnp.concatenate([ref[...].astype(F32)] * (128 // size), 1) if size < 128 else ref[...].astype(F32)
        table(line, jnp.where(lane // size == lax.rem(index, 128 // size), wide, 0.0))
    bm = b_mod[...].astype(F32)
    none = jnp.zeros((1, 64), F32)
    even = lax.rem(index, 2) == 0
    table(20, jnp.where(even, bm[:, :128], jnp.concatenate([none, bm[:, :64]], 1)))
    table(21, jnp.where(even, jnp.concatenate([bm[:, 128:], none], 1), bm[:, 64:]))
    at.barrier()

    def small_send(idx, peer, n):
        links.send(SM.at[idx], SM.at[idx], ssm.at[n], rsm.at[n], peer)

    def small_wait(idx, n):
        links.copy(SM.at[idx], SM.at[idx], ssm.at[n], rsm.at[n], at.xp).wait_recv()

    for k in (1, 2, 3):
        small_send((z, x, y, c), at.z_to(k), k - 1)
    gather_stage(ORDER[0], 0)
    links.send(lat.at[1 - y], xs.at[y], sx.at[0], rx.at[0], at.yp)
    for k in (1, 2, 3):
        small_wait((at.z_from(k), x, y, c), k - 1)
    small_send((ALL, x, y, c), at.xp, 3)
    gather_stage(ORDER[1], 0)
    small_wait((ALL, 1 - x, y, c), 3)
    small_send((ALL, ALL, y, c), at.yp, 4)

    row = lax.broadcasted_iota(jnp.int32, (8, 128), 0)
    for m in range(2):
        for p in range(8):
            tile = SM[p // 2, p % 2, y, c, 8 * m : 8 * m + 8, :]
            cact[8 * m + p : 8 * m + p + 1, :] = jnp.sum(jnp.where(row == at.dp, tile, 0.0), 0, keepdims=True)
    cond = cact[...]
    cond = jnp.where(lane // 32 == at.sq, cond / (1.0 + jnp.exp(-cond)), 0.0)
    cact[...] = cond
    cond_low = ((cond[:, 0:32] + cond[:, 32:64]) + (cond[:, 64:96] + cond[:, 96:128])).astype(BF)
    local_m.wait()
    for i in range(6):
        part = dot_nn(cond_low, wm[:, 1024 * i : 1024 * i + 1024])
        for m in range(2):
            for p in range(8):
                for j in range(8):
                    PM[m, p // 2, p % 2, 8 * i + j : 8 * i + j + 1, :] = part[8 * m + p : 8 * m + p + 1, 128 * j : 128 * j + 128]
    links.send(PM.at[:, :, 1 - x], PX, sx.at[1], rx.at[1], at.xp)
    gather_stage(ORDER[2], 0)
    gather_tick(0)
    links.copy(PM.at[:, :, 1 - x], PX, sx.at[1], rx.at[1], at.xp).wait_recv()
    for m in range(2):
        PM[m, :, x] = PM[m, :, x] + PX[m]
    links.send(PM.at[1 - y, :, x], PY, sx.at[2], rx.at[2], at.yp)
    small_wait((ALL, ALL, 1 - y, c), 4)
    small_send((ALL, ALL, ALL, c), at.cp, 5)
    gather_tick(1)
    links.copy(PM.at[1 - y, :, x], PY, sx.at[2], rx.at[2], at.yp).wait_recv()
    PM[y, :, x] = PM[y, :, x] + PY[...]
    for k in (1, 2, 3):
        to = lax.rem(z + k, ZN)
        links.send(PM.at[y, to, x], PZ.at[k - 1], sx.at[2 + k], rx.at[2 + k], at.z_to(k))
    for k in (1, 2, 3):
        links.copy(PM.at[y, z, x], PZ.at[k - 1], sx.at[2 + k], rx.at[2 + k], at.z_to(k)).wait_recv()
    FM[...] = PM[y, z, x] + PZ[0] + PZ[1] + PZ[2]
    links.send(FM, PC, sx.at[6], rx.at[6], at.cp)
    gather_tick(2)
    small_wait((ALL, ALL, ALL, 1 - c), 5)

    def entry(device, line):
        return SM[device // 8, (device // 4) % 2, (device // 2) % 2, device % 2, line : line + 1, :]

    for t in range(16):
        bias[0:1, 128 * t : 128 * t + 128] = entry(2 * t, 16) + entry(2 * t + 1, 16)
    for t in range(8):
        bias[0:1, 2048 + 128 * t : 2176 + 128 * t] = (entry(4 * t, 17) + entry(4 * t + 1, 17)) + (entry(4 * t + 2, 17) + entry(4 * t + 3, 17))
        bias[0:1, 7168 + 128 * t : 7296 + 128 * t] = (entry(4 * t, 19) + entry(4 * t + 1, 19)) + (entry(4 * t + 2, 19) + entry(4 * t + 3, 19))
    for t in range(32):
        bias[0:1, 3072 + 128 * t : 3200 + 128 * t] = entry(t, 18)
    links.copy(FM, PC, sx.at[6], rx.at[6], at.cp).wait_recv()
    for j in range(48):
        k, third = j // 3, j % 3
        if third == 0:
            b_row = entry(2 * k, 20)
        elif third == 1:
            b_row = entry(2 * k, 21) + entry(2 * k + 1, 20)
        else:
            b_row = entry(2 * k + 1, 21)
        vec[j // 8 : j // 8 + 1, 128 * (j % 8) : 128 * (j % 8) + 128] = FM[j : j + 1, :] + PC[j : j + 1, :] + b_row
    shift_attn, scale_attn, gate_attn = vec[0:1, :], 1.0 + vec[1:2, :], vec[2:3, :]
    shift_mlp, scale_mlp, gate_mlp = vec[3:4, :], 1.0 + vec[4:5, :], vec[5:6, :]
    links.send(cot.at[1 - y], cs.at[y], sx.at[7], rx.at[7], at.yp)

    local_x.wait()
    links.copy(lat.at[1 - y], xs.at[1 - y], sx.at[0], rx.at[0], at.yp).wait_recv()

    def halves(i):
        return i // (256 // RB), pl.ds(pl.multiple_of((i % (256 // RB)) * RB, RB), RB)

    def norm1(i, carry):
        half, rows = halves(i)
        n, _ = norm_rows(xs[half, rows, :].astype(F32))
        gp[0, pl.ds(pl.multiple_of(i * RB, RB), RB), :] = (n * scale_attn + shift_attn).astype(BF)
        return carry

    lax.fori_loop(0, TOK // RB, norm1, 0)
    x_saved = save(xs, t_x)
    m1_saved = save(gp.at[0], t_m1)
    gather_tick(3)
    gather_tick(4)

    def weight(unit, cols):
        return W8[unit, :, :, :, :, :, cols].reshape(1024, -1)

    def project(unit, put):
        for t in range(2):
            cols = slice(512 * t, 512 * t + 512)
            put(cols, dot_nn(gp[0], weight(unit, cols)))

    def rows512(value):
        return value.astype(BF).reshape(2, 2, 2, 2, 32, -1)

    def put_k(cols, value):
        CR[0, :, :, :, :, :, cols] = rows512(value)

    def put_v(cols, value):
        CR[2, :, :, :, :, :, cols] = rows512(value + bias[0:1, 1024 + cols.start : 1024 + cols.stop])

    def put_q(cols, value):
        act[0, :, :, :, :, :, cols] = rows512(value + bias[0:1, cols])

    ready(0)
    w_saved = [save(W8.at[0], t_w.at[0])]
    project(0, put_k)
    k_sent = links.copy(CR.at[0], CR.at[1], sx.at[8], rx.at[8], at.cp)
    k_sent.start()
    gather_tick(5)
    ready(1)
    w_saved.append(save(W8.at[1], t_w.at[1]))
    project(1, put_v)
    v_sent = links.copy(CR.at[2], CR.at[3], sx.at[9], rx.at[9], at.cp)
    v_sent.start()
    gather_tick(6)
    ready(2)
    project(2, put_q)
    q_saved = save(act.at[0], t_q)
    k_sent.wait_recv()
    v_sent.wait_recv()
    kv_saved = [save(CR.at[pl.ds(0, 2)], t_k), save(CR.at[pl.ds(2, 2)], t_v)]

    def attend_pair(p, carry):
        cols = pl.ds(pl.multiple_of(p * 128, 128), 128)
        k2, v2 = CR[0:2, :, :, :, :, :, cols].reshape(1024, 128), CR[2:4, :, :, :, :, :, cols].reshape(1024, 128)
        for t in range(2):
            rows = slice(256 * t, 256 * t + 256)
            q2 = act[0, t, :, :, :, :, cols].reshape(256, 128)
            parts = []
            for e in range(2):
                own = (lane < 64) == (e == 0)
                qe = jnp.where(own, q2, jnp.zeros_like(q2)) * BF(0.125)
                scores = dot_nt(qe, k2)
                top = jnp.max(scores, 1, keepdims=True)
                expon = jnp.exp(scores - top)
                total = jnp.sum(expon, 1, keepdims=True)
                parts.append(dot_nn((expon * (1.0 / total)).astype(BF), v2))
                log_total = jnp.broadcast_to(top + jnp.log(total), (256, 128)).T
                lse[p, e : e + 1, rows] = log_total[0:1, :]
            act[1, t, :, :, :, :, cols] = jnp.where(lane < 64, parts[0], parts[1]).astype(BF).reshape(2, 2, 2, 32, 128)
        return carry

    lax.fori_loop(0, 2, attend_pair, 0)
    gather_tick(7)
    lax.fori_loop(2, 5, attend_pair, 0)
    gather_tick(8)
    lax.fori_loop(5, 8, attend_pair, 0)
    gather_tick(9)
    att_saved = save(act.at[1], t_att)
    for copy in kv_saved + [q_saved]:
        copy.wait()
    k_sent.wait_send()
    v_sent.wait_send()
    pl.semaphore_signal(ready_c, inc=1, device_id=at.cp, device_id_type=MESH_IDS)
    ready(3)
    local_c.wait()
    links.copy(cot.at[1 - y], cs.at[1 - y], sx.at[7], rx.at[7], at.yp).wait_recv()

    for t in range(2):
        cols = slice(512 * t, 512 * t + 512)
        value = dot_nn(act[1].reshape(512, 1024), weight(3, cols)) + bias[0:1, 2048 + 512 * t : 2560 + 512 * t]
        gp[1, :, cols] = value.astype(BF)
        res[:, cols] = xs[:, :, cols].reshape(TOK, 512).astype(F32) + gate_attn[:, cols] * value
    ao_saved = save(gp.at[1], t_ao)
    for i in range(13):
        sums[i] = jnp.zeros((8, 1024), F32)

    def norm2(i, carry):
        rows = pl.ds(pl.multiple_of(i * RB, RB), RB)
        half, part = halves(i)
        n, _ = norm_rows(res[rows, :])
        m2[rows, :] = (n * scale_mlp + shift_mlp).astype(BF)
        low = (cs[half, part, :].astype(F32) * gate_mlp).astype(BF)
        gb[rows, :] = low
        sums[8] = sums[8] + fold(low.astype(F32))
        return carry

    lax.fori_loop(0, TOK // RB, norm2, 0)
    for copy in [x_saved, m1_saved, att_saved, ao_saved] + w_saved:
        copy.wait()
    gather_tick(10)
    for unit in (8, 9, 10, 11):
        ready(unit)
    gather_done(0)
    gather_done(1)

    def down_rows(j, u):
        return WD[j, u].reshape(1024, 256)

    def down_copies(u):
        return [
            links.copy(W8.at[1, pl.ds(2 * xi, 2), 1 - c], CR.at[u, xi], dcs.at[u, xi], dcr.at[u, xi], at.cp)
            for xi in range(2)
        ]

    def mlp(u):
        for t in range(2):
            cols = slice(512 * t, 512 * t + 512)
            first = 3072 + 1024 * u + 512 * t
            v = dot_nn(m2[...], weight(4 + u, cols)) + bias[0:1, first : first + 512]
            rows = jnp.concatenate([WD[j, u, t].reshape(512, 256) for j in range(4)], 1)
            slope = dot_nt(gb[...], rows)
            square = v * v
            th = jnp.tanh(ROOT_2_PI * v * (1.0 + 0.044715 * square))
            up = 0.5 + 0.5 * th
            act[0, :, :, :, :, :, cols] = rows512(v * up)
            low = (slope * (up + 0.5 * v * (1.0 - th * th) * (ROOT_2_PI + (ROOT_2_PI * 3 * 0.044715) * square))).astype(BF)
            gp[0, :, cols] = low
            sums[9 + u, :, cols] = fold(low.astype(F32))
        put_grad(u, 0, m2[...], lambda cols: gp[0, :, cols])
        slot_free(1)
        acts = act[0].reshape(512, 1024)
        for t in range(2):
            cols = slice(512 * t, 512 * t + 512)
            W8[1, :, :, :, :, :, cols] = dot_tn(acts, gb[:, cols]).astype(BF).reshape(4, 2, 2, 2, 32, 512)
        if u == 0:
            pl.semaphore_wait(ready_c, 1)
        cores_sent[1] = down_copies(u)
        for copy in cores_sent[1]:
            copy.start()
        for t in range(2):
            cols = slice(512 * t, 512 * t + 512)
            back = dot_nt(gp[0], W8[4 + u, 2 * t : 2 * t + 2].reshape(512, 1024))
            ahead = dot_nn(acts, jnp.concatenate([down_rows(2 * t, u), down_rows(2 * t + 1, u)], 1))
            acc[:, cols] = back if u == 0 else acc[:, cols] + back
            br[:, cols] = ahead if u == 0 else br[:, cols] + ahead

    def down_sum(u):
        for copy in down_copies(u):
            copy.wait_recv()

        def add(i, carry):
            xi, yi, a, b = i // 8, (i // 4) % 2, (i // 2) % 2, i % 2
            CR[u, xi, yi, a, b] = CR[u, xi, yi, a, b] + W8[1, 2 * xi + yi, c, a, b]
            return carry

        lax.fori_loop(0, 16, add, 0)

    gather_tick(11)
    for u in range(4):
        ready(4 + u)
        mlp(u)
        if u < 3:
            gather_tick(12 + u)
        tick()
        down_sum(u)
    waiting[4] = 1

    def output(i, carry):
        rows = pl.ds(pl.multiple_of(i * RB, RB), RB)
        half, part = halves(i)
        branch = br[rows, :] + bias[0:1, 7168:8192]
        sums[6] = sums[6] + fold(cs[half, part, :].astype(F32) * branch)
        xs[half, part, :] = (res[rows, :] + gate_mlp * branch).astype(BF)
        return carry

    lax.fori_loop(0, TOK // RB, output, 0)
    vec[6:7, :] = jnp.sum(sums[6], 0, keepdims=True)
    out_saved = save(xs.at[y], o_out.at[y])
    links.send(xs.at[1 - y], o_out.at[y], sx.at[10], rx.at[10], at.yp)
    for unit in (2, 3, 4, 5, 6, 7, 8, 9, 10, 11):
        gather_done(unit)
    load("ao", t_ao, gp.at[1])
    for j in range(4):
        cols = pl.ds(256 * j, 256)
        load(f"k{j}", t_k.at[:, :, :, :, :, :, cols], WD.at[j, 0])
        load(f"v{j}", t_v.at[:, :, :, :, :, :, cols], WD.at[j, 1])
        load(f"q{j}", t_q.at[:, :, :, :, :, cols], WD.at[j, 2, 0])
        load(f"att{j}", t_att.at[:, :, :, :, :, cols], WD.at[j, 2, 1])
    load("m1", t_m1, gp.at[0])
    load("wk", t_w.at[0], W8.at[4])
    load("wv", t_w.at[1], W8.at[5])
    tick()
    waiting[5] = 1

    loaded("ao")

    def norm2_back(i, carry):
        rows = pl.ds(pl.multiple_of(i * RB, RB), RB)
        half, part = halves(i)
        n, inv = norm_rows(res[rows, :])
        up = acc[rows, :]
        gn = up * n
        sums[3] = sums[3] + fold(up)
        sums[4] = sums[4] + fold(gn)
        g = up * scale_mlp
        total = cs[half, part, :].astype(F32) + (g - jnp.mean(g, -1, keepdims=True) - n * jnp.mean(gn * scale_mlp, -1, keepdims=True)) * inv
        acc[rows, :] = total
        sums[2] = sums[2] + fold(total * gp[1, rows, :].astype(F32))
        low = (total * gate_attn).astype(BF)
        gb[rows, :] = low
        sums[5] = sums[5] + fold(low.astype(F32))
        return carry

    lax.fori_loop(0, TOK // RB, norm2_back, 0)
    for half in range(2):
        load(f"x{half}", t_x.at[half], gp.at[1, pl.ds(256 * half, 256)])
    tick()
    waiting[6] = 1
    for t in range(2):
        value = dot_nt(gb[...], W8[3, 2 * t : 2 * t + 2].reshape(512, 1024)).astype(BF)
        for h in range(2):
            WD[2 * t + h, 3, 0] = value[:, 256 * h : 256 * h + 256].reshape(2, 2, 2, 2, 32, 256)
    for j in range(4):
        for name in ("k", "v", "q", "att"):
            loaded(f"{name}{j}")

    def wide(a, b):
        return jnp.concatenate([WD[j, a, b].reshape(512, 256) for j in range(4)], 1)

    put_grad(8, 0, wide(2, 1), lambda cols: gb[:, cols])
    tick()
    waiting[7] = 1

    def attend_back(p, carry):
        j, cols = p // 2, pl.ds(pl.multiple_of((p % 2) * 128, 128), 128)
        full = pl.ds(pl.multiple_of(p * 128, 128), 128)
        k2, v2 = WD[j, 0, :, :, :, :, :, :, cols].reshape(1024, 128), WD[j, 1, :, :, :, :, :, :, cols].reshape(1024, 128)
        keys_sum, values_sum = None, None
        for t in range(2):
            rows = slice(256 * t, 256 * t + 256)
            q2, do2 = WD[j, 2, 0, t, :, :, :, :, cols].reshape(256, 128), WD[j, 3, 0, t, :, :, :, :, cols].reshape(256, 128)
            prod = (do2.astype(F32) * WD[j, 2, 1, t, :, :, :, :, cols].reshape(256, 128).astype(F32)).T
            queries = []
            for e in range(2):
                own = (lane < 64) == (e == 0)
                qe = jnp.where(own, q2, jnp.zeros_like(q2)) * BF(0.125)
                de = jnp.where(own, do2, jnp.zeros_like(do2))
                row_dot = jnp.sum(prod[64 * e : 64 * e + 64, :], 0, keepdims=True)
                probs = jnp.exp(dot_nt(k2, qe) - lse[p, e : e + 1, rows])
                grad_scores = (probs * (dot_nt(v2, de) - row_dot)).astype(BF)
                queries.append(dot_tn(grad_scores, k2))
                a, b = dot_nn(grad_scores, qe), dot_nn(probs.astype(BF), de)
                keys_sum = a if keys_sum is None else keys_sum + a
                values_sum = b if values_sum is None else values_sum + b
            grad_query = (jnp.where(lane < 64, queries[0], queries[1]) * 0.125).astype(BF)
            WD[j, 3, 1, t, :, :, :, :, cols] = grad_query.reshape(2, 2, 2, 32, 128)
        W8[6, :, :, :, :, :, full] = keys_sum.astype(BF).reshape(4, 2, 2, 2, 32, 128)
        W8[7, :, :, :, :, :, full] = values_sum.astype(BF).reshape(4, 2, 2, 2, 32, 128)
        return carry

    lax.fori_loop(0, 2, attend_back, 0)
    tick()
    waiting[8] = 1
    lax.fori_loop(2, 4, attend_back, 0)
    tick()
    lax.fori_loop(4, 6, attend_back, 0)
    tick()
    lax.fori_loop(6, 8, attend_back, 0)
    links.send(W8.at[6, pl.ds(2, 2)], act.at[0], sx.at[11], rx.at[11], at.cp)
    links.send(W8.at[7, pl.ds(2, 2)], act.at[1], sx.at[12], rx.at[12], at.cp)
    loaded("m1")
    loaded("wk")
    loaded("wv")
    grad_q = wide(3, 1)
    put_grad(9, 1, gp[0], lambda cols: grad_q[:, cols])
    sums[6] = fold(grad_q.astype(F32))
    tick()
    for own, came in ((6, 0), (7, 1)):
        links.copy(W8.at[own, pl.ds(2, 2)], act.at[came], sx.at[11 + came], rx.at[11 + came], at.cp).wait_recv()

        def join(i, carry):
            a, b = i // 2, i % 2
            W8[own, a, b] = W8[own, a, b] + act[came, a, b]
            return carry

        lax.fori_loop(0, 4, join, 0)

    grad_k, grad_v = W8[6, 0:2].reshape(512, 1024), W8[7, 0:2].reshape(512, 1024)
    sums[7] = fold(grad_v.astype(F32))
    for t in range(2):
        rows = slice(2 * t, 2 * t + 2)
        br[:, 512 * t : 512 * t + 512] = (
            dot_nt(grad_q, W8[2, rows].reshape(512, 1024)) + dot_nt(grad_k, W8[4, rows].reshape(512, 1024)) + dot_nt(grad_v, W8[5, rows].reshape(512, 1024))
        )
    loaded("x0")
    loaded("x1")

    def norm1_back(i):
        rows = pl.ds(pl.multiple_of(i * RB, RB), RB)
        n, inv = norm_rows(gp[1, rows, :].astype(F32))
        up = br[rows, :]
        gn = up * n
        sums[0] = sums[0] + fold(up)
        sums[1] = sums[1] + fold(gn)
        g = up * scale_attn
        return rows, acc[rows, :] + (g - jnp.mean(g, -1, keepdims=True) - n * jnp.mean(gn * scale_attn, -1, keepdims=True)) * inv

    per = 256 // RB

    def away(i, carry):
        _, value = norm1_back(i + (1 - y) * per)
        cs[0, pl.ds(pl.multiple_of(i * RB, RB), RB), :] = value.astype(BF)
        return carry

    def here(i, carry):
        rows, value = norm1_back(i + y * per)
        br[rows, :] = value
        return carry

    lax.fori_loop(0, per, away, 0)
    links.send(cs.at[0], cs.at[1], sx.at[13], rx.at[13], at.yp)
    lax.fori_loop(0, per, here, 0)
    save(br.at[pl.ds(pl.multiple_of(y * 256, 256), 256)], o_gl.at[y])

    def put_kv(n, own, d):
        put_grad(n, d, gp[0], lambda cols: W8[own, 0:2, :, :, :, :, cols].reshape(512, 512))

    for i in range(6):
        value = vec[6:7, :] if i == 5 else jnp.sum(sums[i], 0, keepdims=True)
        for j in range(8):
            GS[8 * i + j : 8 * i + j + 1, :] = value[:, 128 * j : 128 * j + 128]
    links.send(GS, GP, sy.at[4], ry.at[4], at.cp)
    for line, i in enumerate((6, 7, 5, 9, 10, 11, 12, 8)):
        value = jnp.sum(sums[i], 0, keepdims=True)
        for j in range(8):
            BA[8 * line + j : 8 * line + j + 1, :] = value[:, 128 * j : 128 * j + 128]
    links.send(BA, BB.at[0], sy.at[5], ry.at[5], at.cp)
    put_kv(10, 6, 0)
    links.copy(GS, GP, sy.at[4], ry.at[4], at.cp).wait_recv()
    GM[y, z, x] = (GS[...] + GP[...]).astype(BF)
    mine = GM.at[y, z, x]
    for k in (1, 2, 3):
        links.send(mine, mine, sy.at[5 + k], ry.at[5 + k], at.z_to(k))
    tick()
    put_kv(11, 7, 1)
    links.copy(BA, BB.at[0], sy.at[5], ry.at[5], at.cp).wait_recv()
    BB[5] = BA[...] + BB[0]
    links.send(BB.at[5], BB.at[1], sy.at[9], ry.at[9], at.yp)
    for k in (1, 2, 3):
        ref = GM.at[y, at.z_from(k), x]
        links.copy(ref, ref, sy.at[5 + k], ry.at[5 + k], at.z_to(k)).wait_recv()
    ref = GM.at[y, :, x]
    links.send(ref, ref, sy.at[10], ry.at[10], at.xp)
    tick()
    links.copy(BB.at[5], BB.at[1], sy.at[9], ry.at[9], at.yp).wait_recv()
    BB[6] = BB[5] + BB[1]
    links.send(BB.at[6], BB.at[2], sy.at[11], ry.at[11], at.xp)
    ref = GM.at[y, :, 1 - x]
    links.copy(ref, ref, sy.at[10], ry.at[10], at.xp).wait_recv()
    links.send(GM.at[y], GM.at[y], sy.at[12], ry.at[12], at.yp)
    links.copy(BB.at[6], BB.at[2], sy.at[11], ry.at[11], at.xp).wait_recv()
    BB[7] = BB[6] + BB[2]
    bias_in = (BB.at[3], BB.at[4], BB.at[8])
    for k in (1, 2, 3):
        links.send(BB.at[7], bias_in[k - 1], sy.at[12 + k], ry.at[12 + k], at.z_to(k))
    tick()
    links.copy(GM.at[1 - y], GM.at[1 - y], sy.at[12], ry.at[12], at.yp).wait_recv()

    for m in range(2):
        for p in range(8):
            tile = GM[m, p // 2, p % 2].astype(F32)
            for j in range(48):
                first = 256 + 16 * (j // 8) + 8 * m + p
                acc[first : first + 1, 128 * (j % 8) : 128 * (j % 8) + 128] = tile[j : j + 1, :]
    cond = cact[...].astype(BF)
    part_sum = None
    for i in range(6):
        cols = slice(1024 * i, 1024 * i + 1024)
        values = acc[256 + 16 * i : 272 + 16 * i, :]
        low = values.astype(BF)
        brow[0:1, cols] = jnp.sum(values, 0, keepdims=True)
        spread = dot_tn(cond, low)
        acc[32 * i : 32 * i + 32, :] = (spread[0:32] + spread[32:64]) + (spread[64:96] + spread[96:128])
        save(acc.at[pl.ds(32 * i, 32)], o_mod.at[:, pl.ds(1024 * i, 1024)])
        term = dot_nt(low, wm[:, cols])
        part_sum = term if part_sum is None else part_sum + term
    save(brow, o_bmod)
    GCX[0] = jnp.where(lane // 32 == at.sq, jnp.concatenate([part_sum] * 4, 1), 0.0)
    links.send(GCX.at[0], GCX.at[1], sy.at[16], ry.at[16], at.cp)
    for k in (1, 2, 3):
        links.copy(BB.at[7], bias_in[k - 1], sy.at[12 + k], ry.at[12 + k], at.z_to(k)).wait_recv()
    bsum[...] = (BB[7] + BB[3]) + (BB[4] + BB[8])
    save(bsum, o_bias)
    links.copy(GCX.at[0], GCX.at[1], sy.at[16], ry.at[16], at.cp).wait_recv()
    GCX[2] = GCX[0] + GCX[1]
    links.send(GCX.at[2], GCX.at[3], sy.at[17], ry.at[17], at.yp)
    if waiting:
        tick()
    links.copy(GCX.at[2], GCX.at[3], sy.at[17], ry.at[17], at.yp).wait_recv()
    GC[z, x] = GCX[2] + GCX[3]
    mine = GC.at[z, x]
    for k in (1, 2, 3):
        links.send(mine, mine, sy.at[17 + k], ry.at[17 + k], at.z_to(k))
    for k in (1, 2, 3):
        ref = GC.at[at.z_from(k), x]
        links.copy(ref, ref, sy.at[17 + k], ry.at[17 + k], at.z_to(k)).wait_recv()
    links.send(GC.at[:, x], GC.at[:, x], sy.at[21], ry.at[21], at.xp)
    links.copy(cs.at[0], cs.at[1], sx.at[13], rx.at[13], at.yp).wait_recv()

    def widen(i, carry):
        rows = pl.ds(pl.multiple_of(i * RB, RB), RB)
        br[pl.ds(pl.multiple_of((1 - y) * 256 + i * RB, RB), RB), :] = cs[1, rows, :].astype(F32)
        return carry

    lax.fori_loop(0, per, widen, 0)
    save(br.at[pl.ds(pl.multiple_of((1 - y) * 256, 256), 256)], o_gl.at[1 - y])
    while waiting:
        tick()
    links.copy(GC.at[:, 1 - x], GC.at[:, 1 - x], sy.at[21], ry.at[21], at.xp).wait_recv()
    save(GC, o_gc)
    links.copy(xs.at[1 - y], o_out.at[1 - y], sx.at[10], rx.at[10], at.yp).wait_recv()
    slot_free(0)
    slot_free(1)
    for copy in fin_saved.values():
        copy.wait()
    links.drain()
    early = [id(copy) for copy in kv_saved + [q_saved, x_saved, m1_saved, att_saved, ao_saved] + w_saved]
    for copy in outgoing:
        if id(copy) not in early:
            copy.wait()


def run_block(lat, cot, cond, b_mod, b_qv, b_out, b_up, b_down, w_mod, w_qkv, w_out, w_up, w_down):
    S = jax.ShapeDtypeStruct
    V = pltpu.VMEM
    dma = pltpu.SemaphoreType.DMA
    regular = pltpu.SemaphoreType.REGULAR
    half = (2, 2, 2, 2, 32, 1024)
    outs = [
        S((2, 256, 1024), BF), S((2, 256, 1024), F32), S((32, 3072), F32), S((32, 1024), F32), S((32, 4096), F32), S((128, 1024), F32),
        S((32, 6144), F32), S((1, 6144), F32), S((64, 128), F32), S((4, 2, 16, 128), F32),
        S((2, 4, 2, 2, 2, 32, 1024), BF), S((2, 256, 1024), BF), S((512, 1024), BF), S(half, BF), S((2,) + half, BF), S((2,) + half, BF), S(half, BF),
        S((512, 1024), BF),
    ]
    scratch = [
        V((8, 4, 2, 2, 2, 32, 1024), BF), V((4, 4, 2, 2, 2, 2, 2, 32, 256), BF), V((4, 2, 2, 2, 2, 32, 1024), BF), V((4, 4, 2, 2, 32, 1024), BF),
        *[V(shape, BF) for step in LANDING for shape in step],
        V((2,) + half, BF), V((2, 512, 1024), BF), V((512, 1024), BF), V((512, 1024), BF), V((512, 1024), F32), V((512, 1024), F32), V((512, 1024), F32),
        V((2, 256, 1024), BF), V((2, 256, 1024), BF), V((3, 32, 1024), F32), V((8, 8, 512), F32),
        V((4, 2, 2, 2, 24, 128), F32), V((2, 4, 2, 48, 128), F32), V((4, 48, 128), F32), V((2, 4, 48, 128), F32), V((3, 48, 128), F32),
        V((48, 128), F32), V((48, 128), F32), V((32, 6144), BF), V((16, 128), F32), V((8, 1024), F32), V((1, 8192), F32), V((13, 8, 1024), F32),
        V((48, 128), F32), V((48, 128), F32), V((2, 4, 2, 48, 128), BF), V((64, 128), F32), V((64, 128), F32), V((9, 64, 128), F32),
        V((4, 2, 16, 128), F32), V((4, 16, 128), F32), V((1, 6144), F32),
        dma((7, 21)), dma((12, 21)), dma((12,)), dma((12,)), dma((LR, 21)), dma((LR, 21)), dma((12,)), dma((12,)), dma((4, 2)), dma((4, 2)),
        regular((7,)), regular((4,)), regular, dma((14,)), dma((14,)), dma((22,)), dma((22,)), dma((6,)), dma((6,)),
        dma((15,)), dma((22,)), dma((22,)), dma((3,)),
    ]
    return pl.pallas_call(
        block_kernel,
        out_shape=outs,
        in_specs=[ANY, ANY, VM, VM, VM, VM, VM, VM, ANY, ANY, ANY, ANY, ANY],
        out_specs=[ANY] * len(outs),
        scratch_shapes=scratch,
        compiler_params=pltpu.CompilerParams(collective_id=0, has_side_effects=True, vmem_limit_bytes=63 * 2**20),
        cost_estimate=pl.CostEstimate(flops=6 * 10**10, bytes_accessed=10**8, transcendentals=2 * 10**7),
    )(lat, cot, cond, b_mod, b_qv, b_out, b_up, b_down, w_mod, w_qkv, w_out, w_up, w_down.reshape(2, 2, 32, 1024))[:10]


def finish_kernel(h_out, h_gl, h_qkv, h_wo, h_up, h_dn, h_mod, bmod, bias, gcond, cond, o_out, o_gl, o_cond, o_mod, o_bmod, o_qkv, o_bqv, o_wo, o_bo, o_up, o_bu, o_dn, o_bd, v_out, v_gl, v_qkv, v_wo, v_up, v_dn, v_mod, sem_in, sem_out):
    ways = (
        (h_gl, v_gl, o_gl), (h_out, v_out, o_out), (h_mod, v_mod, o_mod), (h_up, v_up, o_up), (h_dn, v_dn, o_dn), (h_qkv, v_qkv, o_qkv), (h_wo, v_wo, o_wo),
    )
    into = [pltpu.make_async_copy(src, mid, sem_in.at[i]) for i, (src, mid, _) in enumerate(ways)]
    copies = [pltpu.make_async_copy(mid, dst, sem_out.at[i]) for i, (_, mid, dst) in enumerate(ways)]
    for copy in into:
        copy.start()
    for first, then in zip(into, copies):
        first.wait()
        then.start()
    dp, sq = lax.axis_index("dp"), lax.axis_index("seq")
    index = dp * (YN * CN) + sq

    def pick(values, row):
        return jnp.sum(jnp.where(lax.broadcasted_iota(jnp.int32, values.shape, 0) == row, values, 0.0), 0, keepdims=True)

    def lanes(row, size, at_):
        total = jnp.where(at_ == 0, row[:, 0:size], 0.0)
        for k in range(1, 128 // size):
            total = jnp.where(at_ == k, row[:, size * k : size * k + size], total)
        return total

    o_bqv[...] = lanes(pick(bias[0:16, :], index // 2), 64, lax.rem(index, 2))
    o_bo[...] = lanes(pick(bias[16:24, :], index // 4), 32, lax.rem(index, 4))
    o_bu[...] = pick(bias[24:56, :], index)
    o_bd[...] = lanes(pick(bias[56:64, :], index // 4), 32, lax.rem(index, 4))
    wide = bmod[0:1, pl.ds(pl.multiple_of((index // 2) * 384 + lax.rem(index, 2) * 128, 128), 256)]
    o_bmod[...] = jnp.where(lax.rem(index, 2) == 0, wide[:, 0:192], wide[:, 64:256])
    for m in range(2):
        for p in range(8):
            v = cond[m : m + 1, 128 * p : 128 * p + 128].astype(F32)
            gate = 1.0 / (1.0 + jnp.exp(-v))
            o_cond[m : m + 1, 128 * p : 128 * p + 128] = pick(gcond[p, 8 * m : 8 * m + 8, :], dp) * (gate * (1.0 + v * (1.0 - gate)))
    for copy in copies:
        copy.wait()


def per_device_kernels(latents, conditioning, w_mod, b_mod, w_qkv, b_qv, w_out, b_out, w_up, b_up, w_down, b_down, cotangent):
    cond = conditioning[:, 0]
    output, grad_lat, g_qkv, g_out, g_up, g_down, g_mod, gb_mod, gb_all, g_cond = run_block(
        latents[:, 0], cotangent[:, 0], cond, b_mod, b_qv, b_out, b_up, b_down, w_mod[0], w_qkv[0], w_out[0], w_up[0], w_down[0]
    )
    S = jax.ShapeDtypeStruct
    shapes = [
        S((2, 256, 1024), BF), S((2, 256, 1024), F32), S((2, 1024), F32), S((32, 6144), F32), S((1, 192), F32), S((32, 3072), F32), S((1, 64), F32),
        S((32, 1024), F32), S((1, 32), F32), S((32, 4096), F32), S((1, 128), F32), S((128, 1024), F32), S((1, 32), F32),
    ]
    (out, gl, gc, mod, bmod, qkv, bqv, wo, bo, up, bu, dn, bd) = pl.pallas_call(
        finish_kernel,
        out_shape=shapes,
        in_specs=[ANY] * 7 + [VM] * 4,
        out_specs=[ANY, ANY, VM, ANY, VM, ANY, VM, ANY, VM, ANY, VM, ANY, VM],
        scratch_shapes=[pltpu.VMEM(s.shape, s.dtype) for s in (output, grad_lat, g_qkv, g_out, g_up, g_down, g_mod)]
        + [pltpu.SemaphoreType.DMA((7,)), pltpu.SemaphoreType.DMA((7,))],
        cost_estimate=pl.CostEstimate(flops=10**6, bytes_accessed=10**7, transcendentals=2048),
    )(output, grad_lat, g_qkv, g_out, g_up, g_down, g_mod, gb_mod, gb_all, g_cond.reshape(8, 16, 128), cond)
    return (out[:, None], gl[:, None], gc[:, None], mod[None], bmod, qkv[None], bqv, wo[None], bo, up[None], bu, dn[None], bd)


def solution(mesh):
    placed = (
        P(None, "dp", "seq", None),
        P(None, "dp", None),
        P(None, ("dp", "seq"), None),
        P(None, ("dp", "seq")),
        P(None, ("dp", "seq"), None),
        P(None, ("dp", "seq")),
        P(None, ("dp", "seq"), None),
        P(None, ("dp", "seq")),
        P(None, ("dp", "seq"), None),
        P(None, ("dp", "seq")),
        P(None, ("dp", "seq"), None),
        P(None, ("dp", "seq")),
        P(None, "dp", "seq", None),
    )
    return jax.shard_map(
        per_device_kernels if dict(mesh.shape) == {"dp": 8, "seq": 4} else per_device,
        mesh=mesh,
        in_specs=placed,
        out_specs=(
            P(None, "dp", "seq", None),
            P(None, "dp", "seq", None),
            P(None, "dp", None),
            P(None, ("dp", "seq"), None),
            P(None, ("dp", "seq")),
            P(None, ("dp", "seq"), None),
            P(None, ("dp", "seq")),
            P(None, ("dp", "seq"), None),
            P(None, ("dp", "seq")),
            P(None, ("dp", "seq"), None),
            P(None, ("dp", "seq")),
            P(None, ("dp", "seq"), None),
            P(None, ("dp", "seq")),
        ),
        check_vma=False,
    )
```

```python
import jax
import jax.numpy as jnp
from jax import lax
from jax.sharding import PartitionSpec as P
from jax.experimental import pallas as pl
from jax.experimental.pallas import tpu as pltpu

EPS = 1e-06
HEADS = 16


def modulate(stream, shift_vec, scale_vec):
    row_mean = jnp.mean(stream, -1, keepdims=True)
    centred = stream - row_mean
    row_var = jnp.mean(centred * centred, -1, keepdims=True)
    return centred * lax.rsqrt(row_var + EPS) * (1.0 + scale_vec) + shift_vec


def gelu_tanh(values):
    return jax.nn.gelu(values, approximate=True)


def matmul(left, right):
    return jnp.dot(left, right, preferred_element_type=jnp.float32)


def weight_grad(inputs, upstream):
    return jnp.einsum("ti,to->io", inputs, upstream, preferred_element_type=jnp.float32)


def input_grad(upstream, weight):
    return jnp.einsum("to,io->ti", upstream, weight, preferred_element_type=jnp.float32)


def column_sums(values):
    return jnp.sum(values.astype(jnp.float32), 0)


def gather_once(params, layer_index):
    return (
        lax.all_gather(params[0][layer_index], ("dp", "seq"), axis=0, tiled=True),
        lax.all_gather(params[1][layer_index], ("dp", "seq"), axis=0, tiled=True),
        lax.all_gather(params[2][layer_index], ("dp", "seq"), axis=0, tiled=True),
        lax.all_gather(params[3][layer_index], ("dp", "seq"), axis=0, tiled=True),
        lax.all_gather(params[4][layer_index], ("dp", "seq"), axis=0, tiled=True),
        lax.all_gather(params[5][layer_index], ("dp", "seq"), axis=0, tiled=True),
        lax.all_gather(params[6][layer_index], ("dp", "seq"), axis=0, tiled=True),
        lax.all_gather(params[7][layer_index], ("dp", "seq"), axis=0, tiled=True),
        lax.all_gather(params[8][layer_index], ("dp", "seq"), axis=0, tiled=True),
        lax.all_gather(params[9][layer_index], ("dp", "seq"), axis=0, tiled=True),
    )


def owner_layout(grad, dp_count, seq_count):
    per_owner = grad.shape[1] // (dp_count * seq_count)
    shaped = grad.reshape((grad.shape[0], dp_count, seq_count, per_owner) + grad.shape[2:])
    return jnp.moveaxis(shaped, 0, 2)


def attend(query, keys, values):
    head_size = query.shape[1] // HEADS
    query_rows = query.reshape(query.shape[0], HEADS, head_size)
    key_rows = keys.reshape(keys.shape[0], HEADS, head_size)
    value_rows = values.reshape(values.shape[0], HEADS, head_size)
    scores = jnp.einsum(
        "qhd,khd->hqk", query_rows, key_rows, preferred_element_type=jnp.float32
    ) * head_size ** (-0.5)
    row_max = jnp.max(scores, -1, keepdims=True)
    expon = jnp.exp(scores - row_max)
    row_sum = jnp.sum(expon, -1, keepdims=True)
    probs_low = (expon / row_sum).astype(jnp.bfloat16)
    attended = jnp.einsum("hqk,khd->qhd", probs_low, value_rows, preferred_element_type=jnp.float32)
    return (attended.reshape(query.shape[0], -1).astype(jnp.bfloat16), row_max + jnp.log(row_sum))


def attend_back(query, keys, values, log_total, grad_attended):
    head_size = query.shape[1] // HEADS
    inv_root = head_size ** (-0.5)
    query_rows = query.reshape(query.shape[0], HEADS, head_size)
    key_rows = keys.reshape(keys.shape[0], HEADS, head_size)
    value_rows = values.reshape(values.shape[0], HEADS, head_size)
    grad_rows = grad_attended.reshape(query.shape[0], HEADS, head_size)
    scores = (
        jnp.einsum("qhd,khd->hqk", query_rows, key_rows, preferred_element_type=jnp.float32)
        * inv_root
    )
    probs = jnp.exp(scores - log_total)
    grad_probs = jnp.einsum(
        "qhd,khd->hqk", grad_rows, value_rows, preferred_element_type=jnp.float32
    )
    row_dot = jnp.sum(probs * grad_probs, -1, keepdims=True)
    grad_scores = (probs * (grad_probs - row_dot)).astype(jnp.bfloat16)
    grad_query = (
        jnp.einsum("hqk,khd->qhd", grad_scores, key_rows, preferred_element_type=jnp.float32)
        * inv_root
    )
    grad_keys = (
        jnp.einsum("hqk,qhd->khd", grad_scores, query_rows, preferred_element_type=jnp.float32)
        * inv_root
    )
    grad_values = jnp.einsum(
        "hqk,qhd->khd", probs.astype(jnp.bfloat16), grad_rows, preferred_element_type=jnp.float32
    )
    return (
        grad_query.reshape(query.shape[0], -1),
        grad_keys.reshape(keys.shape[0], -1),
        grad_values.reshape(values.shape[0], -1),
    )


def forward_layer(stream, cond_act, gathered):
    w_mod, b_mod, w_qkv, b_qv, w_out, b_out, w_up, b_up, w_down, b_down = gathered
    model_width = stream.shape[1]
    modulation = matmul(cond_act, w_mod)[0] + b_mod.astype(jnp.float32)
    shift_attn, scale_attn, gate_attn, shift_mlp, scale_mlp, gate_mlp = jnp.split(modulation, 6)
    mixed1 = modulate(stream, shift_attn, scale_attn).astype(jnp.bfloat16)
    qkv = matmul(mixed1, w_qkv)
    qv_bias = b_qv.astype(jnp.float32)
    query = (qkv[:, :model_width] + qv_bias[:model_width]).astype(jnp.bfloat16)
    keys = qkv[:, model_width : 2 * model_width].astype(jnp.bfloat16)
    values = (qkv[:, 2 * model_width :] + qv_bias[model_width:]).astype(jnp.bfloat16)
    all_keys, all_values = (
        lax.all_gather(keys, "seq", axis=0, tiled=True),
        lax.all_gather(values, "seq", axis=0, tiled=True),
    )
    attended, log_total = attend(query, all_keys, all_values)
    attn_out = matmul(attended, w_out) + b_out.astype(jnp.float32)
    resid = stream + gate_attn * attn_out
    mixed2 = modulate(resid, shift_mlp, scale_mlp).astype(jnp.bfloat16)
    preact = matmul(mixed2, w_up) + b_up.astype(jnp.float32)
    activation = gelu_tanh(preact).astype(jnp.bfloat16)
    branch = matmul(activation, w_down) + b_down.astype(jnp.float32)
    saved_acts = (
        stream,
        modulation,
        query,
        all_keys,
        all_values,
        log_total,
        attended,
        attn_out,
        resid,
        preact,
        branch,
    )
    return (resid + gate_mlp * branch, saved_acts)


def backward_layer(gradient, saved_acts, gathered, cond_act):
    w_mod, b_mod, w_qkv, b_qv, w_out, b_out, w_up, b_up, w_down, b_down = gathered
    (
        stream,
        modulation,
        query,
        all_keys,
        all_values,
        log_total,
        attended,
        attn_out,
        resid,
        preact,
        branch,
    ) = saved_acts
    model_width = stream.shape[1]
    shift_attn, scale_attn, gate_attn, shift_mlp, scale_mlp, gate_mlp = jnp.split(modulation, 6)
    grad_branch = (gradient * gate_mlp).astype(jnp.bfloat16)
    grad_gate_mlp = jnp.sum(gradient * branch, 0)
    activation_f, gelu_pull = jax.vjp(gelu_tanh, preact)
    activation = activation_f.astype(jnp.bfloat16)
    grad_b_down = column_sums(grad_branch)
    grad_preact = gelu_pull(input_grad(grad_branch, w_down))[0].astype(jnp.bfloat16)
    mixed2_f, norm_pull_mlp = jax.vjp(modulate, resid, shift_mlp, scale_mlp)
    mixed2 = mixed2_f.astype(jnp.bfloat16)
    grad_b_up = column_sums(grad_preact)
    grad_resid_norm, grad_shift_mlp, grad_scale_mlp = norm_pull_mlp(input_grad(grad_preact, w_up))
    grad_resid = gradient + grad_resid_norm
    grad_attn = (grad_resid * gate_attn).astype(jnp.bfloat16)
    grad_gate_attn = jnp.sum(grad_resid * attn_out, 0)
    grad_b_out = column_sums(grad_attn)
    grad_attended = input_grad(grad_attn, w_out).astype(jnp.bfloat16)
    grad_query, grad_keys_all, grad_values_all = attend_back(
        query, all_keys, all_values, log_total, grad_attended
    )
    grad_keys, grad_values = (
        lax.psum_scatter(
            grad_keys_all.astype(jnp.bfloat16), "seq", scatter_dimension=0, tiled=True
        ).astype(jnp.float32),
        lax.psum_scatter(
            grad_values_all.astype(jnp.bfloat16), "seq", scatter_dimension=0, tiled=True
        ).astype(jnp.float32),
    )
    grad_qkv = jnp.concatenate(
        [
            grad_query.astype(jnp.bfloat16),
            grad_keys.astype(jnp.bfloat16),
            grad_values.astype(jnp.bfloat16),
        ],
        1,
    )
    mixed1_f, norm_pull_attn = jax.vjp(modulate, stream, shift_attn, scale_attn)
    mixed1 = mixed1_f.astype(jnp.bfloat16)
    qkv_sums = column_sums(grad_qkv)
    grad_b_qv = jnp.concatenate([qkv_sums[:model_width], qkv_sums[2 * model_width :]])
    grad_stream_norm, grad_shift_attn, grad_scale_attn = norm_pull_attn(input_grad(grad_qkv, w_qkv))
    grad_stream = grad_resid + grad_stream_norm
    grad_mod_part = jnp.concatenate(
        [
            grad_shift_attn,
            grad_scale_attn,
            grad_gate_attn,
            grad_shift_mlp,
            grad_scale_mlp,
            grad_gate_mlp,
        ]
    )
    grad_mod = lax.psum(grad_mod_part, "seq").astype(jnp.bfloat16)
    seq_share = 1.0 / lax.axis_size("seq")
    grad_b_mod = grad_mod.astype(jnp.float32) * seq_share
    grad_cond_act = input_grad(grad_mod[None], w_mod)
    operands = (
        activation,
        grad_branch,
        mixed2,
        grad_preact,
        attended,
        grad_attn,
        mixed1,
        grad_qkv,
        cond_act,
        grad_mod[None],
    )
    bias_terms = (grad_b_mod, grad_b_qv, grad_b_out, grad_b_up, grad_b_down)
    return (grad_stream, grad_cond_act, operands, bias_terms)


def per_device(
    latents,
    conditioning,
    w_mod,
    b_mod,
    w_qkv,
    b_qv,
    w_out,
    b_out,
    w_up,
    b_up,
    w_down,
    b_down,
    cotangent,
):
    params = (w_mod, b_mod, w_qkv, b_qv, w_out, b_out, w_up, b_up, w_down, b_down)
    layer_count = w_mod.shape[0]
    micro_count = latents.shape[0]
    seq_share = 1.0 / lax.axis_size("seq")
    stored = [gather_once(params, 0)]
    kept_operands = [[]]
    bias_totals = [None] * layer_count
    outputs = []
    grads_in = []
    grads_cond = []
    for micro_step in range(micro_count):
        stream = latents[micro_step, 0].astype(jnp.float32)
        cond_row = conditioning[micro_step, 0:1].astype(jnp.float32)
        cond_act = jax.nn.silu(cond_row).astype(jnp.bfloat16)
        layer_index = 0
        gathered = stored[layer_index]
        stream, saved_acts = forward_layer(stream, cond_act, gathered)
        saved_list = [saved_acts]
        outputs.append(stream.astype(jnp.bfloat16))
        gradient = cotangent[micro_step, 0].astype(jnp.float32)
        grad_cond_act = jnp.zeros(cond_row.shape, jnp.float32)
        for layer_index in reversed(range(layer_count)):
            gathered = stored[layer_index]
            gradient, grad_cond_part, operands, bias_terms = backward_layer(
                gradient, saved_list[layer_index], gathered, cond_act
            )
            grad_cond_act = grad_cond_part
            kept_operands[layer_index].append(operands)
            if bias_totals[layer_index] is None:
                bias_totals[layer_index] = bias_terms
            else:
                bias_totals[layer_index] = tuple(
                    (first + second for first, second in zip(bias_totals[layer_index], bias_terms))
                )
        grads_in.append(gradient)
        silu_pull = jax.vjp(jax.nn.silu, cond_row)[1]
        grads_cond.append(silu_pull(grad_cond_act)[0])
    layer_index = 0
    joined = [
        jnp.concatenate(
            [kept_operands[layer_index][step][member] for step in range(micro_count)], 0
        )
        for member in range(10)
    ]
    grad_w_down = weight_grad(joined[0], joined[1])
    grad_w_up = weight_grad(joined[2], joined[3])
    grad_w_out = weight_grad(joined[4], joined[5])
    grad_w_qkv = weight_grad(joined[6], joined[7])
    grad_w_mod = weight_grad(joined[8], joined[9]) * seq_share
    grad_b_mod, grad_b_qv, grad_b_out, grad_b_up, grad_b_down = bias_totals[layer_index]
    totals = (
        grad_w_mod,
        grad_b_mod,
        grad_w_qkv,
        grad_b_qv,
        grad_w_out,
        grad_b_out,
        grad_w_up,
        grad_b_up,
        grad_w_down,
        grad_b_down,
    )
    dp_count = lax.axis_size("dp")
    seq_count = lax.axis_size("seq")
    stacked = [
        owner_layout(jnp.stack([totals[member]]), dp_count, seq_count) for member in range(10)
    ]
    flat = [member.reshape((dp_count * seq_count,) + member.shape[2:]) for member in stacked]
    owned = (
        lax.psum_scatter(flat[0], ("dp", "seq"), scatter_dimension=0, tiled=True),
        lax.psum_scatter(flat[1], ("dp", "seq"), scatter_dimension=0, tiled=True),
        lax.psum_scatter(flat[2], ("dp", "seq"), scatter_dimension=0, tiled=True),
        lax.psum_scatter(flat[3], ("dp", "seq"), scatter_dimension=0, tiled=True),
        lax.psum_scatter(flat[4], ("dp", "seq"), scatter_dimension=0, tiled=True),
        lax.psum_scatter(flat[5], ("dp", "seq"), scatter_dimension=0, tiled=True),
        lax.psum_scatter(flat[6], ("dp", "seq"), scatter_dimension=0, tiled=True),
        lax.psum_scatter(flat[7], ("dp", "seq"), scatter_dimension=0, tiled=True),
        lax.psum_scatter(flat[8], ("dp", "seq"), scatter_dimension=0, tiled=True),
        lax.psum_scatter(flat[9], ("dp", "seq"), scatter_dimension=0, tiled=True),
    )
    shards = [
        member.reshape(member.shape[member.ndim - stacked_member.ndim + 2 :])
        for member, stacked_member in zip(owned, stacked)
    ]
    output = jnp.stack(outputs)[:, None]
    grad_latents = jnp.stack(grads_in)[:, None]
    grad_cond = jnp.stack(grads_cond)
    return (
        output,
        grad_latents,
        grad_cond,
        shards[0],
        shards[1],
        shards[2],
        shards[3],
        shards[4],
        shards[5],
        shards[6],
        shards[7],
        shards[8],
        shards[9],
    )


MESH_IDS = pl.DeviceIdType.MESH
ANY = pl.BlockSpec(memory_space=pl.ANY)
VM = pl.BlockSpec(memory_space=pltpu.VMEM)
F32, BF = jnp.float32, jnp.bfloat16
ALL = slice(None)
ZN, XN, YN, CN = 4, 2, 2, 2
TOK = 512
CUT = 512
ROOT_2_PI = 0.7978845608028654


def dot_nn(left, right):
    return lax.dot_general(left, right, (((1,), (0,)), ((), ())), preferred_element_type=F32)


def dot_nt(left, right):
    return lax.dot_general(left, right, (((1,), (1,)), ((), ())), preferred_element_type=F32)


def dot_tn(left, right):
    return lax.dot_general(left, right, (((0,), (0,)), ((), ())), preferred_element_type=F32)


class Place:
    def __init__(self):
        dp, sq = lax.axis_index("dp"), lax.axis_index("seq")
        self.dp, self.sq = dp, sq
        self.z, self.x = dp // XN, dp % XN
        self.y, self.c = sq // CN, sq % CN
        self.xp = (self.z * XN + 1 - self.x, sq)
        self.yp = (dp, (1 - self.y) * CN + self.c)
        self.cp = (dp, self.y * CN + 1 - self.c)
        self.xyp = (self.xp[0], self.yp[1])
        self.ycp = (dp, (1 - self.y) * CN + 1 - self.c)

    def z_to(self, k):
        return (lax.rem(self.z + k, ZN) * XN + self.x, self.sq)

    def z_at(self, z):
        return (z * XN + self.x, self.sq)

    def z_from(self, k):
        return lax.rem(self.z + ZN - k, ZN)

    def barrier(self):
        sem = pltpu.get_barrier_semaphore()
        peers = [self.z_to(1), self.z_to(2), self.z_to(3), self.xp, self.yp, self.cp, self.xyp, self.ycp]
        for peer in peers:
            pl.semaphore_signal(sem, inc=1, device_id=peer, device_id_type=MESH_IDS)
        pl.semaphore_wait(sem, len(peers))


class Links:
    def __init__(self):
        self.sent = []

    def copy(self, src, dst, send_sem, recv_sem, peer):
        return pltpu.make_async_remote_copy(
            src_ref=src, dst_ref=dst, send_sem=send_sem, recv_sem=recv_sem, device_id=peer, device_id_type=MESH_IDS
        )

    def send(self, src, dst, send_sem, recv_sem, peer, when=None):
        copy = self.copy(src, dst, send_sem, recv_sem, peer)
        guarded(when, copy.start)
        self.sent.append((copy, when))

    def drain(self):
        for copy, when in self.sent:
            guarded(when, copy.wait_send)
        self.sent = []


def pieces_of(rows, cols):
    if rows == 32:
        return (
            ("zyx", (pl.ds(0, 16), pl.ds(0, cols))),
            ("zxy", (pl.ds(16, 16), pl.ds(0, CUT))),
            ("yxz", (pl.ds(16, 16), pl.ds(CUT, cols - CUT))),
        )
    return (("zyx", (0,)), ("zxy", (1, 0)), ("yxz", (1, 1)))


def line_gather(at, idx_of):
    z = at.z
    inner, outer = (z == 1) | (z == 2), (z == 0) | (z == 3)
    near = jnp.where(z == 1, 0, 3)
    return (
        [
            (idx_of(z), at.z_at(jnp.minimum(z + 1, 3)), idx_of(jnp.maximum(z - 1, 0)), z < 3, z > 0),
            (idx_of(z), at.z_at(jnp.maximum(z - 1, 0)), idx_of(jnp.minimum(z + 1, 3)), z > 0, z < 3),
        ],
        [
            (idx_of(3 - z), at.z_at(near), idx_of(jnp.where(z == 0, 2, 1)), inner, outer),
            (idx_of(near), at.z_at(jnp.where(z == 1, 2, 1)), idx_of(jnp.where(z == 2, 0, 3)), inner, inner),
            (idx_of(near), at.z_at(3 - near), idx_of(jnp.where(z == 3, 0, 3)), inner, outer),
        ],
    )


def gather_steps(at, kind):
    z, x, y, c = at.z, at.x, at.y, at.c
    if kind == "yxz":
        return (
            [((z, x, y, c), at.yp, (z, x, 1 - y, c), None, None)],
            [((z, x, ALL, c), at.xp, (z, 1 - x, ALL, c), None, None)],
            *line_gather(at, lambda q: (q, ALL, ALL, c)),
        )
    first = line_gather(at, lambda q: (q, x, y, c))
    if kind == "zyx":
        return (
            *first,
            [((ALL, x, y, c), at.yp, (ALL, x, 1 - y, c), None, None)],
            [((ALL, x, ALL, c), at.xp, (ALL, 1 - x, ALL, c), None, None)],
        )
    return (
        *first,
        [((ALL, x, y, c), at.xp, (ALL, 1 - x, y, c), None, None)],
        [((ALL, ALL, y, c), at.yp, (ALL, ALL, 1 - y, c), None, None)],
    )


def line_scatter(at):
    z = at.z
    inner, outer = (z == 1) | (z == 2), (z == 0) | (z == 3)
    return (
        [
            (jnp.where(z == 0, 2, 1), jnp.where(z == 0, 1, 2), 0, outer, inner),
            (jnp.where(z == 2, 0, 3), 3 - z, 1, inner, inner),
            (3 - z, jnp.where(z == 0, 2, 1), 2, outer, inner),
        ],
        [(jnp.minimum(z + 1, 3), jnp.minimum(z + 1, 3), 0, z < 3, z > 0), (jnp.maximum(z - 1, 0), jnp.maximum(z - 1, 0), 1, z > 0, z < 3)],
    )


def guarded(condition, action):
    if condition is None:
        action()
    else:
        pl.when(condition)(action)


def norm_rows(values):
    centred = values - jnp.mean(values, -1, keepdims=True)
    inv = lax.rsqrt(jnp.mean(centred * centred, -1, keepdims=True) + EPS)
    return centred * inv, inv


def scatter_steps(at):
    z, x, y = at.z, at.x, at.y

    def line(piece, number, block):
        return [(piece, block(q), at.z_at(to), slot, sends, receives) for q, to, slot, sends, receives in line_scatter(at)[number]]

    def ends(q):
        return (q, x, y)

    return (
        [(0, (ALL, 1 - x, ALL), at.xp, None, None, None), (1, (ALL, ALL, 1 - y), at.yp, None, None, None)] + line(2, 0, lambda q: (q, ALL, ALL)),
        [(0, (ALL, x, 1 - y), at.yp, None, None, None), (1, (ALL, 1 - x, y), at.xp, None, None, None)] + line(2, 1, lambda q: (q, ALL, ALL)),
        line(0, 0, ends) + line(1, 0, ends) + [(2, (z, 1 - x, ALL), at.xp, None, None, None)],
        line(0, 1, ends) + line(1, 1, ends) + [(2, (z, x, 1 - y), at.yp, None, None, None)],
    )


LR = 5
PIECE_ROWS = (slice(0, 16), slice(16, 32), slice(16, 32))
PIECE_COLS = (slice(0, 1024), slice(0, CUT), slice(CUT, 1024))
LANDING = (
    ((LR, 4, 2, 16, 1024), (LR, 4, 2, 16, CUT), (LR, 3, 2, 2, 16, 1024 - CUT)),
    ((LR, 4, 16, 1024), (LR, 4, 16, CUT), (LR, 2, 2, 2, 16, 1024 - CUT)),
    ((LR, 3, 16, 1024), (LR, 3, 16, CUT), (LR, 2, 16, 1024 - CUT)),
    ((LR, 2, 16, 1024), (LR, 2, 16, CUT), (LR, 16, 1024 - CUT)),
)


RB = 128


def block_kernel(
    lat, cot, cond_in, b_mod, b_qv, b_out, b_up, b_down, w_mod, w_qkv, w_out, w_up, w_down,
    o_out, o_gl, o_qkv, o_wo, o_up, o_dn, o_mod, o_bmod, o_bias, o_gc, t_w, t_x, t_m1, t_q, t_k, t_v, t_att, t_ao,
    W8, WD, CR, RC, L00, L01, L02, L10, L11, L12, L20, L21, L22, L30, L31, L32,
    act, gp, m2, gb, res, acc, br, cs, xs, fin, lse,
    SM, PM, PY, PX, PZ, FM, PC, wm, cact, vec, bias, sums, GS, GP, GM, bsum, BA, BB, GC, GCX, brow,
    gs, gr, gcs, gcr, rss, rsr, rcs, rcr, dcs, dcr, credit, credit_c, ready_c, sx, rx, sy, ry, ssm, rsm, lw, lo, ld, lf,
):
    at = Place()
    z, x, y, c = at.z, at.x, at.y, at.c
    links = Links()
    lane = lax.broadcasted_iota(jnp.int32, (1, 128), 1)
    inner = (z == 1) | (z == 2)
    near = jnp.where(z == 1, 0, 3)

    outgoing = []

    def save(src, dst):
        copy = pltpu.make_async_copy(src, dst, lo.at[len(outgoing)])
        copy.start()
        outgoing.append(copy)
        return copy

    loads = {}

    def load(name, src, dst):
        copy = pltpu.make_async_copy(src, dst, ld.at[len(loads)])
        copy.start()
        loads[name] = copy

    def loaded(name):
        loads[name].wait()

    ORDER = (0, 1, 2, 3, 8, 9, 10, 11, 4, 5, 6, 7)
    plans = {kind: gather_steps(at, kind) for kind in ("zyx", "zxy", "yxz")}

    def block(unit, idx, part=()):
        ref = W8.at[unit] if unit < 8 else WD.at[unit - 8]
        return ref.at[idx + part]

    def shard(unit):
        if unit < 3:
            return w_qkv.at[:, pl.ds((1024, 2048, 0)[unit], 1024)]
        if unit == 3:
            return w_out
        if unit < 8:
            return w_up.at[:, pl.ds((unit - 4) * 1024, 1024)]
        return w_down.at[:, :, :, pl.ds((unit - 8) * 256, 256)]

    def pieces(unit):
        return pieces_of(32, 1024) if unit < 8 else pieces_of(128, 256)

    gather_sent = {unit: [] for unit in range(12)}
    steps_at = {}
    for i, (kind, _) in enumerate(pieces(0)):
        for number in range(4):
            for j in range(len(plans[kind][number])):
                steps_at[number, i, j] = len(steps_at)

    def gather_sems(unit, number, i, j):
        k = steps_at[number, i, j]
        return gs.at[ORDER.index(unit) % 7, k], gr.at[unit, k]

    def step(unit, number):
        for i, (kind, part) in enumerate(pieces(unit)):
            for j, (idx, peer, _, sends, _) in enumerate(plans[kind][number]):
                ref = block(unit, idx, part)
                copy = links.copy(ref, ref, *gather_sems(unit, number, i, j), peer)
                guarded(sends, copy.start)
                gather_sent[unit].append((copy, sends))

    def arrived(unit, number):
        for i, (kind, part) in enumerate(pieces(unit)):
            for j, (_, peer, idx, _, receives) in enumerate(plans[kind][number]):
                ref = block(unit, idx, part)
                guarded(receives, links.copy(ref, ref, *gather_sems(unit, number, i, j), peer).wait_recv)

    local_w = [pltpu.make_async_copy(shard(u), block(u, (z, x, y, c)), lw.at[u]) for u in range(12)]

    def gather_stage(unit, number):
        if number == 0:
            if ORDER.index(unit) >= 7:
                gather_done(ORDER[ORDER.index(unit) - 7])
            local_w[unit].wait()
        else:
            arrived(unit, number - 1)
        if number < 4:
            step(unit, number)
        else:
            ref = block(unit, (ALL, ALL, ALL, c))
            copy = links.copy(ref, ref, gcs.at[unit], gcr.at[unit], at.cp)
            copy.start()
            gather_sent[unit].append((copy, None))

    def ready(unit):
        ref = block(unit, (ALL, ALL, ALL, 1 - c))
        links.copy(ref, ref, gcs.at[unit], gcr.at[unit], at.cp).wait_recv()

    def gather_tick(t):
        for number in (1, 2, 3):
            if 0 <= t + 1 - number < 12:
                gather_stage(ORDER[t + 1 - number], number)
        if t + 3 < 12:
            gather_stage(ORDER[t + 3], 0)
        if 0 <= t - 3 < 12:
            gather_stage(ORDER[t - 3], 4)

    def gather_done(unit):
        for copy, sends in gather_sent.pop(unit, ()):
            guarded(sends, copy.wait_send)

    scatter_plan = scatter_steps(at)
    landing = ((L00, L01, L02), (L10, L11, L12), (L20, L21, L22), (L30, L31, L32))
    unit_sent = [[] for _ in range(12)]
    finished = set()

    def at_block(n, idx):
        if 4 <= n < 8:
            return CR, idx + ((n - 4) // 2, (n - 4) % 2)
        return RC, (n % 4 if n < 4 else n - 8,) + idx

    def part_ref(n, idx, piece):
        ref, full = at_block(n, idx)
        return ref.at[full + (PIECE_ROWS[piece], PIECE_COLS[piece])]

    def copies(n, number):
        result = []
        for i, (piece, go, peer, slot, sends, receives) in enumerate(scatter_plan[number]):
            dst = landing[number][piece].at[n % LR]
            dst = dst if slot is None else dst.at[slot]
            k = (0, 5, 9, 16)[number] + i
            result.append((links.copy(part_ref(n, go, piece), dst, rss.at[n % LR, k], rsr.at[n % LR, k], peer), sends, receives))
        return result

    def send_step(n, number):
        for copy, sends, _ in copies(n, number):
            guarded(sends, copy.start)
            unit_sent[n].append((copy, sends))

    def add_into(n, number):
        for copy, _, receives in copies(n, number):
            guarded(receives, copy.wait_recv)
        s = n % LR

        def plus(idx, piece, *came):
            ref, full = at_block(n, idx)
            full = full + (PIECE_ROWS[piece], PIECE_COLS[piece])
            if len(came) == 1:
                ref[full] = ref[full] + came[0]
            else:
                ref[full] = (ref[full].astype(F32) + (came[0].astype(F32) + came[1].astype(F32))).astype(BF)

        if number == 0:
            def add(i, carry):
                for e in range(2):
                    plus((i, x, e), 0, L00[s, i, e])
                    plus((i, e, y), 1, L01[s, i, e])
                return carry

            lax.fori_loop(0, 4, add, 0)

            @pl.when(inner)
            def _():
                def add_line(i, carry):
                    xi, yi = i // 2, i % 2
                    plus((3 - z, xi, yi), 2, L02[s, 0, xi, yi])
                    plus((near, xi, yi), 2, L02[s, 1, xi, yi], L02[s, 2, xi, yi])
                    return carry

                lax.fori_loop(0, 4, add_line, 0)
        elif number == 1:
            def add(i, carry):
                plus((i, x, y), 0, L10[s, i])
                plus((i, x, y), 1, L11[s, i])
                return carry

            lax.fori_loop(0, 4, add, 0)
            for slot_in, came in ((0, z > 0), (1, z < 3)):
                @pl.when(came)
                def _():
                    def add_line(i, carry):
                        xi, yi = i // 2, i % 2
                        plus((z, xi, yi), 2, L12[s, slot_in, xi, yi])
                        return carry

                    lax.fori_loop(0, 4, add_line, 0)
        elif number == 2:
            @pl.when(inner)
            def _():
                for piece, ref in ((0, L20), (1, L21)):
                    plus((3 - z, x, y), piece, ref[s, 0])
                    plus((near, x, y), piece, ref[s, 1], ref[s, 2])

            for e in range(2):
                plus((z, x, e), 2, L22[s, e])

    cores_sent = {}

    def core_copy(n, d):
        return links.copy(W8.at[d, :, :, :, 1 - c], RC.at[n % 4 if n < 4 else n - 8], rcs.at[n], rcr.at[n], at.cp)

    def slot_free(d):
        for copy in cores_sent.pop(d, ()):
            copy.wait_send()

    def put_grad(n, d, left, right):
        slot_free(d)
        for t in range(2):
            cols = slice(512 * t, 512 * t + 512)
            W8[d, :, :, :, :, :, cols] = dot_tn(left, right(cols)).astype(BF).reshape(4, 2, 2, 2, 32, 512)
        if n >= 8:
            assert n - 8 in finished
            pl.semaphore_wait(credit_c.at[n - 8], 1)
        copy = core_copy(n, d)
        copy.start()
        cores_sent[d] = (copy,)
        slot_of_unit[n] = d
        if n != 8:
            waiting[n] = 1

    slot_of_unit = {}

    def r1(n):
        if not 4 <= n < 8:
            d = slot_of_unit[n]
            core_copy(n, d).wait_recv()
            slot = n % 4 if n < 4 else n - 8

            def add(i, carry):
                zi, xi, yi = i // 4, (i // 2) % 2, i % 2
                RC[slot, zi, xi, yi] = RC[slot, zi, xi, yi] + W8[d, zi, xi, yi, c]
                return carry

            lax.fori_loop(0, 16, add, 0)
        if n >= LR:
            assert n - LR in finished
            pl.semaphore_wait(credit.at[n - LR], 5)
        send_step(n, 0)

    def middle(number):
        def run(n):
            add_into(n, number)
            send_step(n, number + 1)

        return run

    fin_saved = {}

    def r5(n):
        for copy, _, receives in copies(n, 3):
            guarded(receives, copy.wait_recv)
        s, f = n % LR, n % 3
        if n - 3 in fin_saved:
            fin_saved.pop(n - 3).wait()
        ref_, full = at_block(n, (z, x, y))
        for piece, ref in ((0, L30), (1, L31)):
            rows, cols = PIECE_ROWS[piece], PIECE_COLS[piece]
            fin[f, rows, cols] = ref_[full + (rows, cols)].astype(F32)
            for slot_in, came in ((0, z > 0), (1, z < 3)):
                @pl.when(came)
                def _():
                    fin[f, rows, cols] = fin[f, rows, cols] + ref[s, slot_in].astype(F32)
        fin[f, 16:32, CUT:] = ref_[full + (slice(16, 32), slice(CUT, 1024))].astype(F32) + L32[s].astype(F32)
        if n < 4:
            dst = o_up.at[:, pl.ds(1024 * n, 1024)]
        elif n < 8:
            dst = o_dn.at[pl.ds(32 * (n - 4), 32)]
        elif n == 8:
            dst = o_wo
        else:
            dst = o_qkv.at[:, pl.ds(1024 * (n - 9), 1024)]
        fin_saved[n] = pltpu.make_async_copy(fin.at[f], dst, lf.at[f])
        fin_saved[n].start()
        for copy, sends in unit_sent[n]:
            guarded(sends, copy.wait_send)
        if n + LR < 12:
            for peer in (at.z_to(1), at.z_to(2), at.z_to(3), at.xp, at.yp):
                pl.semaphore_signal(credit.at[n], inc=1, device_id=peer, device_id_type=MESH_IDS)
        if n < 4:
            pl.semaphore_signal(credit_c.at[n], inc=1, device_id=at.cp, device_id_type=MESH_IDS)
        finished.add(n)

    stages = {1: r1, 2: middle(0), 3: middle(1), 4: middle(2), 5: r5}
    waiting = {}

    def tick():
        for n in sorted(waiting, reverse=True):
            stages[waiting[n]](n)
            waiting[n] += 1
            if waiting[n] == 6:
                del waiting[n]

    def fold(values):
        return jnp.sum(values.reshape(-1, 8, values.shape[-1]), 0)

    local_m = pltpu.make_async_copy(w_mod, wm, lw.at[12])
    local_x = pltpu.make_async_copy(lat.at[y], xs.at[y], lw.at[13])
    local_c = pltpu.make_async_copy(cot.at[y], cs.at[y], lw.at[14])
    for copy in local_w[:3] + [local_m, local_x] + local_w[3:] + [local_c]:
        copy.start()
    index = at.dp * (YN * CN) + at.sq

    def table(line, value):
        SM[z, x, y, c, line : line + 1, :] = value

    rows_in = cond_in[...].astype(F32)
    for m in range(2):
        for j in range(8):
            table(8 * m + j, rows_in[m : m + 1, 128 * j : 128 * j + 128])
    for line, ref in ((16, b_qv), (17, b_out), (18, b_up), (19, b_down)):
        size = ref.shape[1]
        wide = jnp.concatenate([ref[...].astype(F32)] * (128 // size), 1) if size < 128 else ref[...].astype(F32)
        table(line, jnp.where(lane // size == lax.rem(index, 128 // size), wide, 0.0))
    bm = b_mod[...].astype(F32)
    none = jnp.zeros((1, 64), F32)
    even = lax.rem(index, 2) == 0
    table(20, jnp.where(even, bm[:, :128], jnp.concatenate([none, bm[:, :64]], 1)))
    table(21, jnp.where(even, jnp.concatenate([bm[:, 128:], none], 1), bm[:, 64:]))
    at.barrier()

    def small_send(idx, peer, n):
        links.send(SM.at[idx], SM.at[idx], ssm.at[n], rsm.at[n], peer)

    def small_wait(idx, n):
        links.copy(SM.at[idx], SM.at[idx], ssm.at[n], rsm.at[n], at.xp).wait_recv()

    for k in (1, 2, 3):
        small_send((z, x, y, c), at.z_to(k), k - 1)
    gather_stage(ORDER[0], 0)
    links.send(lat.at[1 - y], xs.at[y], sx.at[0], rx.at[0], at.yp)
    gather_stage(ORDER[1], 0)
    for k in (1, 2, 3):
        small_wait((at.z_from(k), x, y, c), k - 1)
    small_send((ALL, x, y, c), at.xp, 3)
    gather_stage(ORDER[2], 0)
    gather_tick(0)
    small_wait((ALL, 1 - x, y, c), 3)
    small_send((ALL, ALL, y, c), at.yp, 4)

    row = lax.broadcasted_iota(jnp.int32, (8, 128), 0)
    for m in range(2):
        for p in range(8):
            tile = SM[p // 2, p % 2, y, c, 8 * m : 8 * m + 8, :]
            cact[8 * m + p : 8 * m + p + 1, :] = jnp.sum(jnp.where(row == at.dp, tile, 0.0), 0, keepdims=True)
    cond = cact[...]
    cond = jnp.where(lane // 32 == at.sq, cond / (1.0 + jnp.exp(-cond)), 0.0)
    cact[...] = cond
    cond_low = ((cond[:, 0:32] + cond[:, 32:64]) + (cond[:, 64:96] + cond[:, 96:128])).astype(BF)
    local_m.wait()
    for i in range(6):
        part = dot_nn(cond_low, wm[:, 1024 * i : 1024 * i + 1024])
        for m in range(2):
            for p in range(8):
                for j in range(8):
                    PM[m, p // 2, p % 2, 8 * i + j : 8 * i + j + 1, :] = part[8 * m + p : 8 * m + p + 1, 128 * j : 128 * j + 128]
    links.send(PM.at[:, :, 1 - x], PX, sx.at[1], rx.at[1], at.xp)
    gather_tick(1)
    links.copy(PM.at[:, :, 1 - x], PX, sx.at[1], rx.at[1], at.xp).wait_recv()
    for m in range(2):
        PM[m, :, x] = PM[m, :, x] + PX[m]
    links.send(PM.at[1 - y, :, x], PY, sx.at[2], rx.at[2], at.yp)
    small_wait((ALL, ALL, 1 - y, c), 4)
    small_send((ALL, ALL, ALL, c), at.cp, 5)
    gather_tick(2)
    links.copy(PM.at[1 - y, :, x], PY, sx.at[2], rx.at[2], at.yp).wait_recv()
    PM[y, :, x] = PM[y, :, x] + PY[...]
    for k in (1, 2, 3):
        to = lax.rem(z + k, ZN)
        links.send(PM.at[y, to, x], PZ.at[k - 1], sx.at[2 + k], rx.at[2 + k], at.z_to(k))
    gather_tick(3)
    for k in (1, 2, 3):
        links.copy(PM.at[y, z, x], PZ.at[k - 1], sx.at[2 + k], rx.at[2 + k], at.z_to(k)).wait_recv()
    FM[...] = PM[y, z, x] + PZ[0] + PZ[1] + PZ[2]
    links.send(FM, PC, sx.at[6], rx.at[6], at.cp)
    small_wait((ALL, ALL, ALL, 1 - c), 5)

    def entry(device, line):
        return SM[device // 8, (device // 4) % 2, (device // 2) % 2, device % 2, line : line + 1, :]

    for t in range(16):
        bias[0:1, 128 * t : 128 * t + 128] = entry(2 * t, 16) + entry(2 * t + 1, 16)
    for t in range(8):
        bias[0:1, 2048 + 128 * t : 2176 + 128 * t] = (entry(4 * t, 17) + entry(4 * t + 1, 17)) + (entry(4 * t + 2, 17) + entry(4 * t + 3, 17))
        bias[0:1, 7168 + 128 * t : 7296 + 128 * t] = (entry(4 * t, 19) + entry(4 * t + 1, 19)) + (entry(4 * t + 2, 19) + entry(4 * t + 3, 19))
    for t in range(32):
        bias[0:1, 3072 + 128 * t : 3200 + 128 * t] = entry(t, 18)
    links.copy(FM, PC, sx.at[6], rx.at[6], at.cp).wait_recv()
    for j in range(48):
        k, third = j // 3, j % 3
        if third == 0:
            b_row = entry(2 * k, 20)
        elif third == 1:
            b_row = entry(2 * k, 21) + entry(2 * k + 1, 20)
        else:
            b_row = entry(2 * k + 1, 21)
        vec[j // 8 : j // 8 + 1, 128 * (j % 8) : 128 * (j % 8) + 128] = FM[j : j + 1, :] + PC[j : j + 1, :] + b_row
    shift_attn, scale_attn, gate_attn = vec[0:1, :], 1.0 + vec[1:2, :], vec[2:3, :]
    shift_mlp, scale_mlp, gate_mlp = vec[3:4, :], 1.0 + vec[4:5, :], vec[5:6, :]

    local_x.wait()
    links.copy(lat.at[1 - y], xs.at[1 - y], sx.at[0], rx.at[0], at.yp).wait_recv()

    def halves(i):
        return i // (256 // RB), pl.ds(pl.multiple_of((i % (256 // RB)) * RB, RB), RB)

    def norm1(i, carry):
        half, rows = halves(i)
        n, _ = norm_rows(xs[half, rows, :].astype(F32))
        gp[0, pl.ds(pl.multiple_of(i * RB, RB), RB), :] = (n * scale_attn + shift_attn).astype(BF)
        return carry

    lax.fori_loop(0, TOK // RB, norm1, 0)
    x_saved = save(xs, t_x)
    m1_saved = save(gp.at[0], t_m1)
    gather_tick(4)

    def weight(unit, cols):
        return W8[unit, :, :, :, :, :, cols].reshape(1024, -1)

    def project(unit, put):
        for t in range(2):
            cols = slice(512 * t, 512 * t + 512)
            put(cols, dot_nn(gp[0], weight(unit, cols)))

    def rows512(value):
        return value.astype(BF).reshape(2, 2, 2, 2, 32, -1)

    def put_k(cols, value):
        CR[0, :, :, :, :, :, cols] = rows512(value)

    def put_v(cols, value):
        CR[2, :, :, :, :, :, cols] = rows512(value + bias[0:1, 1024 + cols.start : 1024 + cols.stop])

    def put_q(cols, value):
        act[0, :, :, :, :, :, cols] = rows512(value + bias[0:1, cols])

    ready(0)
    w_saved = [save(W8.at[0], t_w.at[0])]
    project(0, put_k)
    k_sent = links.copy(CR.at[0], CR.at[1], sx.at[8], rx.at[8], at.cp)
    k_sent.start()
    gather_tick(5)
    ready(1)
    w_saved.append(save(W8.at[1], t_w.at[1]))
    project(1, put_v)
    v_sent = links.copy(CR.at[2], CR.at[3], sx.at[9], rx.at[9], at.cp)
    v_sent.start()
    gather_tick(6)
    ready(2)
    links.send(cot.at[1 - y], cs.at[y], sx.at[7], rx.at[7], at.yp)
    project(2, put_q)
    q_saved = save(act.at[0], t_q)
    k_sent.wait_recv()
    v_sent.wait_recv()
    kv_saved = [save(CR.at[pl.ds(0, 2)], t_k), save(CR.at[pl.ds(2, 2)], t_v)]

    def attend_pair(p, carry):
        cols = pl.ds(pl.multiple_of(p * 128, 128), 128)
        k2, v2 = CR[0:2, :, :, :, :, :, cols].reshape(1024, 128), CR[2:4, :, :, :, :, :, cols].reshape(1024, 128)
        for t in range(2):
            rows = slice(256 * t, 256 * t + 256)
            q2 = act[0, t, :, :, :, :, cols].reshape(256, 128)
            parts = []
            for e in range(2):
                own = (lane < 64) == (e == 0)
                qe = jnp.where(own, q2, jnp.zeros_like(q2)) * BF(0.125)
                scores = dot_nt(qe, k2)
                top = jnp.max(scores, 1, keepdims=True)
                expon = jnp.exp(scores - top)
                total = jnp.sum(expon, 1, keepdims=True)
                parts.append(dot_nn((expon * (1.0 / total)).astype(BF), v2))
                log_total = jnp.broadcast_to(top + jnp.log(total), (256, 128)).T
                lse[p, e : e + 1, rows] = log_total[0:1, :]
            act[1, t, :, :, :, :, cols] = jnp.where(lane < 64, parts[0], parts[1]).astype(BF).reshape(2, 2, 2, 32, 128)
        return carry

    lax.fori_loop(0, 2, attend_pair, 0)
    gather_tick(7)
    lax.fori_loop(2, 4, attend_pair, 0)
    gather_tick(8)
    lax.fori_loop(4, 6, attend_pair, 0)
    gather_tick(9)
    lax.fori_loop(6, 8, attend_pair, 0)
    gather_tick(10)
    att_saved = save(act.at[1], t_att)
    for copy in kv_saved + [q_saved]:
        copy.wait()
    k_sent.wait_send()
    v_sent.wait_send()
    pl.semaphore_signal(ready_c, inc=1, device_id=at.cp, device_id_type=MESH_IDS)
    ready(3)
    local_c.wait()
    links.copy(cot.at[1 - y], cs.at[1 - y], sx.at[7], rx.at[7], at.yp).wait_recv()

    for t in range(2):
        cols = slice(512 * t, 512 * t + 512)
        value = dot_nn(act[1].reshape(512, 1024), weight(3, cols)) + bias[0:1, 2048 + 512 * t : 2560 + 512 * t]
        gp[1, :, cols] = value.astype(BF)
        res[:, cols] = xs[:, :, cols].reshape(TOK, 512).astype(F32) + gate_attn[:, cols] * value
    ao_saved = save(gp.at[1], t_ao)
    gather_tick(11)
    for i in range(13):
        sums[i] = jnp.zeros((8, 1024), F32)

    def norm2(i, carry):
        rows = pl.ds(pl.multiple_of(i * RB, RB), RB)
        half, part = halves(i)
        n, _ = norm_rows(res[rows, :])
        m2[rows, :] = (n * scale_mlp + shift_mlp).astype(BF)
        low = (cs[half, part, :].astype(F32) * gate_mlp).astype(BF)
        gb[rows, :] = low
        sums[8] = sums[8] + fold(low.astype(F32))
        return carry

    lax.fori_loop(0, TOK // RB, norm2, 0)
    for copy in [x_saved, m1_saved, att_saved, ao_saved] + w_saved:
        copy.wait()
    for unit in (8, 9, 10, 11):
        ready(unit)
    gather_done(0)
    gather_done(1)

    def down_rows(j, u):
        return WD[j, u].reshape(1024, 256)

    def down_copies(u):
        return [
            links.copy(W8.at[1, pl.ds(2 * xi, 2), 1 - c], CR.at[u, xi], dcs.at[u, xi], dcr.at[u, xi], at.cp)
            for xi in range(2)
        ]

    def mlp(u):
        for t in range(2):
            cols = slice(512 * t, 512 * t + 512)
            first = 3072 + 1024 * u + 512 * t
            v = dot_nn(m2[...], weight(4 + u, cols)) + bias[0:1, first : first + 512]
            rows = jnp.concatenate([WD[j, u, t].reshape(512, 256) for j in range(4)], 1)
            slope = dot_nt(gb[...], rows)
            square = v * v
            th = jnp.tanh(ROOT_2_PI * v * (1.0 + 0.044715 * square))
            up = 0.5 + 0.5 * th
            act[0, :, :, :, :, :, cols] = rows512(v * up)
            low = (slope * (up + 0.5 * v * (1.0 - th * th) * (ROOT_2_PI + (ROOT_2_PI * 3 * 0.044715) * square))).astype(BF)
            gp[0, :, cols] = low
            sums[9 + u, :, cols] = fold(low.astype(F32))
        put_grad(u, 0, m2[...], lambda cols: gp[0, :, cols])
        slot_free(1)
        acts = act[0].reshape(512, 1024)
        for t in range(2):
            cols = slice(512 * t, 512 * t + 512)
            W8[1, :, :, :, :, :, cols] = dot_tn(acts, gb[:, cols]).astype(BF).reshape(4, 2, 2, 2, 32, 512)
        if u == 0:
            pl.semaphore_wait(ready_c, 1)
        cores_sent[1] = down_copies(u)
        for copy in cores_sent[1]:
            copy.start()
        for t in range(2):
            cols = slice(512 * t, 512 * t + 512)
            back = dot_nt(gp[0], W8[4 + u, 2 * t : 2 * t + 2].reshape(512, 1024))
            ahead = dot_nn(acts, jnp.concatenate([down_rows(2 * t, u), down_rows(2 * t + 1, u)], 1))
            acc[:, cols] = back if u == 0 else acc[:, cols] + back
            br[:, cols] = ahead if u == 0 else br[:, cols] + ahead

    def down_sum(u):
        for copy in down_copies(u):
            copy.wait_recv()

        def add(i, carry):
            xi, yi, a, b = i // 8, (i // 4) % 2, (i // 2) % 2, i % 2
            CR[u, xi, yi, a, b] = CR[u, xi, yi, a, b] + W8[1, 2 * xi + yi, c, a, b]
            return carry

        lax.fori_loop(0, 16, add, 0)

    for u in range(4):
        ready(4 + u)
        mlp(u)
        if u < 3:
            gather_tick(12 + u)
        tick()
        down_sum(u)
    waiting[4] = 1

    def output(i, carry):
        rows = pl.ds(pl.multiple_of(i * RB, RB), RB)
        half, part = halves(i)
        branch = br[rows, :] + bias[0:1, 7168:8192]
        sums[6] = sums[6] + fold(cs[half, part, :].astype(F32) * branch)
        xs[half, part, :] = (res[rows, :] + gate_mlp * branch).astype(BF)
        return carry

    lax.fori_loop(0, TOK // RB, output, 0)
    vec[6:7, :] = jnp.sum(sums[6], 0, keepdims=True)
    out_saved = save(xs.at[y], o_out.at[y])
    links.send(xs.at[1 - y], o_out.at[y], sx.at[10], rx.at[10], at.yp)
    for unit in (2, 3, 4, 5, 6, 7, 8, 9, 10, 11):
        gather_done(unit)
    load("ao", t_ao, gp.at[1])
    for j in range(4):
        cols = pl.ds(256 * j, 256)
        load(f"k{j}", t_k.at[:, :, :, :, :, :, cols], WD.at[j, 0])
        load(f"v{j}", t_v.at[:, :, :, :, :, :, cols], WD.at[j, 1])
        load(f"q{j}", t_q.at[:, :, :, :, :, cols], WD.at[j, 2, 0])
        load(f"att{j}", t_att.at[:, :, :, :, :, cols], WD.at[j, 2, 1])
    load("m1", t_m1, gp.at[0])
    load("wk", t_w.at[0], W8.at[4])
    load("wv", t_w.at[1], W8.at[5])

    loaded("ao")

    def norm2_back(i, carry):
        rows = pl.ds(pl.multiple_of(i * RB, RB), RB)
        half, part = halves(i)
        n, inv = norm_rows(res[rows, :])
        up = acc[rows, :]
        gn = up * n
        sums[3] = sums[3] + fold(up)
        sums[4] = sums[4] + fold(gn)
        g = up * scale_mlp
        total = cs[half, part, :].astype(F32) + (g - jnp.mean(g, -1, keepdims=True) - n * jnp.mean(gn * scale_mlp, -1, keepdims=True)) * inv
        acc[rows, :] = total
        sums[2] = sums[2] + fold(total * gp[1, rows, :].astype(F32))
        low = (total * gate_attn).astype(BF)
        gb[rows, :] = low
        sums[5] = sums[5] + fold(low.astype(F32))
        return carry

    lax.fori_loop(0, TOK // RB, norm2_back, 0)
    for half in range(2):
        load(f"x{half}", t_x.at[half], gp.at[1, pl.ds(256 * half, 256)])
    for t in range(2):
        value = dot_nt(gb[...], W8[3, 2 * t : 2 * t + 2].reshape(512, 1024)).astype(BF)
        for h in range(2):
            WD[2 * t + h, 3, 0] = value[:, 256 * h : 256 * h + 256].reshape(2, 2, 2, 2, 32, 256)
    tick()
    for j in range(4):
        for name in ("k", "v", "q", "att"):
            loaded(f"{name}{j}")

    def wide(a, b):
        return jnp.concatenate([WD[j, a, b].reshape(512, 256) for j in range(4)], 1)

    put_grad(8, 0, wide(2, 1), lambda cols: gb[:, cols])

    def attend_back(p, carry):
        j, cols = p // 2, pl.ds(pl.multiple_of((p % 2) * 128, 128), 128)
        full = pl.ds(pl.multiple_of(p * 128, 128), 128)
        k2, v2 = WD[j, 0, :, :, :, :, :, :, cols].reshape(1024, 128), WD[j, 1, :, :, :, :, :, :, cols].reshape(1024, 128)
        keys_sum, values_sum = None, None
        for t in range(2):
            rows = slice(256 * t, 256 * t + 256)
            q2, do2 = WD[j, 2, 0, t, :, :, :, :, cols].reshape(256, 128), WD[j, 3, 0, t, :, :, :, :, cols].reshape(256, 128)
            prod = (do2.astype(F32) * WD[j, 2, 1, t, :, :, :, :, cols].reshape(256, 128).astype(F32)).T
            queries = []
            for e in range(2):
                own = (lane < 64) == (e == 0)
                qe = jnp.where(own, q2, jnp.zeros_like(q2)) * BF(0.125)
                de = jnp.where(own, do2, jnp.zeros_like(do2))
                row_dot = jnp.sum(prod[64 * e : 64 * e + 64, :], 0, keepdims=True)
                probs = jnp.exp(dot_nt(k2, qe) - lse[p, e : e + 1, rows])
                grad_scores = (probs * (dot_nt(v2, de) - row_dot)).astype(BF)
                queries.append(dot_tn(grad_scores, k2))
                a, b = dot_nn(grad_scores, qe), dot_nn(probs.astype(BF), de)
                keys_sum = a if keys_sum is None else keys_sum + a
                values_sum = b if values_sum is None else values_sum + b
            grad_query = (jnp.where(lane < 64, queries[0], queries[1]) * 0.125).astype(BF)
            WD[j, 3, 1, t, :, :, :, :, cols] = grad_query.reshape(2, 2, 2, 32, 128)
        W8[6, :, :, :, :, :, full] = keys_sum.astype(BF).reshape(4, 2, 2, 2, 32, 128)
        W8[7, :, :, :, :, :, full] = values_sum.astype(BF).reshape(4, 2, 2, 2, 32, 128)
        return carry

    for first, release in ((0, 5), (2, 6), (4, 7)):
        lax.fori_loop(first, first + 2, attend_back, 0)
        waiting[release] = 1
        tick()
    lax.fori_loop(6, 8, attend_back, 0)
    waiting[8] = 1
    links.send(W8.at[6, pl.ds(2, 2)], act.at[0], sx.at[11], rx.at[11], at.cp)
    links.send(W8.at[7, pl.ds(2, 2)], act.at[1], sx.at[12], rx.at[12], at.cp)
    loaded("m1")
    loaded("wk")
    loaded("wv")
    grad_q = wide(3, 1)
    put_grad(9, 1, gp[0], lambda cols: grad_q[:, cols])
    del waiting[9]
    sums[6] = fold(grad_q.astype(F32))
    tick()
    waiting[9] = 1
    for own, came in ((6, 0), (7, 1)):
        links.copy(W8.at[own, pl.ds(2, 2)], act.at[came], sx.at[11 + came], rx.at[11 + came], at.cp).wait_recv()

        def join(i, carry):
            a, b = i // 2, i % 2
            W8[own, a, b] = W8[own, a, b] + act[came, a, b]
            return carry

        lax.fori_loop(0, 4, join, 0)

    grad_k, grad_v = W8[6, 0:2].reshape(512, 1024), W8[7, 0:2].reshape(512, 1024)
    sums[7] = fold(grad_v.astype(F32))
    for t in range(2):
        rows = slice(2 * t, 2 * t + 2)
        br[:, 512 * t : 512 * t + 512] = (
            dot_nt(grad_q, W8[2, rows].reshape(512, 1024)) + dot_nt(grad_k, W8[4, rows].reshape(512, 1024)) + dot_nt(grad_v, W8[5, rows].reshape(512, 1024))
        )
    loaded("x0")
    loaded("x1")

    def norm1_back(i):
        rows = pl.ds(pl.multiple_of(i * RB, RB), RB)
        n, inv = norm_rows(gp[1, rows, :].astype(F32))
        up = br[rows, :]
        gn = up * n
        sums[0] = sums[0] + fold(up)
        sums[1] = sums[1] + fold(gn)
        g = up * scale_attn
        return rows, acc[rows, :] + (g - jnp.mean(g, -1, keepdims=True) - n * jnp.mean(gn * scale_attn, -1, keepdims=True)) * inv

    per = 256 // RB

    def away(i, carry):
        _, value = norm1_back(i + (1 - y) * per)
        cs[0, pl.ds(pl.multiple_of(i * RB, RB), RB), :] = value.astype(BF)
        return carry

    def here(i, carry):
        rows, value = norm1_back(i + y * per)
        br[rows, :] = value
        return carry

    lax.fori_loop(0, per, away, 0)
    links.send(cs.at[0], cs.at[1], sx.at[13], rx.at[13], at.yp)
    lax.fori_loop(0, per, here, 0)
    save(br.at[pl.ds(pl.multiple_of(y * 256, 256), 256)], o_gl.at[y])
    tick()

    def put_kv(n, own, d):
        put_grad(n, d, gp[0], lambda cols: W8[own, 0:2, :, :, :, :, cols].reshape(512, 512))

    for i in range(6):
        value = vec[6:7, :] if i == 5 else jnp.sum(sums[i], 0, keepdims=True)
        for j in range(8):
            GS[8 * i + j : 8 * i + j + 1, :] = value[:, 128 * j : 128 * j + 128]
    links.send(GS, GP, sy.at[4], ry.at[4], at.cp)
    for line, i in enumerate((6, 7, 5, 9, 10, 11, 12, 8)):
        value = jnp.sum(sums[i], 0, keepdims=True)
        for j in range(8):
            BA[8 * line + j : 8 * line + j + 1, :] = value[:, 128 * j : 128 * j + 128]
    links.send(BA, BB.at[0], sy.at[5], ry.at[5], at.cp)
    put_kv(10, 6, 0)
    links.copy(GS, GP, sy.at[4], ry.at[4], at.cp).wait_recv()
    GM[y, z, x] = (GS[...] + GP[...]).astype(BF)
    mine = GM.at[y, z, x]
    for k in (1, 2, 3):
        links.send(mine, mine, sy.at[5 + k], ry.at[5 + k], at.z_to(k))
    tick()
    put_kv(11, 7, 1)
    links.copy(BA, BB.at[0], sy.at[5], ry.at[5], at.cp).wait_recv()
    BB[5] = BA[...] + BB[0]
    links.send(BB.at[5], BB.at[1], sy.at[9], ry.at[9], at.yp)
    for k in (1, 2, 3):
        ref = GM.at[y, at.z_from(k), x]
        links.copy(ref, ref, sy.at[5 + k], ry.at[5 + k], at.z_to(k)).wait_recv()
    ref = GM.at[y, :, x]
    for k, peer in ((10, at.xp), (12, at.yp), (0, at.xyp)):
        links.send(ref, ref, sy.at[k], ry.at[k], peer)
    tick()
    links.copy(BB.at[5], BB.at[1], sy.at[9], ry.at[9], at.yp).wait_recv()
    BB[6] = BB[5] + BB[1]
    links.send(BB.at[6], BB.at[2], sy.at[11], ry.at[11], at.xp)
    for ref, k, peer in ((GM.at[y, :, 1 - x], 10, at.xp), (GM.at[1 - y, :, x], 12, at.yp), (GM.at[1 - y, :, 1 - x], 0, at.xyp)):
        links.copy(ref, ref, sy.at[k], ry.at[k], peer).wait_recv()
    links.copy(BB.at[6], BB.at[2], sy.at[11], ry.at[11], at.xp).wait_recv()
    BB[7] = BB[6] + BB[2]
    bias_in = (BB.at[3], BB.at[4], BB.at[8])
    for k in (1, 2, 3):
        links.send(BB.at[7], bias_in[k - 1], sy.at[12 + k], ry.at[12 + k], at.z_to(k))
    tick()

    for m in range(2):
        for p in range(8):
            tile = GM[m, p // 2, p % 2].astype(F32)
            for j in range(48):
                first = 256 + 16 * (j // 8) + 8 * m + p
                acc[first : first + 1, 128 * (j % 8) : 128 * (j % 8) + 128] = tile[j : j + 1, :]
    cond = cact[...].astype(BF)
    part_sum = None
    for i in range(6):
        cols = slice(1024 * i, 1024 * i + 1024)
        values = acc[256 + 16 * i : 272 + 16 * i, :]
        low = values.astype(BF)
        brow[0:1, cols] = jnp.sum(values, 0, keepdims=True)
        spread = dot_tn(cond, low)
        acc[32 * i : 32 * i + 32, :] = (spread[0:32] + spread[32:64]) + (spread[64:96] + spread[96:128])
        save(acc.at[pl.ds(32 * i, 32)], o_mod.at[:, pl.ds(1024 * i, 1024)])
        term = dot_nt(low, wm[:, cols])
        part_sum = term if part_sum is None else part_sum + term
    save(brow, o_bmod)
    GCX[0] = jnp.where(lane // 32 == at.sq, jnp.concatenate([part_sum] * 4, 1), 0.0)
    to_row = ((1, 16, at.cp), (2, 17, at.yp), (3, 1, at.ycp))
    for k, sem, peer in to_row:
        links.send(GCX.at[0], GCX.at[k], sy.at[sem], ry.at[sem], peer)
    for k in (1, 2, 3):
        links.copy(BB.at[7], bias_in[k - 1], sy.at[12 + k], ry.at[12 + k], at.z_to(k)).wait_recv()
    bsum[...] = (BB[7] + BB[3]) + (BB[4] + BB[8])
    save(bsum, o_bias)
    tick()
    for k, sem, peer in to_row:
        links.copy(GCX.at[0], GCX.at[k], sy.at[sem], ry.at[sem], peer).wait_recv()
    GC[z, x] = (GCX[0] + GCX[1]) + (GCX[2] + GCX[3])
    mine = GC.at[z, x]
    for k in (1, 2, 3):
        links.send(mine, mine, sy.at[17 + k], ry.at[17 + k], at.z_to(k))
    for k in (1, 2, 3):
        ref = GC.at[at.z_from(k), x]
        links.copy(ref, ref, sy.at[17 + k], ry.at[17 + k], at.z_to(k)).wait_recv()
    links.send(GC.at[:, x], GC.at[:, x], sy.at[21], ry.at[21], at.xp)
    links.copy(cs.at[0], cs.at[1], sx.at[13], rx.at[13], at.yp).wait_recv()

    def widen(i, carry):
        rows = pl.ds(pl.multiple_of(i * RB, RB), RB)
        br[pl.ds(pl.multiple_of((1 - y) * 256 + i * RB, RB), RB), :] = cs[1, rows, :].astype(F32)
        return carry

    lax.fori_loop(0, per, widen, 0)
    save(br.at[pl.ds(pl.multiple_of((1 - y) * 256, 256), 256)], o_gl.at[1 - y])
    while waiting:
        tick()
    links.copy(GC.at[:, 1 - x], GC.at[:, 1 - x], sy.at[21], ry.at[21], at.xp).wait_recv()
    save(GC, o_gc)
    links.copy(xs.at[1 - y], o_out.at[1 - y], sx.at[10], rx.at[10], at.yp).wait_recv()
    slot_free(0)
    slot_free(1)
    for copy in fin_saved.values():
        copy.wait()
    links.drain()
    early = [id(copy) for copy in kv_saved + [q_saved, x_saved, m1_saved, att_saved, ao_saved] + w_saved]
    for copy in outgoing:
        if id(copy) not in early:
            copy.wait()


def run_block(lat, cot, cond, b_mod, b_qv, b_out, b_up, b_down, w_mod, w_qkv, w_out, w_up, w_down):
    S = jax.ShapeDtypeStruct
    V = pltpu.VMEM
    dma = pltpu.SemaphoreType.DMA
    regular = pltpu.SemaphoreType.REGULAR
    half = (2, 2, 2, 2, 32, 1024)
    outs = [
        S((2, 256, 1024), BF), S((2, 256, 1024), F32), S((32, 3072), F32), S((32, 1024), F32), S((32, 4096), F32), S((128, 1024), F32),
        S((32, 6144), F32), S((1, 6144), F32), S((64, 128), F32), S((4, 2, 16, 128), F32),
        S((2, 4, 2, 2, 2, 32, 1024), BF), S((2, 256, 1024), BF), S((512, 1024), BF), S(half, BF), S((2,) + half, BF), S((2,) + half, BF), S(half, BF),
        S((512, 1024), BF),
    ]
    scratch = [
        V((8, 4, 2, 2, 2, 32, 1024), BF), V((4, 4, 2, 2, 2, 2, 2, 32, 256), BF), V((4, 2, 2, 2, 2, 32, 1024), BF), V((4, 4, 2, 2, 32, 1024), BF),
        *[V(shape, BF) for step in LANDING for shape in step],
        V((2,) + half, BF), V((2, 512, 1024), BF), V((512, 1024), BF), V((512, 1024), BF), V((512, 1024), F32), V((512, 1024), F32), V((512, 1024), F32),
        V((2, 256, 1024), BF), V((2, 256, 1024), BF), V((3, 32, 1024), F32), V((8, 8, 512), F32),
        V((4, 2, 2, 2, 24, 128), F32), V((2, 4, 2, 48, 128), F32), V((4, 48, 128), F32), V((2, 4, 48, 128), F32), V((3, 48, 128), F32),
        V((48, 128), F32), V((48, 128), F32), V((32, 6144), BF), V((16, 128), F32), V((8, 1024), F32), V((1, 8192), F32), V((13, 8, 1024), F32),
        V((48, 128), F32), V((48, 128), F32), V((2, 4, 2, 48, 128), BF), V((64, 128), F32), V((64, 128), F32), V((9, 64, 128), F32),
        V((4, 2, 16, 128), F32), V((4, 16, 128), F32), V((1, 6144), F32),
        dma((7, 21)), dma((12, 21)), dma((12,)), dma((12,)), dma((LR, 21)), dma((LR, 21)), dma((12,)), dma((12,)), dma((4, 2)), dma((4, 2)),
        regular((7,)), regular((4,)), regular, dma((14,)), dma((14,)), dma((22,)), dma((22,)), dma((6,)), dma((6,)),
        dma((15,)), dma((22,)), dma((22,)), dma((3,)),
    ]
    return pl.pallas_call(
        block_kernel,
        out_shape=outs,
        in_specs=[ANY, ANY, VM, VM, VM, VM, VM, VM, ANY, ANY, ANY, ANY, ANY],
        out_specs=[ANY] * len(outs),
        scratch_shapes=scratch,
        compiler_params=pltpu.CompilerParams(collective_id=0, has_side_effects=True, vmem_limit_bytes=63 * 2**20),
        cost_estimate=pl.CostEstimate(flops=6 * 10**10, bytes_accessed=10**8, transcendentals=2 * 10**7),
    )(lat, cot, cond, b_mod, b_qv, b_out, b_up, b_down, w_mod, w_qkv, w_out, w_up, w_down.reshape(2, 2, 32, 1024))[:10]


def finish_kernel(h_out, h_gl, h_qkv, h_wo, h_up, h_dn, h_mod, bmod, bias, gcond, cond, o_out, o_gl, o_cond, o_mod, o_bmod, o_qkv, o_bqv, o_wo, o_bo, o_up, o_bu, o_dn, o_bd, v_out, v_gl, v_qkv, v_wo, v_up, v_dn, v_mod, sem_in, sem_out):
    ways = (
        (h_gl, v_gl, o_gl), (h_out, v_out, o_out), (h_mod, v_mod, o_mod), (h_up, v_up, o_up), (h_dn, v_dn, o_dn), (h_qkv, v_qkv, o_qkv), (h_wo, v_wo, o_wo),
    )
    into = [pltpu.make_async_copy(src, mid, sem_in.at[i]) for i, (src, mid, _) in enumerate(ways)]
    copies = [pltpu.make_async_copy(mid, dst, sem_out.at[i]) for i, (_, mid, dst) in enumerate(ways)]
    for copy in into:
        copy.start()
    for first, then in zip(into, copies):
        first.wait()
        then.start()
    dp, sq = lax.axis_index("dp"), lax.axis_index("seq")
    index = dp * (YN * CN) + sq

    def pick(values, row):
        return jnp.sum(jnp.where(lax.broadcasted_iota(jnp.int32, values.shape, 0) == row, values, 0.0), 0, keepdims=True)

    def lanes(row, size, at_):
        total = jnp.where(at_ == 0, row[:, 0:size], 0.0)
        for k in range(1, 128 // size):
            total = jnp.where(at_ == k, row[:, size * k : size * k + size], total)
        return total

    o_bqv[...] = lanes(pick(bias[0:16, :], index // 2), 64, lax.rem(index, 2))
    o_bo[...] = lanes(pick(bias[16:24, :], index // 4), 32, lax.rem(index, 4))
    o_bu[...] = pick(bias[24:56, :], index)
    o_bd[...] = lanes(pick(bias[56:64, :], index // 4), 32, lax.rem(index, 4))
    wide = bmod[0:1, pl.ds(pl.multiple_of((index // 2) * 384 + lax.rem(index, 2) * 128, 128), 256)]
    o_bmod[...] = jnp.where(lax.rem(index, 2) == 0, wide[:, 0:192], wide[:, 64:256])
    for m in range(2):
        for p in range(8):
            v = cond[m : m + 1, 128 * p : 128 * p + 128].astype(F32)
            gate = 1.0 / (1.0 + jnp.exp(-v))
            o_cond[m : m + 1, 128 * p : 128 * p + 128] = pick(gcond[p, 8 * m : 8 * m + 8, :], dp) * (gate * (1.0 + v * (1.0 - gate)))
    for copy in copies:
        copy.wait()


def per_device_kernels(latents, conditioning, w_mod, b_mod, w_qkv, b_qv, w_out, b_out, w_up, b_up, w_down, b_down, cotangent):
    cond = conditioning[:, 0]
    output, grad_lat, g_qkv, g_out, g_up, g_down, g_mod, gb_mod, gb_all, g_cond = run_block(
        latents[:, 0], cotangent[:, 0], cond, b_mod, b_qv, b_out, b_up, b_down, w_mod[0], w_qkv[0], w_out[0], w_up[0], w_down[0]
    )
    S = jax.ShapeDtypeStruct
    shapes = [
        S((2, 256, 1024), BF), S((2, 256, 1024), F32), S((2, 1024), F32), S((32, 6144), F32), S((1, 192), F32), S((32, 3072), F32), S((1, 64), F32),
        S((32, 1024), F32), S((1, 32), F32), S((32, 4096), F32), S((1, 128), F32), S((128, 1024), F32), S((1, 32), F32),
    ]
    (out, gl, gc, mod, bmod, qkv, bqv, wo, bo, up, bu, dn, bd) = pl.pallas_call(
        finish_kernel,
        out_shape=shapes,
        in_specs=[ANY] * 7 + [VM] * 4,
        out_specs=[ANY, ANY, VM, ANY, VM, ANY, VM, ANY, VM, ANY, VM, ANY, VM],
        scratch_shapes=[pltpu.VMEM(s.shape, s.dtype) for s in (output, grad_lat, g_qkv, g_out, g_up, g_down, g_mod)]
        + [pltpu.SemaphoreType.DMA((7,)), pltpu.SemaphoreType.DMA((7,))],
        cost_estimate=pl.CostEstimate(flops=10**6, bytes_accessed=10**7, transcendentals=2048),
    )(output, grad_lat, g_qkv, g_out, g_up, g_down, g_mod, gb_mod, gb_all, g_cond.reshape(8, 16, 128), cond)
    return (out[:, None], gl[:, None], gc[:, None], mod[None], bmod, qkv[None], bqv, wo[None], bo, up[None], bu, dn[None], bd)


def solution(mesh):
    placed = (
        P(None, "dp", "seq", None),
        P(None, "dp", None),
        P(None, ("dp", "seq"), None),
        P(None, ("dp", "seq")),
        P(None, ("dp", "seq"), None),
        P(None, ("dp", "seq")),
        P(None, ("dp", "seq"), None),
        P(None, ("dp", "seq")),
        P(None, ("dp", "seq"), None),
        P(None, ("dp", "seq")),
        P(None, ("dp", "seq"), None),
        P(None, ("dp", "seq")),
        P(None, "dp", "seq", None),
    )
    return jax.shard_map(
        per_device_kernels if dict(mesh.shape) == {"dp": 8, "seq": 4} else per_device,
        mesh=mesh,
        in_specs=placed,
        out_specs=(
            P(None, "dp", "seq", None),
            P(None, "dp", "seq", None),
            P(None, "dp", None),
            P(None, ("dp", "seq"), None),
            P(None, ("dp", "seq")),
            P(None, ("dp", "seq"), None),
            P(None, ("dp", "seq")),
            P(None, ("dp", "seq"), None),
            P(None, ("dp", "seq")),
            P(None, ("dp", "seq"), None),
            P(None, ("dp", "seq")),
            P(None, ("dp", "seq"), None),
            P(None, ("dp", "seq")),
        ),
        check_vma=False,
    )
```

```python
import jax
import jax.numpy as jnp
from jax import lax
from jax.sharding import PartitionSpec as P
from jax.experimental import pallas as pl
from jax.experimental.pallas import tpu as pltpu

EPS = 1e-06
HEADS = 16


def modulate(stream, shift_vec, scale_vec):
    row_mean = jnp.mean(stream, -1, keepdims=True)
    centred = stream - row_mean
    row_var = jnp.mean(centred * centred, -1, keepdims=True)
    return centred * lax.rsqrt(row_var + EPS) * (1.0 + scale_vec) + shift_vec


def gelu_tanh(values):
    return jax.nn.gelu(values, approximate=True)


def matmul(left, right):
    return jnp.dot(left, right, preferred_element_type=jnp.float32)


def weight_grad(inputs, upstream):
    return jnp.einsum("ti,to->io", inputs, upstream, preferred_element_type=jnp.float32)


def input_grad(upstream, weight):
    return jnp.einsum("to,io->ti", upstream, weight, preferred_element_type=jnp.float32)


def column_sums(values):
    return jnp.sum(values.astype(jnp.float32), 0)


def gather_once(params, layer_index):
    return (
        lax.all_gather(params[0][layer_index], ("dp", "seq"), axis=0, tiled=True),
        lax.all_gather(params[1][layer_index], ("dp", "seq"), axis=0, tiled=True),
        lax.all_gather(params[2][layer_index], ("dp", "seq"), axis=0, tiled=True),
        lax.all_gather(params[3][layer_index], ("dp", "seq"), axis=0, tiled=True),
        lax.all_gather(params[4][layer_index], ("dp", "seq"), axis=0, tiled=True),
        lax.all_gather(params[5][layer_index], ("dp", "seq"), axis=0, tiled=True),
        lax.all_gather(params[6][layer_index], ("dp", "seq"), axis=0, tiled=True),
        lax.all_gather(params[7][layer_index], ("dp", "seq"), axis=0, tiled=True),
        lax.all_gather(params[8][layer_index], ("dp", "seq"), axis=0, tiled=True),
        lax.all_gather(params[9][layer_index], ("dp", "seq"), axis=0, tiled=True),
    )


def owner_layout(grad, dp_count, seq_count):
    per_owner = grad.shape[1] // (dp_count * seq_count)
    shaped = grad.reshape((grad.shape[0], dp_count, seq_count, per_owner) + grad.shape[2:])
    return jnp.moveaxis(shaped, 0, 2)


def attend(query, keys, values):
    head_size = query.shape[1] // HEADS
    query_rows = query.reshape(query.shape[0], HEADS, head_size)
    key_rows = keys.reshape(keys.shape[0], HEADS, head_size)
    value_rows = values.reshape(values.shape[0], HEADS, head_size)
    scores = jnp.einsum(
        "qhd,khd->hqk", query_rows, key_rows, preferred_element_type=jnp.float32
    ) * head_size ** (-0.5)
    row_max = jnp.max(scores, -1, keepdims=True)
    expon = jnp.exp(scores - row_max)
    row_sum = jnp.sum(expon, -1, keepdims=True)
    probs_low = (expon / row_sum).astype(jnp.bfloat16)
    attended = jnp.einsum("hqk,khd->qhd", probs_low, value_rows, preferred_element_type=jnp.float32)
    return (attended.reshape(query.shape[0], -1).astype(jnp.bfloat16), row_max + jnp.log(row_sum))


def attend_back(query, keys, values, log_total, grad_attended):
    head_size = query.shape[1] // HEADS
    inv_root = head_size ** (-0.5)
    query_rows = query.reshape(query.shape[0], HEADS, head_size)
    key_rows = keys.reshape(keys.shape[0], HEADS, head_size)
    value_rows = values.reshape(values.shape[0], HEADS, head_size)
    grad_rows = grad_attended.reshape(query.shape[0], HEADS, head_size)
    scores = (
        jnp.einsum("qhd,khd->hqk", query_rows, key_rows, preferred_element_type=jnp.float32)
        * inv_root
    )
    probs = jnp.exp(scores - log_total)
    grad_probs = jnp.einsum(
        "qhd,khd->hqk", grad_rows, value_rows, preferred_element_type=jnp.float32
    )
    row_dot = jnp.sum(probs * grad_probs, -1, keepdims=True)
    grad_scores = (probs * (grad_probs - row_dot)).astype(jnp.bfloat16)
    grad_query = (
        jnp.einsum("hqk,khd->qhd", grad_scores, key_rows, preferred_element_type=jnp.float32)
        * inv_root
    )
    grad_keys = (
        jnp.einsum("hqk,qhd->khd", grad_scores, query_rows, preferred_element_type=jnp.float32)
        * inv_root
    )
    grad_values = jnp.einsum(
        "hqk,qhd->khd", probs.astype(jnp.bfloat16), grad_rows, preferred_element_type=jnp.float32
    )
    return (
        grad_query.reshape(query.shape[0], -1),
        grad_keys.reshape(keys.shape[0], -1),
        grad_values.reshape(values.shape[0], -1),
    )


def forward_layer(stream, cond_act, gathered):
    w_mod, b_mod, w_qkv, b_qv, w_out, b_out, w_up, b_up, w_down, b_down = gathered
    model_width = stream.shape[1]
    modulation = matmul(cond_act, w_mod)[0] + b_mod.astype(jnp.float32)
    shift_attn, scale_attn, gate_attn, shift_mlp, scale_mlp, gate_mlp = jnp.split(modulation, 6)
    mixed1 = modulate(stream, shift_attn, scale_attn).astype(jnp.bfloat16)
    qkv = matmul(mixed1, w_qkv)
    qv_bias = b_qv.astype(jnp.float32)
    query = (qkv[:, :model_width] + qv_bias[:model_width]).astype(jnp.bfloat16)
    keys = qkv[:, model_width : 2 * model_width].astype(jnp.bfloat16)
    values = (qkv[:, 2 * model_width :] + qv_bias[model_width:]).astype(jnp.bfloat16)
    all_keys, all_values = (
        lax.all_gather(keys, "seq", axis=0, tiled=True),
        lax.all_gather(values, "seq", axis=0, tiled=True),
    )
    attended, log_total = attend(query, all_keys, all_values)
    attn_out = matmul(attended, w_out) + b_out.astype(jnp.float32)
    resid = stream + gate_attn * attn_out
    mixed2 = modulate(resid, shift_mlp, scale_mlp).astype(jnp.bfloat16)
    preact = matmul(mixed2, w_up) + b_up.astype(jnp.float32)
    activation = gelu_tanh(preact).astype(jnp.bfloat16)
    branch = matmul(activation, w_down) + b_down.astype(jnp.float32)
    saved_acts = (
        stream,
        modulation,
        query,
        all_keys,
        all_values,
        log_total,
        attended,
        attn_out,
        resid,
        preact,
        branch,
    )
    return (resid + gate_mlp * branch, saved_acts)


def backward_layer(gradient, saved_acts, gathered, cond_act):
    w_mod, b_mod, w_qkv, b_qv, w_out, b_out, w_up, b_up, w_down, b_down = gathered
    (
        stream,
        modulation,
        query,
        all_keys,
        all_values,
        log_total,
        attended,
        attn_out,
        resid,
        preact,
        branch,
    ) = saved_acts
    model_width = stream.shape[1]
    shift_attn, scale_attn, gate_attn, shift_mlp, scale_mlp, gate_mlp = jnp.split(modulation, 6)
    grad_branch = (gradient * gate_mlp).astype(jnp.bfloat16)
    grad_gate_mlp = jnp.sum(gradient * branch, 0)
    activation_f, gelu_pull = jax.vjp(gelu_tanh, preact)
    activation = activation_f.astype(jnp.bfloat16)
    grad_b_down = column_sums(grad_branch)
    grad_preact = gelu_pull(input_grad(grad_branch, w_down))[0].astype(jnp.bfloat16)
    mixed2_f, norm_pull_mlp = jax.vjp(modulate, resid, shift_mlp, scale_mlp)
    mixed2 = mixed2_f.astype(jnp.bfloat16)
    grad_b_up = column_sums(grad_preact)
    grad_resid_norm, grad_shift_mlp, grad_scale_mlp = norm_pull_mlp(input_grad(grad_preact, w_up))
    grad_resid = gradient + grad_resid_norm
    grad_attn = (grad_resid * gate_attn).astype(jnp.bfloat16)
    grad_gate_attn = jnp.sum(grad_resid * attn_out, 0)
    grad_b_out = column_sums(grad_attn)
    grad_attended = input_grad(grad_attn, w_out).astype(jnp.bfloat16)
    grad_query, grad_keys_all, grad_values_all = attend_back(
        query, all_keys, all_values, log_total, grad_attended
    )
    grad_keys, grad_values = (
        lax.psum_scatter(
            grad_keys_all.astype(jnp.bfloat16), "seq", scatter_dimension=0, tiled=True
        ).astype(jnp.float32),
        lax.psum_scatter(
            grad_values_all.astype(jnp.bfloat16), "seq", scatter_dimension=0, tiled=True
        ).astype(jnp.float32),
    )
    grad_qkv = jnp.concatenate(
        [
            grad_query.astype(jnp.bfloat16),
            grad_keys.astype(jnp.bfloat16),
            grad_values.astype(jnp.bfloat16),
        ],
        1,
    )
    mixed1_f, norm_pull_attn = jax.vjp(modulate, stream, shift_attn, scale_attn)
    mixed1 = mixed1_f.astype(jnp.bfloat16)
    qkv_sums = column_sums(grad_qkv)
    grad_b_qv = jnp.concatenate([qkv_sums[:model_width], qkv_sums[2 * model_width :]])
    grad_stream_norm, grad_shift_attn, grad_scale_attn = norm_pull_attn(input_grad(grad_qkv, w_qkv))
    grad_stream = grad_resid + grad_stream_norm
    grad_mod_part = jnp.concatenate(
        [
            grad_shift_attn,
            grad_scale_attn,
            grad_gate_attn,
            grad_shift_mlp,
            grad_scale_mlp,
            grad_gate_mlp,
        ]
    )
    grad_mod = lax.psum(grad_mod_part, "seq").astype(jnp.bfloat16)
    seq_share = 1.0 / lax.axis_size("seq")
    grad_b_mod = grad_mod.astype(jnp.float32) * seq_share
    grad_cond_act = input_grad(grad_mod[None], w_mod)
    operands = (
        activation,
        grad_branch,
        mixed2,
        grad_preact,
        attended,
        grad_attn,
        mixed1,
        grad_qkv,
        cond_act,
        grad_mod[None],
    )
    bias_terms = (grad_b_mod, grad_b_qv, grad_b_out, grad_b_up, grad_b_down)
    return (grad_stream, grad_cond_act, operands, bias_terms)


def per_device(
    latents,
    conditioning,
    w_mod,
    b_mod,
    w_qkv,
    b_qv,
    w_out,
    b_out,
    w_up,
    b_up,
    w_down,
    b_down,
    cotangent,
):
    params = (w_mod, b_mod, w_qkv, b_qv, w_out, b_out, w_up, b_up, w_down, b_down)
    layer_count = w_mod.shape[0]
    micro_count = latents.shape[0]
    seq_share = 1.0 / lax.axis_size("seq")
    stored = [gather_once(params, 0)]
    kept_operands = [[]]
    bias_totals = [None] * layer_count
    outputs = []
    grads_in = []
    grads_cond = []
    for micro_step in range(micro_count):
        stream = latents[micro_step, 0].astype(jnp.float32)
        cond_row = conditioning[micro_step, 0:1].astype(jnp.float32)
        cond_act = jax.nn.silu(cond_row).astype(jnp.bfloat16)
        layer_index = 0
        gathered = stored[layer_index]
        stream, saved_acts = forward_layer(stream, cond_act, gathered)
        saved_list = [saved_acts]
        outputs.append(stream.astype(jnp.bfloat16))
        gradient = cotangent[micro_step, 0].astype(jnp.float32)
        grad_cond_act = jnp.zeros(cond_row.shape, jnp.float32)
        for layer_index in reversed(range(layer_count)):
            gathered = stored[layer_index]
            gradient, grad_cond_part, operands, bias_terms = backward_layer(
                gradient, saved_list[layer_index], gathered, cond_act
            )
            grad_cond_act = grad_cond_part
            kept_operands[layer_index].append(operands)
            if bias_totals[layer_index] is None:
                bias_totals[layer_index] = bias_terms
            else:
                bias_totals[layer_index] = tuple(
                    (first + second for first, second in zip(bias_totals[layer_index], bias_terms))
                )
        grads_in.append(gradient)
        silu_pull = jax.vjp(jax.nn.silu, cond_row)[1]
        grads_cond.append(silu_pull(grad_cond_act)[0])
    layer_index = 0
    joined = [
        jnp.concatenate(
            [kept_operands[layer_index][step][member] for step in range(micro_count)], 0
        )
        for member in range(10)
    ]
    grad_w_down = weight_grad(joined[0], joined[1])
    grad_w_up = weight_grad(joined[2], joined[3])
    grad_w_out = weight_grad(joined[4], joined[5])
    grad_w_qkv = weight_grad(joined[6], joined[7])
    grad_w_mod = weight_grad(joined[8], joined[9]) * seq_share
    grad_b_mod, grad_b_qv, grad_b_out, grad_b_up, grad_b_down = bias_totals[layer_index]
    totals = (
        grad_w_mod,
        grad_b_mod,
        grad_w_qkv,
        grad_b_qv,
        grad_w_out,
        grad_b_out,
        grad_w_up,
        grad_b_up,
        grad_w_down,
        grad_b_down,
    )
    dp_count = lax.axis_size("dp")
    seq_count = lax.axis_size("seq")
    stacked = [
        owner_layout(jnp.stack([totals[member]]), dp_count, seq_count) for member in range(10)
    ]
    flat = [member.reshape((dp_count * seq_count,) + member.shape[2:]) for member in stacked]
    owned = (
        lax.psum_scatter(flat[0], ("dp", "seq"), scatter_dimension=0, tiled=True),
        lax.psum_scatter(flat[1], ("dp", "seq"), scatter_dimension=0, tiled=True),
        lax.psum_scatter(flat[2], ("dp", "seq"), scatter_dimension=0, tiled=True),
        lax.psum_scatter(flat[3], ("dp", "seq"), scatter_dimension=0, tiled=True),
        lax.psum_scatter(flat[4], ("dp", "seq"), scatter_dimension=0, tiled=True),
        lax.psum_scatter(flat[5], ("dp", "seq"), scatter_dimension=0, tiled=True),
        lax.psum_scatter(flat[6], ("dp", "seq"), scatter_dimension=0, tiled=True),
        lax.psum_scatter(flat[7], ("dp", "seq"), scatter_dimension=0, tiled=True),
        lax.psum_scatter(flat[8], ("dp", "seq"), scatter_dimension=0, tiled=True),
        lax.psum_scatter(flat[9], ("dp", "seq"), scatter_dimension=0, tiled=True),
    )
    shards = [
        member.reshape(member.shape[member.ndim - stacked_member.ndim + 2 :])
        for member, stacked_member in zip(owned, stacked)
    ]
    output = jnp.stack(outputs)[:, None]
    grad_latents = jnp.stack(grads_in)[:, None]
    grad_cond = jnp.stack(grads_cond)
    return (
        output,
        grad_latents,
        grad_cond,
        shards[0],
        shards[1],
        shards[2],
        shards[3],
        shards[4],
        shards[5],
        shards[6],
        shards[7],
        shards[8],
        shards[9],
    )


MESH_IDS = pl.DeviceIdType.MESH
ANY = pl.BlockSpec(memory_space=pl.ANY)
VM = pl.BlockSpec(memory_space=pltpu.VMEM)
F32, BF = jnp.float32, jnp.bfloat16
ALL = slice(None)
ZN, XN, YN, CN = 4, 2, 2, 2
TOK = 512
CUT = 512
ROOT_2_PI = 0.7978845608028654


def dot_nn(left, right):
    return lax.dot_general(left, right, (((1,), (0,)), ((), ())), preferred_element_type=F32)


def dot_nt(left, right):
    return lax.dot_general(left, right, (((1,), (1,)), ((), ())), preferred_element_type=F32)


def dot_tn(left, right):
    return lax.dot_general(left, right, (((0,), (0,)), ((), ())), preferred_element_type=F32)


class Place:
    def __init__(self):
        dp, sq = lax.axis_index("dp"), lax.axis_index("seq")
        self.dp, self.sq = dp, sq
        self.z, self.x = dp // XN, dp % XN
        self.y, self.c = sq // CN, sq % CN
        self.xp = (self.z * XN + 1 - self.x, sq)
        self.yp = (dp, (1 - self.y) * CN + self.c)
        self.cp = (dp, self.y * CN + 1 - self.c)
        self.xyp = (self.xp[0], self.yp[1])
        self.ycp = (dp, (1 - self.y) * CN + 1 - self.c)

    def z_to(self, k):
        return (lax.rem(self.z + k, ZN) * XN + self.x, self.sq)

    def z_at(self, z):
        return (z * XN + self.x, self.sq)

    def z_from(self, k):
        return lax.rem(self.z + ZN - k, ZN)

    def barrier(self):
        sem = pltpu.get_barrier_semaphore()
        peers = [self.z_to(1), self.z_to(2), self.z_to(3), self.xp, self.yp, self.cp, self.xyp, self.ycp]
        for peer in peers:
            pl.semaphore_signal(sem, inc=1, device_id=peer, device_id_type=MESH_IDS)
        pl.semaphore_wait(sem, len(peers))


class Links:
    def __init__(self):
        self.sent = []

    def copy(self, src, dst, send_sem, recv_sem, peer):
        return pltpu.make_async_remote_copy(
            src_ref=src, dst_ref=dst, send_sem=send_sem, recv_sem=recv_sem, device_id=peer, device_id_type=MESH_IDS
        )

    def send(self, src, dst, send_sem, recv_sem, peer, when=None):
        copy = self.copy(src, dst, send_sem, recv_sem, peer)
        guarded(when, copy.start)
        self.sent.append((copy, when))

    def drain(self):
        for copy, when in self.sent:
            guarded(when, copy.wait_send)
        self.sent = []


def pieces_of(rows, cols):
    if rows == 32:
        return (
            ("zyx", (pl.ds(0, 16), pl.ds(0, cols))),
            ("zxy", (pl.ds(16, 16), pl.ds(0, CUT))),
            ("yxz", (pl.ds(16, 16), pl.ds(CUT, cols - CUT))),
        )
    return (("zyx", (0,)), ("zxy", (1, 0)), ("yxz", (1, 1)))


def line_gather(at, idx_of):
    z = at.z
    inner, outer = (z == 1) | (z == 2), (z == 0) | (z == 3)
    near = jnp.where(z == 1, 0, 3)
    return (
        [
            (idx_of(z), at.z_at(jnp.minimum(z + 1, 3)), idx_of(jnp.maximum(z - 1, 0)), z < 3, z > 0),
            (idx_of(z), at.z_at(jnp.maximum(z - 1, 0)), idx_of(jnp.minimum(z + 1, 3)), z > 0, z < 3),
        ],
        [
            (idx_of(3 - z), at.z_at(near), idx_of(jnp.where(z == 0, 2, 1)), inner, outer),
            (idx_of(near), at.z_at(jnp.where(z == 1, 2, 1)), idx_of(jnp.where(z == 2, 0, 3)), inner, inner),
            (idx_of(near), at.z_at(3 - near), idx_of(jnp.where(z == 3, 0, 3)), inner, outer),
        ],
    )


def gather_steps(at, kind):
    z, x, y, c = at.z, at.x, at.y, at.c
    if kind == "yxz":
        return (
            [((z, x, y, c), at.yp, (z, x, 1 - y, c), None, None)],
            [((z, x, ALL, c), at.xp, (z, 1 - x, ALL, c), None, None)],
            *line_gather(at, lambda q: (q, ALL, ALL, c)),
        )
    first = line_gather(at, lambda q: (q, x, y, c))
    if kind == "zyx":
        return (
            *first,
            [((ALL, x, y, c), at.yp, (ALL, x, 1 - y, c), None, None)],
            [((ALL, x, ALL, c), at.xp, (ALL, 1 - x, ALL, c), None, None)],
        )
    return (
        *first,
        [((ALL, x, y, c), at.xp, (ALL, 1 - x, y, c), None, None)],
        [((ALL, ALL, y, c), at.yp, (ALL, ALL, 1 - y, c), None, None)],
    )


def line_scatter(at):
    z = at.z
    inner, outer = (z == 1) | (z == 2), (z == 0) | (z == 3)
    return (
        [
            (jnp.where(z == 0, 2, 1), jnp.where(z == 0, 1, 2), 0, outer, inner),
            (jnp.where(z == 2, 0, 3), 3 - z, 1, inner, inner),
            (3 - z, jnp.where(z == 0, 2, 1), 2, outer, inner),
        ],
        [(jnp.minimum(z + 1, 3), jnp.minimum(z + 1, 3), 0, z < 3, z > 0), (jnp.maximum(z - 1, 0), jnp.maximum(z - 1, 0), 1, z > 0, z < 3)],
    )


def guarded(condition, action):
    if condition is None:
        action()
    else:
        pl.when(condition)(action)


def norm_rows(values):
    centred = values - jnp.mean(values, -1, keepdims=True)
    inv = lax.rsqrt(jnp.mean(centred * centred, -1, keepdims=True) + EPS)
    return centred * inv, inv


def scatter_steps(at):
    z, x, y = at.z, at.x, at.y

    def line(piece, number, block):
        return [(piece, block(q), at.z_at(to), slot, sends, receives) for q, to, slot, sends, receives in line_scatter(at)[number]]

    def ends(q):
        return (q, x, y)

    return (
        [(0, (ALL, 1 - x, ALL), at.xp, None, None, None), (1, (ALL, ALL, 1 - y), at.yp, None, None, None)] + line(2, 0, lambda q: (q, ALL, ALL)),
        [(0, (ALL, x, 1 - y), at.yp, None, None, None), (1, (ALL, 1 - x, y), at.xp, None, None, None)] + line(2, 1, lambda q: (q, ALL, ALL)),
        line(0, 0, ends) + line(1, 0, ends) + [(2, (z, 1 - x, ALL), at.xp, None, None, None)],
        line(0, 1, ends) + line(1, 1, ends) + [(2, (z, x, 1 - y), at.yp, None, None, None)],
    )


LR = 5
PIECE_ROWS = (slice(0, 16), slice(16, 32), slice(16, 32))
PIECE_COLS = (slice(0, 1024), slice(0, CUT), slice(CUT, 1024))
LANDING = (
    ((LR, 4, 2, 16, 1024), (LR, 4, 2, 16, CUT), (LR, 3, 2, 2, 16, 1024 - CUT)),
    ((LR, 4, 16, 1024), (LR, 4, 16, CUT), (LR, 2, 2, 2, 16, 1024 - CUT)),
    ((LR, 3, 16, 1024), (LR, 3, 16, CUT), (LR, 2, 16, 1024 - CUT)),
    ((LR, 2, 16, 1024), (LR, 2, 16, CUT), (LR, 16, 1024 - CUT)),
)


RB = 128


def block_kernel(
    lat, cot, cond_in, b_mod, b_qv, b_out, b_up, b_down, w_mod, w_qkv, w_out, w_up, w_down,
    o_out, o_gl, o_qkv, o_wo, o_up, o_dn, o_mod, o_bmod, o_bias, o_gc, t_w, t_x, t_m1, t_q, t_k, t_v, t_att, t_ao,
    W8, WD, CR, RC, L00, L01, L02, L10, L11, L12, L20, L21, L22, L30, L31, L32,
    act, gp, m2, gb, res, acc, br, cs, xs, fin, lse,
    SM, PM, PY, PX, PZ, FM, PC, wm, cact, vec, bias, sums, GS, GP, GM, bsum, BA, BB, GC, GCX, brow,
    gs, gr, gcs, gcr, rss, rsr, rcs, rcr, dcs, dcr, credit, credit_c, ready_c, sx, rx, sy, ry, ssm, rsm, lw, lo, ld, lf,
):
    at = Place()
    z, x, y, c = at.z, at.x, at.y, at.c
    links = Links()
    lane = lax.broadcasted_iota(jnp.int32, (1, 128), 1)
    inner = (z == 1) | (z == 2)
    near = jnp.where(z == 1, 0, 3)

    outgoing = []

    def save(src, dst):
        copy = pltpu.make_async_copy(src, dst, lo.at[len(outgoing)])
        copy.start()
        outgoing.append(copy)
        return copy

    loads = {}

    def load(name, src, dst):
        copy = pltpu.make_async_copy(src, dst, ld.at[len(loads)])
        copy.start()
        loads[name] = copy

    def loaded(name):
        loads[name].wait()

    ORDER = (0, 1, 2, 3, 8, 9, 10, 11, 4, 5, 6, 7)
    plans = {kind: gather_steps(at, kind) for kind in ("zyx", "zxy", "yxz")}

    def block(unit, idx, part=()):
        ref = W8.at[unit] if unit < 8 else WD.at[unit - 8]
        return ref.at[idx + part]

    def shard(unit):
        if unit < 3:
            return w_qkv.at[:, pl.ds((1024, 2048, 0)[unit], 1024)]
        if unit == 3:
            return w_out
        if unit < 8:
            return w_up.at[:, pl.ds((unit - 4) * 1024, 1024)]
        return w_down.at[:, :, :, pl.ds((unit - 8) * 256, 256)]

    def pieces(unit):
        return pieces_of(32, 1024) if unit < 8 else pieces_of(128, 256)

    gather_sent = {unit: [] for unit in range(12)}
    steps_at = {}
    for i, (kind, _) in enumerate(pieces(0)):
        for number in range(4):
            for j in range(len(plans[kind][number])):
                steps_at[number, i, j] = len(steps_at)

    def gather_sems(unit, number, i, j):
        k = steps_at[number, i, j]
        return gs.at[ORDER.index(unit) % 7, k], gr.at[ORDER.index(unit) % 7, k]

    def step(unit, number):
        for i, (kind, part) in enumerate(pieces(unit)):
            for j, (idx, peer, _, sends, _) in enumerate(plans[kind][number]):
                ref = block(unit, idx, part)
                copy = links.copy(ref, ref, *gather_sems(unit, number, i, j), peer)
                guarded(sends, copy.start)
                gather_sent[unit].append((copy, sends))

    def arrived(unit, number):
        for i, (kind, part) in enumerate(pieces(unit)):
            for j, (_, peer, idx, _, receives) in enumerate(plans[kind][number]):
                ref = block(unit, idx, part)
                guarded(receives, links.copy(ref, ref, *gather_sems(unit, number, i, j), peer).wait_recv)

    local_w = [pltpu.make_async_copy(shard(u), block(u, (z, x, y, c)), lw.at[u]) for u in range(12)]

    def gather_stage(unit, number):
        if number == 0:
            if ORDER.index(unit) >= 7:
                gather_done(ORDER[ORDER.index(unit) - 7])
            local_w[unit].wait()
        else:
            arrived(unit, number - 1)
        if number < 4:
            step(unit, number)
        else:
            ref = block(unit, (ALL, ALL, ALL, c))
            copy = links.copy(ref, ref, gcs.at[unit], gcr.at[unit], at.cp)
            copy.start()
            gather_sent[unit].append((copy, None))

    def ready(unit):
        ref = block(unit, (ALL, ALL, ALL, 1 - c))
        links.copy(ref, ref, gcs.at[unit], gcr.at[unit], at.cp).wait_recv()

    def gather_tick(t):
        for number in (1, 2, 3):
            if 0 <= t + 1 - number < 12:
                gather_stage(ORDER[t + 1 - number], number)
        if t + 3 < 12:
            gather_stage(ORDER[t + 3], 0)
        if 0 <= t - 3 < 12:
            gather_stage(ORDER[t - 3], 4)

    def gather_done(unit):
        for copy, sends in gather_sent.pop(unit, ()):
            guarded(sends, copy.wait_send)

    scatter_plan = scatter_steps(at)
    landing = ((L00, L01, L02), (L10, L11, L12), (L20, L21, L22), (L30, L31, L32))
    unit_sent = [[] for _ in range(12)]
    finished = set()

    def at_block(n, idx):
        if 4 <= n < 8:
            return CR, idx + ((n - 4) // 2, (n - 4) % 2)
        return RC, (n % 4 if n < 4 else n - 8,) + idx

    def part_ref(n, idx, piece):
        ref, full = at_block(n, idx)
        return ref.at[full + (PIECE_ROWS[piece], PIECE_COLS[piece])]

    def copies(n, number):
        result = []
        for i, (piece, go, peer, slot, sends, receives) in enumerate(scatter_plan[number]):
            dst = landing[number][piece].at[n % LR]
            dst = dst if slot is None else dst.at[slot]
            k = (0, 5, 9, 16)[number] + i
            result.append((links.copy(part_ref(n, go, piece), dst, rss.at[n % LR, k], rsr.at[n % LR, k], peer), sends, receives))
        return result

    def send_step(n, number):
        for copy, sends, _ in copies(n, number):
            guarded(sends, copy.start)
            unit_sent[n].append((copy, sends))

    def add_into(n, number):
        for copy, _, receives in copies(n, number):
            guarded(receives, copy.wait_recv)
        s = n % LR

        def plus(idx, piece, *came):
            ref, full = at_block(n, idx)
            full = full + (PIECE_ROWS[piece], PIECE_COLS[piece])
            if len(came) == 1:
                ref[full] = ref[full] + came[0]
            else:
                ref[full] = (ref[full].astype(F32) + (came[0].astype(F32) + came[1].astype(F32))).astype(BF)

        if number == 0:
            def add(i, carry):
                for e in range(2):
                    plus((i, x, e), 0, L00[s, i, e])
                    plus((i, e, y), 1, L01[s, i, e])
                return carry

            lax.fori_loop(0, 4, add, 0)

            @pl.when(inner)
            def _():
                def add_line(i, carry):
                    xi, yi = i // 2, i % 2
                    plus((3 - z, xi, yi), 2, L02[s, 0, xi, yi])
                    plus((near, xi, yi), 2, L02[s, 1, xi, yi], L02[s, 2, xi, yi])
                    return carry

                lax.fori_loop(0, 4, add_line, 0)
        elif number == 1:
            def add(i, carry):
                plus((i, x, y), 0, L10[s, i])
                plus((i, x, y), 1, L11[s, i])
                return carry

            lax.fori_loop(0, 4, add, 0)
            for slot_in, came in ((0, z > 0), (1, z < 3)):
                @pl.when(came)
                def _():
                    def add_line(i, carry):
                        xi, yi = i // 2, i % 2
                        plus((z, xi, yi), 2, L12[s, slot_in, xi, yi])
                        return carry

                    lax.fori_loop(0, 4, add_line, 0)
        elif number == 2:
            @pl.when(inner)
            def _():
                for piece, ref in ((0, L20), (1, L21)):
                    plus((3 - z, x, y), piece, ref[s, 0])
                    plus((near, x, y), piece, ref[s, 1], ref[s, 2])

            for e in range(2):
                plus((z, x, e), 2, L22[s, e])

    cores_sent = {}

    def core_copy(n, d):
        return links.copy(W8.at[d, :, :, :, 1 - c], RC.at[n % 4 if n < 4 else n - 8], rcs.at[n], rcr.at[n], at.cp)

    def slot_free(d):
        for copy in cores_sent.pop(d, ()):
            copy.wait_send()

    def put_grad(n, d, left, right):
        slot_free(d)
        for t in range(2):
            cols = slice(512 * t, 512 * t + 512)
            W8[d, :, :, :, :, :, cols] = dot_tn(left, right(cols)).astype(BF).reshape(4, 2, 2, 2, 32, 512)
        if n >= 8:
            assert n - 8 in finished
            pl.semaphore_wait(credit_c.at[n - 8], 1)
        copy = core_copy(n, d)
        copy.start()
        cores_sent[d] = (copy,)
        slot_of_unit[n] = d
        if n != 8:
            waiting[n] = 1

    slot_of_unit = {}

    def r1(n):
        if not 4 <= n < 8:
            d = slot_of_unit[n]
            core_copy(n, d).wait_recv()
            slot = n % 4 if n < 4 else n - 8

            def add(i, carry):
                zi, xi, yi = i // 4, (i // 2) % 2, i % 2
                RC[slot, zi, xi, yi] = RC[slot, zi, xi, yi] + W8[d, zi, xi, yi, c]
                return carry

            lax.fori_loop(0, 16, add, 0)
        if n >= LR:
            assert n - LR in finished
            pl.semaphore_wait(credit.at[n - LR], 5)
        send_step(n, 0)

    def middle(number):
        def run(n):
            add_into(n, number)
            send_step(n, number + 1)

        return run

    fin_saved = {}

    def r5(n):
        for copy, _, receives in copies(n, 3):
            guarded(receives, copy.wait_recv)
        s, f = n % LR, n % 3
        if n - 3 in fin_saved:
            fin_saved.pop(n - 3).wait()
        ref_, full = at_block(n, (z, x, y))
        for piece, ref in ((0, L30), (1, L31)):
            rows, cols = PIECE_ROWS[piece], PIECE_COLS[piece]
            fin[f, rows, cols] = ref_[full + (rows, cols)].astype(F32)
            for slot_in, came in ((0, z > 0), (1, z < 3)):
                @pl.when(came)
                def _():
                    fin[f, rows, cols] = fin[f, rows, cols] + ref[s, slot_in].astype(F32)
        fin[f, 16:32, CUT:] = ref_[full + (slice(16, 32), slice(CUT, 1024))].astype(F32) + L32[s].astype(F32)
        if n < 4:
            dst = o_up.at[:, pl.ds(1024 * n, 1024)]
        elif n < 8:
            dst = o_dn.at[pl.ds(32 * (n - 4), 32)]
        elif n == 8:
            dst = o_wo
        else:
            dst = o_qkv.at[:, pl.ds(1024 * (n - 9), 1024)]
        fin_saved[n] = pltpu.make_async_copy(fin.at[f], dst, lf.at[f])
        fin_saved[n].start()
        for copy, sends in unit_sent[n]:
            guarded(sends, copy.wait_send)
        if n + LR < 12:
            for peer in (at.z_to(1), at.z_to(2), at.z_to(3), at.xp, at.yp):
                pl.semaphore_signal(credit.at[n], inc=1, device_id=peer, device_id_type=MESH_IDS)
        if n < 4:
            pl.semaphore_signal(credit_c.at[n], inc=1, device_id=at.cp, device_id_type=MESH_IDS)
        finished.add(n)

    stages = {1: r1, 2: middle(0), 3: middle(1), 4: middle(2), 5: r5}
    waiting = {}

    def tick():
        for n in sorted(waiting, reverse=True):
            stages[waiting[n]](n)
            waiting[n] += 1
            if waiting[n] == 6:
                del waiting[n]

    def fold(values):
        return jnp.sum(values.reshape(-1, 8, values.shape[-1]), 0)

    local_m = pltpu.make_async_copy(w_mod, wm, lw.at[12])
    local_x = pltpu.make_async_copy(lat.at[y], xs.at[y], lw.at[13])
    local_c = pltpu.make_async_copy(cot.at[y], cs.at[y], lw.at[14])
    for copy in local_w[:3] + [local_m, local_x] + local_w[3:] + [local_c]:
        copy.start()
    index = at.dp * (YN * CN) + at.sq

    def table(line, value):
        SM[z, x, y, c, line : line + 1, :] = value

    rows_in = cond_in[...].astype(F32)
    for m in range(2):
        for j in range(8):
            table(8 * m + j, rows_in[m : m + 1, 128 * j : 128 * j + 128])
    for line, ref in ((16, b_qv), (17, b_out), (18, b_up), (19, b_down)):
        size = ref.shape[1]
        wide = jnp.concatenate([ref[...].astype(F32)] * (128 // size), 1) if size < 128 else ref[...].astype(F32)
        table(line, jnp.where(lane // size == lax.rem(index, 128 // size), wide, 0.0))
    bm = b_mod[...].astype(F32)
    none = jnp.zeros((1, 64), F32)
    even = lax.rem(index, 2) == 0
    table(20, jnp.where(even, bm[:, :128], jnp.concatenate([none, bm[:, :64]], 1)))
    table(21, jnp.where(even, jnp.concatenate([bm[:, 128:], none], 1), bm[:, 64:]))
    at.barrier()

    def small_send(idx, peer, n):
        links.send(SM.at[idx], SM.at[idx], ssm.at[n], rsm.at[n], peer)

    def small_wait(idx, n):
        links.copy(SM.at[idx], SM.at[idx], ssm.at[n], rsm.at[n], at.xp).wait_recv()

    for k in (1, 2, 3):
        small_send((z, x, y, c), at.z_to(k), k - 1)
    gather_stage(ORDER[0], 0)
    links.send(lat.at[1 - y], xs.at[y], sx.at[0], rx.at[0], at.yp)
    gather_stage(ORDER[1], 0)
    for k in (1, 2, 3):
        small_wait((at.z_from(k), x, y, c), k - 1)
    small_send((ALL, x, y, c), at.xp, 3)
    gather_stage(ORDER[2], 0)
    gather_tick(0)
    small_wait((ALL, 1 - x, y, c), 3)
    small_send((ALL, ALL, y, c), at.yp, 4)

    row = lax.broadcasted_iota(jnp.int32, (8, 128), 0)
    for m in range(2):
        for p in range(8):
            tile = SM[p // 2, p % 2, y, c, 8 * m : 8 * m + 8, :]
            cact[8 * m + p : 8 * m + p + 1, :] = jnp.sum(jnp.where(row == at.dp, tile, 0.0), 0, keepdims=True)
    cond = cact[...]
    cond = jnp.where(lane // 32 == at.sq, cond / (1.0 + jnp.exp(-cond)), 0.0)
    cact[...] = cond
    cond_low = ((cond[:, 0:32] + cond[:, 32:64]) + (cond[:, 64:96] + cond[:, 96:128])).astype(BF)
    local_m.wait()
    for i in range(6):
        part = dot_nn(cond_low, wm[:, 1024 * i : 1024 * i + 1024])
        for m in range(2):
            for p in range(8):
                for j in range(8):
                    PM[m, p // 2, p % 2, 8 * i + j : 8 * i + j + 1, :] = part[8 * m + p : 8 * m + p + 1, 128 * j : 128 * j + 128]
    links.send(PM.at[:, :, 1 - x], PX, sx.at[1], rx.at[1], at.xp)
    gather_tick(1)
    links.copy(PM.at[:, :, 1 - x], PX, sx.at[1], rx.at[1], at.xp).wait_recv()
    for m in range(2):
        PM[m, :, x] = PM[m, :, x] + PX[m]
    links.send(PM.at[1 - y, :, x], PY, sx.at[2], rx.at[2], at.yp)
    small_wait((ALL, ALL, 1 - y, c), 4)
    small_send((ALL, ALL, ALL, c), at.cp, 5)
    gather_tick(2)
    links.copy(PM.at[1 - y, :, x], PY, sx.at[2], rx.at[2], at.yp).wait_recv()
    PM[y, :, x] = PM[y, :, x] + PY[...]
    for k in (1, 2, 3):
        to = lax.rem(z + k, ZN)
        links.send(PM.at[y, to, x], PZ.at[k - 1], sx.at[2 + k], rx.at[2 + k], at.z_to(k))
    gather_tick(3)
    for k in (1, 2, 3):
        links.copy(PM.at[y, z, x], PZ.at[k - 1], sx.at[2 + k], rx.at[2 + k], at.z_to(k)).wait_recv()
    FM[...] = PM[y, z, x] + PZ[0] + PZ[1] + PZ[2]
    links.send(FM, PC, sx.at[6], rx.at[6], at.cp)
    small_wait((ALL, ALL, ALL, 1 - c), 5)

    def entry(device, line):
        return SM[device // 8, (device // 4) % 2, (device // 2) % 2, device % 2, line : line + 1, :]

    for t in range(16):
        bias[0:1, 128 * t : 128 * t + 128] = entry(2 * t, 16) + entry(2 * t + 1, 16)
    for t in range(8):
        bias[0:1, 2048 + 128 * t : 2176 + 128 * t] = (entry(4 * t, 17) + entry(4 * t + 1, 17)) + (entry(4 * t + 2, 17) + entry(4 * t + 3, 17))
        bias[0:1, 7168 + 128 * t : 7296 + 128 * t] = (entry(4 * t, 19) + entry(4 * t + 1, 19)) + (entry(4 * t + 2, 19) + entry(4 * t + 3, 19))
    for t in range(32):
        bias[0:1, 3072 + 128 * t : 3200 + 128 * t] = entry(t, 18)
    links.copy(FM, PC, sx.at[6], rx.at[6], at.cp).wait_recv()
    for j in range(48):
        k, third = j // 3, j % 3
        if third == 0:
            b_row = entry(2 * k, 20)
        elif third == 1:
            b_row = entry(2 * k, 21) + entry(2 * k + 1, 20)
        else:
            b_row = entry(2 * k + 1, 21)
        vec[j // 8 : j // 8 + 1, 128 * (j % 8) : 128 * (j % 8) + 128] = FM[j : j + 1, :] + PC[j : j + 1, :] + b_row
    shift_attn, scale_attn, gate_attn = vec[0:1, :], 1.0 + vec[1:2, :], vec[2:3, :]
    shift_mlp, scale_mlp, gate_mlp = vec[3:4, :], 1.0 + vec[4:5, :], vec[5:6, :]

    local_x.wait()
    links.copy(lat.at[1 - y], xs.at[1 - y], sx.at[0], rx.at[0], at.yp).wait_recv()

    def halves(i):
        return i // (256 // RB), pl.ds(pl.multiple_of((i % (256 // RB)) * RB, RB), RB)

    def norm1(i, carry):
        half, rows = halves(i)
        n, _ = norm_rows(xs[half, rows, :].astype(F32))
        gp[0, pl.ds(pl.multiple_of(i * RB, RB), RB), :] = (n * scale_attn + shift_attn).astype(BF)
        return carry

    lax.fori_loop(0, TOK // RB, norm1, 0)
    x_saved = save(xs, t_x)
    m1_saved = save(gp.at[0], t_m1)
    gather_tick(4)

    def weight(unit, cols):
        return W8[unit, :, :, :, :, :, cols].reshape(1024, -1)

    def project(unit, put):
        for t in range(2):
            cols = slice(512 * t, 512 * t + 512)
            put(cols, dot_nn(gp[0], weight(unit, cols)))

    def rows512(value):
        return value.astype(BF).reshape(2, 2, 2, 2, 32, -1)

    def put_k(cols, value):
        CR[0, :, :, :, :, :, cols] = rows512(value)

    def put_v(cols, value):
        CR[2, :, :, :, :, :, cols] = rows512(value + bias[0:1, 1024 + cols.start : 1024 + cols.stop])

    def put_q(cols, value):
        act[0, :, :, :, :, :, cols] = rows512(value + bias[0:1, cols])

    ready(0)
    w_saved = [save(W8.at[0], t_w.at[0])]
    project(0, put_k)
    k_sent = links.copy(CR.at[0], CR.at[1], sx.at[8], rx.at[8], at.cp)
    k_sent.start()
    gather_tick(5)
    ready(1)
    w_saved.append(save(W8.at[1], t_w.at[1]))
    project(1, put_v)
    v_sent = links.copy(CR.at[2], CR.at[3], sx.at[9], rx.at[9], at.cp)
    v_sent.start()
    gather_tick(6)
    ready(2)
    links.send(cot.at[1 - y], cs.at[y], sx.at[7], rx.at[7], at.yp)
    project(2, put_q)
    q_saved = save(act.at[0], t_q)
    k_sent.wait_recv()
    v_sent.wait_recv()
    kv_saved = [save(CR.at[pl.ds(0, 2)], t_k), save(CR.at[pl.ds(2, 2)], t_v)]

    def attend_pair(p, carry):
        cols = pl.ds(pl.multiple_of(p * 128, 128), 128)
        k2, v2 = CR[0:2, :, :, :, :, :, cols].reshape(1024, 128), CR[2:4, :, :, :, :, :, cols].reshape(1024, 128)
        for t in range(2):
            rows = slice(256 * t, 256 * t + 256)
            q2 = act[0, t, :, :, :, :, cols].reshape(256, 128)
            parts = []
            for e in range(2):
                own = (lane < 64) == (e == 0)
                qe = jnp.where(own, q2, jnp.zeros_like(q2)) * BF(0.125)
                scores = dot_nt(qe, k2)
                top = jnp.max(scores, 1, keepdims=True)
                expon = jnp.exp(scores - top)
                total = jnp.sum(expon, 1, keepdims=True)
                parts.append(dot_nn((expon * (1.0 / total)).astype(BF), v2))
                log_total = jnp.broadcast_to(top + jnp.log(total), (256, 128)).T
                lse[p, e : e + 1, rows] = log_total[0:1, :]
            act[1, t, :, :, :, :, cols] = jnp.where(lane < 64, parts[0], parts[1]).astype(BF).reshape(2, 2, 2, 32, 128)
        return carry

    lax.fori_loop(0, 2, attend_pair, 0)
    gather_tick(7)
    lax.fori_loop(2, 4, attend_pair, 0)
    gather_tick(8)
    lax.fori_loop(4, 6, attend_pair, 0)
    gather_tick(9)
    lax.fori_loop(6, 8, attend_pair, 0)
    gather_tick(10)
    att_saved = save(act.at[1], t_att)
    for copy in kv_saved + [q_saved]:
        copy.wait()
    k_sent.wait_send()
    v_sent.wait_send()
    pl.semaphore_signal(ready_c, inc=1, device_id=at.cp, device_id_type=MESH_IDS)
    ready(3)
    local_c.wait()
    links.copy(cot.at[1 - y], cs.at[1 - y], sx.at[7], rx.at[7], at.yp).wait_recv()

    for t in range(2):
        cols = slice(512 * t, 512 * t + 512)
        value = dot_nn(act[1].reshape(512, 1024), weight(3, cols)) + bias[0:1, 2048 + 512 * t : 2560 + 512 * t]
        gp[1, :, cols] = value.astype(BF)
        res[:, cols] = xs[:, :, cols].reshape(TOK, 512).astype(F32) + gate_attn[:, cols] * value
    ao_saved = save(gp.at[1], t_ao)
    gather_tick(11)
    for i in range(13):
        sums[i] = jnp.zeros((8, 1024), F32)

    def norm2(i, carry):
        rows = pl.ds(pl.multiple_of(i * RB, RB), RB)
        half, part = halves(i)
        n, _ = norm_rows(res[rows, :])
        m2[rows, :] = (n * scale_mlp + shift_mlp).astype(BF)
        low = (cs[half, part, :].astype(F32) * gate_mlp).astype(BF)
        gb[rows, :] = low
        sums[8] = sums[8] + fold(low.astype(F32))
        return carry

    lax.fori_loop(0, TOK // RB, norm2, 0)
    for copy in [x_saved, m1_saved, att_saved, ao_saved] + w_saved:
        copy.wait()
    for unit in (8, 9, 10, 11):
        ready(unit)
    gather_done(0)
    gather_done(1)

    def down_rows(j, u):
        return WD[j, u].reshape(1024, 256)

    def down_copies(u):
        return [
            links.copy(W8.at[1, pl.ds(2 * xi, 2), 1 - c], CR.at[u, xi], dcs.at[u, xi], dcr.at[u, xi], at.cp)
            for xi in range(2)
        ]

    def mlp(u):
        for t in range(2):
            cols = slice(512 * t, 512 * t + 512)
            first = 3072 + 1024 * u + 512 * t
            v = dot_nn(m2[...], weight(4 + u, cols)) + bias[0:1, first : first + 512]
            rows = jnp.concatenate([WD[j, u, t].reshape(512, 256) for j in range(4)], 1)
            slope = dot_nt(gb[...], rows)
            square = v * v
            th = jnp.tanh(ROOT_2_PI * v * (1.0 + 0.044715 * square))
            up = 0.5 + 0.5 * th
            act[0, :, :, :, :, :, cols] = rows512(v * up)
            low = (slope * (up + 0.5 * v * (1.0 - th * th) * (ROOT_2_PI + (ROOT_2_PI * 3 * 0.044715) * square))).astype(BF)
            gp[0, :, cols] = low
            sums[9 + u, :, cols] = fold(low.astype(F32))
        put_grad(u, 0, m2[...], lambda cols: gp[0, :, cols])
        slot_free(1)
        acts = act[0].reshape(512, 1024)
        for t in range(2):
            cols = slice(512 * t, 512 * t + 512)
            W8[1, :, :, :, :, :, cols] = dot_tn(acts, gb[:, cols]).astype(BF).reshape(4, 2, 2, 2, 32, 512)
        if u == 0:
            pl.semaphore_wait(ready_c, 1)
        cores_sent[1] = down_copies(u)
        for copy in cores_sent[1]:
            copy.start()
        for t in range(2):
            cols = slice(512 * t, 512 * t + 512)
            back = dot_nt(gp[0], W8[4 + u, 2 * t : 2 * t + 2].reshape(512, 1024))
            ahead = dot_nn(acts, jnp.concatenate([down_rows(2 * t, u), down_rows(2 * t + 1, u)], 1))
            acc[:, cols] = back if u == 0 else acc[:, cols] + back
            br[:, cols] = ahead if u == 0 else br[:, cols] + ahead

    def down_sum(u):
        for copy in down_copies(u):
            copy.wait_recv()

        def add(i, carry):
            xi, yi, a, b = i // 8, (i // 4) % 2, (i // 2) % 2, i % 2
            CR[u, xi, yi, a, b] = CR[u, xi, yi, a, b] + W8[1, 2 * xi + yi, c, a, b]
            return carry

        lax.fori_loop(0, 16, add, 0)

    for u in range(4):
        ready(4 + u)
        mlp(u)
        if u < 3:
            gather_tick(12 + u)
        tick()
        down_sum(u)
    waiting[4] = 1

    def output(i, carry):
        rows = pl.ds(pl.multiple_of(i * RB, RB), RB)
        half, part = halves(i)
        branch = br[rows, :] + bias[0:1, 7168:8192]
        sums[6] = sums[6] + fold(cs[half, part, :].astype(F32) * branch)
        xs[half, part, :] = (res[rows, :] + gate_mlp * branch).astype(BF)
        return carry

    lax.fori_loop(0, TOK // RB, output, 0)
    vec[6:7, :] = jnp.sum(sums[6], 0, keepdims=True)
    out_saved = save(xs.at[y], o_out.at[y])
    links.send(xs.at[1 - y], o_out.at[y], sx.at[10], rx.at[10], at.yp)
    for unit in (2, 3, 4, 5, 6, 7, 8, 9, 10, 11):
        gather_done(unit)
    load("ao", t_ao, gp.at[1])
    for j in range(4):
        cols = pl.ds(256 * j, 256)
        load(f"k{j}", t_k.at[:, :, :, :, :, :, cols], WD.at[j, 0])
        load(f"v{j}", t_v.at[:, :, :, :, :, :, cols], WD.at[j, 1])
        load(f"q{j}", t_q.at[:, :, :, :, :, cols], WD.at[j, 2, 0])
        load(f"att{j}", t_att.at[:, :, :, :, :, cols], WD.at[j, 2, 1])
    load("m1", t_m1, gp.at[0])
    load("wk", t_w.at[0], W8.at[4])
    load("wv", t_w.at[1], W8.at[5])

    loaded("ao")

    def norm2_back(i, carry):
        rows = pl.ds(pl.multiple_of(i * RB, RB), RB)
        half, part = halves(i)
        n, inv = norm_rows(res[rows, :])
        up = acc[rows, :]
        gn = up * n
        sums[3] = sums[3] + fold(up)
        sums[4] = sums[4] + fold(gn)
        g = up * scale_mlp
        total = cs[half, part, :].astype(F32) + (g - jnp.mean(g, -1, keepdims=True) - n * jnp.mean(gn * scale_mlp, -1, keepdims=True)) * inv
        acc[rows, :] = total
        sums[2] = sums[2] + fold(total * gp[1, rows, :].astype(F32))
        low = (total * gate_attn).astype(BF)
        gb[rows, :] = low
        sums[5] = sums[5] + fold(low.astype(F32))
        return carry

    lax.fori_loop(0, TOK // RB, norm2_back, 0)
    for half in range(2):
        load(f"x{half}", t_x.at[half], gp.at[1, pl.ds(256 * half, 256)])
    for t in range(2):
        value = dot_nt(gb[...], W8[3, 2 * t : 2 * t + 2].reshape(512, 1024)).astype(BF)
        for h in range(2):
            WD[2 * t + h, 3, 0] = value[:, 256 * h : 256 * h + 256].reshape(2, 2, 2, 2, 32, 256)
    tick()
    for j in range(4):
        for name in ("k", "v", "q", "att"):
            loaded(f"{name}{j}")

    def wide(a, b):
        return jnp.concatenate([WD[j, a, b].reshape(512, 256) for j in range(4)], 1)

    put_grad(8, 0, wide(2, 1), lambda cols: gb[:, cols])

    def attend_back(p, carry):
        j, cols = p // 2, pl.ds(pl.multiple_of((p % 2) * 128, 128), 128)
        full = pl.ds(pl.multiple_of(p * 128, 128), 128)
        k2, v2 = WD[j, 0, :, :, :, :, :, :, cols].reshape(1024, 128), WD[j, 1, :, :, :, :, :, :, cols].reshape(1024, 128)
        keys_sum, values_sum = None, None
        for t in range(2):
            rows = slice(256 * t, 256 * t + 256)
            q2, do2 = WD[j, 2, 0, t, :, :, :, :, cols].reshape(256, 128), WD[j, 3, 0, t, :, :, :, :, cols].reshape(256, 128)
            prod = (do2.astype(F32) * WD[j, 2, 1, t, :, :, :, :, cols].reshape(256, 128).astype(F32)).T
            queries = []
            for e in range(2):
                own = (lane < 64) == (e == 0)
                qe = jnp.where(own, q2, jnp.zeros_like(q2)) * BF(0.125)
                de = jnp.where(own, do2, jnp.zeros_like(do2))
                row_dot = jnp.sum(prod[64 * e : 64 * e + 64, :], 0, keepdims=True)
                probs = jnp.exp(dot_nt(k2, qe) - lse[p, e : e + 1, rows])
                grad_scores = (probs * (dot_nt(v2, de) - row_dot)).astype(BF)
                queries.append(dot_tn(grad_scores, k2))
                a, b = dot_nn(grad_scores, qe), dot_nn(probs.astype(BF), de)
                keys_sum = a if keys_sum is None else keys_sum + a
                values_sum = b if values_sum is None else values_sum + b
            grad_query = (jnp.where(lane < 64, queries[0], queries[1]) * 0.125).astype(BF)
            WD[j, 3, 1, t, :, :, :, :, cols] = grad_query.reshape(2, 2, 2, 32, 128)
        W8[6, :, :, :, :, :, full] = keys_sum.astype(BF).reshape(4, 2, 2, 2, 32, 128)
        W8[7, :, :, :, :, :, full] = values_sum.astype(BF).reshape(4, 2, 2, 2, 32, 128)
        return carry

    for first, release in ((0, 5), (2, 6), (4, 7)):
        lax.fori_loop(first, first + 2, attend_back, 0)
        waiting[release] = 1
        tick()
    lax.fori_loop(6, 8, attend_back, 0)
    waiting[8] = 1
    links.send(W8.at[6, pl.ds(2, 2)], act.at[0], sx.at[11], rx.at[11], at.cp)
    links.send(W8.at[7, pl.ds(2, 2)], act.at[1], sx.at[12], rx.at[12], at.cp)
    loaded("m1")
    loaded("wk")
    loaded("wv")
    grad_q = wide(3, 1)
    put_grad(9, 1, gp[0], lambda cols: grad_q[:, cols])
    del waiting[9]
    sums[6] = fold(grad_q.astype(F32))
    tick()
    waiting[9] = 1
    for own, came in ((6, 0), (7, 1)):
        links.copy(W8.at[own, pl.ds(2, 2)], act.at[came], sx.at[11 + came], rx.at[11 + came], at.cp).wait_recv()

        def join(i, carry):
            a, b = i // 2, i % 2
            W8[own, a, b] = W8[own, a, b] + act[came, a, b]
            return carry

        lax.fori_loop(0, 4, join, 0)

    grad_k, grad_v = W8[6, 0:2].reshape(512, 1024), W8[7, 0:2].reshape(512, 1024)
    sums[7] = fold(grad_v.astype(F32))
    for t in range(2):
        rows = slice(2 * t, 2 * t + 2)
        br[:, 512 * t : 512 * t + 512] = (
            dot_nt(grad_q, W8[2, rows].reshape(512, 1024)) + dot_nt(grad_k, W8[4, rows].reshape(512, 1024)) + dot_nt(grad_v, W8[5, rows].reshape(512, 1024))
        )
    loaded("x0")
    loaded("x1")

    def norm1_back(i):
        rows = pl.ds(pl.multiple_of(i * RB, RB), RB)
        n, inv = norm_rows(gp[1, rows, :].astype(F32))
        up = br[rows, :]
        gn = up * n
        sums[0] = sums[0] + fold(up)
        sums[1] = sums[1] + fold(gn)
        g = up * scale_attn
        return rows, acc[rows, :] + (g - jnp.mean(g, -1, keepdims=True) - n * jnp.mean(gn * scale_attn, -1, keepdims=True)) * inv

    per = 256 // RB

    def away(i, carry):
        _, value = norm1_back(i + (1 - y) * per)
        cs[0, pl.ds(pl.multiple_of(i * RB, RB), RB), :] = value.astype(BF)
        return carry

    def here(i, carry):
        rows, value = norm1_back(i + y * per)
        br[rows, :] = value
        return carry

    lax.fori_loop(0, per, away, 0)
    links.send(cs.at[0], cs.at[1], sx.at[13], rx.at[13], at.yp)
    lax.fori_loop(0, per, here, 0)
    save(br.at[pl.ds(pl.multiple_of(y * 256, 256), 256)], o_gl.at[y])
    tick()

    def put_kv(n, own, d):
        put_grad(n, d, gp[0], lambda cols: W8[own, 0:2, :, :, :, :, cols].reshape(512, 512))

    for i in range(6):
        value = vec[6:7, :] if i == 5 else jnp.sum(sums[i], 0, keepdims=True)
        for j in range(8):
            GS[8 * i + j : 8 * i + j + 1, :] = value[:, 128 * j : 128 * j + 128]
    links.send(GS, GP, sy.at[4], ry.at[4], at.cp)
    for line, i in enumerate((6, 7, 5, 9, 10, 11, 12, 8)):
        value = jnp.sum(sums[i], 0, keepdims=True)
        for j in range(8):
            BA[8 * line + j : 8 * line + j + 1, :] = value[:, 128 * j : 128 * j + 128]
    links.send(BA, BB.at[0], sy.at[5], ry.at[5], at.cp)
    put_kv(10, 6, 0)
    links.copy(GS, GP, sy.at[4], ry.at[4], at.cp).wait_recv()
    GM[y, z, x] = (GS[...] + GP[...]).astype(BF)
    mine = GM.at[y, z, x]
    for k in (1, 2, 3):
        links.send(mine, mine, sy.at[5 + k], ry.at[5 + k], at.z_to(k))
    tick()
    put_kv(11, 7, 1)
    links.copy(BA, BB.at[0], sy.at[5], ry.at[5], at.cp).wait_recv()
    BB[5] = BA[...] + BB[0]
    links.send(BB.at[5], BB.at[1], sy.at[9], ry.at[9], at.yp)
    for k in (1, 2, 3):
        ref = GM.at[y, at.z_from(k), x]
        links.copy(ref, ref, sy.at[5 + k], ry.at[5 + k], at.z_to(k)).wait_recv()
    ref = GM.at[y, :, x]
    for k, peer in ((10, at.xp), (12, at.yp), (0, at.xyp)):
        links.send(ref, ref, sy.at[k], ry.at[k], peer)
    tick()
    links.copy(BB.at[5], BB.at[1], sy.at[9], ry.at[9], at.yp).wait_recv()
    BB[6] = BB[5] + BB[1]
    links.send(BB.at[6], BB.at[2], sy.at[11], ry.at[11], at.xp)
    for ref, k, peer in ((GM.at[y, :, 1 - x], 10, at.xp), (GM.at[1 - y, :, x], 12, at.yp), (GM.at[1 - y, :, 1 - x], 0, at.xyp)):
        links.copy(ref, ref, sy.at[k], ry.at[k], peer).wait_recv()
    links.copy(BB.at[6], BB.at[2], sy.at[11], ry.at[11], at.xp).wait_recv()
    BB[7] = BB[6] + BB[2]
    bias_in = (BB.at[3], BB.at[4], BB.at[8])
    for k in (1, 2, 3):
        links.send(BB.at[7], bias_in[k - 1], sy.at[12 + k], ry.at[12 + k], at.z_to(k))
    tick()

    for m in range(2):
        for p in range(8):
            tile = GM[m, p // 2, p % 2].astype(F32)
            for j in range(48):
                first = 256 + 16 * (j // 8) + 8 * m + p
                acc[first : first + 1, 128 * (j % 8) : 128 * (j % 8) + 128] = tile[j : j + 1, :]
    cond = cact[...].astype(BF)
    part_sum = None
    for i in range(6):
        cols = slice(1024 * i, 1024 * i + 1024)
        values = acc[256 + 16 * i : 272 + 16 * i, :]
        low = values.astype(BF)
        brow[0:1, cols] = jnp.sum(values, 0, keepdims=True)
        spread = dot_tn(cond, low)
        acc[32 * i : 32 * i + 32, :] = (spread[0:32] + spread[32:64]) + (spread[64:96] + spread[96:128])
        save(acc.at[pl.ds(32 * i, 32)], o_mod.at[:, pl.ds(1024 * i, 1024)])
        term = dot_nt(low, wm[:, cols])
        part_sum = term if part_sum is None else part_sum + term
    save(brow, o_bmod)
    GCX[0] = jnp.where(lane // 32 == at.sq, jnp.concatenate([part_sum] * 4, 1), 0.0)
    to_row = ((1, 16, at.cp), (2, 17, at.yp), (3, 1, at.ycp))
    for k, sem, peer in to_row:
        links.send(GCX.at[0], GCX.at[k], sy.at[sem], ry.at[sem], peer)
    for k in (1, 2, 3):
        links.copy(BB.at[7], bias_in[k - 1], sy.at[12 + k], ry.at[12 + k], at.z_to(k)).wait_recv()
    bsum[...] = (BB[7] + BB[3]) + (BB[4] + BB[8])
    save(bsum, o_bias)
    tick()
    for k, sem, peer in to_row:
        links.copy(GCX.at[0], GCX.at[k], sy.at[sem], ry.at[sem], peer).wait_recv()
    GC[z, x] = (GCX[0] + GCX[1]) + (GCX[2] + GCX[3])
    mine = GC.at[z, x]
    for k in (1, 2, 3):
        links.send(mine, mine, sy.at[17 + k], ry.at[17 + k], at.z_to(k))
    for k in (1, 2, 3):
        ref = GC.at[at.z_from(k), x]
        links.copy(ref, ref, sy.at[17 + k], ry.at[17 + k], at.z_to(k)).wait_recv()
    links.send(GC.at[:, x], GC.at[:, x], sy.at[21], ry.at[21], at.xp)
    links.copy(cs.at[0], cs.at[1], sx.at[13], rx.at[13], at.yp).wait_recv()

    def widen(i, carry):
        rows = pl.ds(pl.multiple_of(i * RB, RB), RB)
        br[pl.ds(pl.multiple_of((1 - y) * 256 + i * RB, RB), RB), :] = cs[1, rows, :].astype(F32)
        return carry

    lax.fori_loop(0, per, widen, 0)
    save(br.at[pl.ds(pl.multiple_of((1 - y) * 256, 256), 256)], o_gl.at[1 - y])
    while waiting:
        tick()
    links.copy(GC.at[:, 1 - x], GC.at[:, 1 - x], sy.at[21], ry.at[21], at.xp).wait_recv()
    save(GC, o_gc)
    links.copy(xs.at[1 - y], o_out.at[1 - y], sx.at[10], rx.at[10], at.yp).wait_recv()
    slot_free(0)
    slot_free(1)
    for copy in fin_saved.values():
        copy.wait()
    links.drain()
    early = [id(copy) for copy in kv_saved + [q_saved, x_saved, m1_saved, att_saved, ao_saved] + w_saved]
    for copy in outgoing:
        if id(copy) not in early:
            copy.wait()


def run_block(lat, cot, cond, b_mod, b_qv, b_out, b_up, b_down, w_mod, w_qkv, w_out, w_up, w_down):
    S = jax.ShapeDtypeStruct
    V = pltpu.VMEM
    dma = pltpu.SemaphoreType.DMA
    regular = pltpu.SemaphoreType.REGULAR
    half = (2, 2, 2, 2, 32, 1024)
    outs = [
        S((2, 256, 1024), BF), S((2, 256, 1024), F32), S((32, 3072), F32), S((32, 1024), F32), S((32, 4096), F32), S((128, 1024), F32),
        S((32, 6144), F32), S((1, 6144), F32), S((64, 128), F32), S((4, 2, 16, 128), F32),
        S((2, 4, 2, 2, 2, 32, 1024), BF), S((2, 256, 1024), BF), S((512, 1024), BF), S(half, BF), S((2,) + half, BF), S((2,) + half, BF), S(half, BF),
        S((512, 1024), BF),
    ]
    scratch = [
        V((8, 4, 2, 2, 2, 32, 1024), BF), V((4, 4, 2, 2, 2, 2, 2, 32, 256), BF), V((4, 2, 2, 2, 2, 32, 1024), BF), V((4, 4, 2, 2, 32, 1024), BF),
        *[V(shape, BF) for step in LANDING for shape in step],
        V((2,) + half, BF), V((2, 512, 1024), BF), V((512, 1024), BF), V((512, 1024), BF), V((512, 1024), F32), V((512, 1024), F32), V((512, 1024), F32),
        V((2, 256, 1024), BF), V((2, 256, 1024), BF), V((3, 32, 1024), F32), V((8, 8, 512), F32),
        V((4, 2, 2, 2, 24, 128), F32), V((2, 4, 2, 48, 128), F32), V((4, 48, 128), F32), V((2, 4, 48, 128), F32), V((3, 48, 128), F32),
        V((48, 128), F32), V((48, 128), F32), V((32, 6144), BF), V((16, 128), F32), V((8, 1024), F32), V((1, 8192), F32), V((13, 8, 1024), F32),
        V((48, 128), F32), V((48, 128), F32), V((2, 4, 2, 48, 128), BF), V((64, 128), F32), V((64, 128), F32), V((9, 64, 128), F32),
        V((4, 2, 16, 128), F32), V((4, 16, 128), F32), V((1, 6144), F32),
        dma((7, 21)), dma((7, 21)), dma((12,)), dma((12,)), dma((LR, 21)), dma((LR, 21)), dma((12,)), dma((12,)), dma((4, 2)), dma((4, 2)),
        regular((7,)), regular((4,)), regular, dma((14,)), dma((14,)), dma((22,)), dma((22,)), dma((6,)), dma((6,)),
        dma((15,)), dma((22,)), dma((22,)), dma((3,)),
    ]
    return pl.pallas_call(
        block_kernel,
        out_shape=outs,
        in_specs=[ANY, ANY, VM, VM, VM, VM, VM, VM, ANY, ANY, ANY, ANY, ANY],
        out_specs=[ANY] * len(outs),
        scratch_shapes=scratch,
        compiler_params=pltpu.CompilerParams(collective_id=0, has_side_effects=True, vmem_limit_bytes=63 * 2**20),
        cost_estimate=pl.CostEstimate(flops=6 * 10**10, bytes_accessed=10**8, transcendentals=2 * 10**7),
    )(lat, cot, cond, b_mod, b_qv, b_out, b_up, b_down, w_mod, w_qkv, w_out, w_up, w_down.reshape(2, 2, 32, 1024))[:10]


def finish_kernel(h_out, h_gl, h_qkv, h_wo, h_up, h_dn, h_mod, bmod, bias, gcond, cond, o_out, o_gl, o_cond, o_mod, o_bmod, o_qkv, o_bqv, o_wo, o_bo, o_up, o_bu, o_dn, o_bd, v_out, v_gl, v_qkv, v_wo, v_up, v_dn, v_mod, sem_in, sem_out):
    ways = (
        (h_gl, v_gl, o_gl), (h_out, v_out, o_out), (h_mod, v_mod, o_mod), (h_up, v_up, o_up), (h_dn, v_dn, o_dn), (h_qkv, v_qkv, o_qkv), (h_wo, v_wo, o_wo),
    )
    into = [pltpu.make_async_copy(src, mid, sem_in.at[i]) for i, (src, mid, _) in enumerate(ways)]
    copies = [pltpu.make_async_copy(mid, dst, sem_out.at[i]) for i, (_, mid, dst) in enumerate(ways)]
    for copy in into:
        copy.start()
    for first, then in zip(into, copies):
        first.wait()
        then.start()
    dp, sq = lax.axis_index("dp"), lax.axis_index("seq")
    index = dp * (YN * CN) + sq

    def pick(values, row):
        return jnp.sum(jnp.where(lax.broadcasted_iota(jnp.int32, values.shape, 0) == row, values, 0.0), 0, keepdims=True)

    def lanes(row, size, at_):
        total = jnp.where(at_ == 0, row[:, 0:size], 0.0)
        for k in range(1, 128 // size):
            total = jnp.where(at_ == k, row[:, size * k : size * k + size], total)
        return total

    o_bqv[...] = lanes(pick(bias[0:16, :], index // 2), 64, lax.rem(index, 2))
    o_bo[...] = lanes(pick(bias[16:24, :], index // 4), 32, lax.rem(index, 4))
    o_bu[...] = pick(bias[24:56, :], index)
    o_bd[...] = lanes(pick(bias[56:64, :], index // 4), 32, lax.rem(index, 4))
    wide = bmod[0:1, pl.ds(pl.multiple_of((index // 2) * 384 + lax.rem(index, 2) * 128, 128), 256)]
    o_bmod[...] = jnp.where(lax.rem(index, 2) == 0, wide[:, 0:192], wide[:, 64:256])
    for m in range(2):
        for p in range(8):
            v = cond[m : m + 1, 128 * p : 128 * p + 128].astype(F32)
            gate = 1.0 / (1.0 + jnp.exp(-v))
            o_cond[m : m + 1, 128 * p : 128 * p + 128] = pick(gcond[p, 8 * m : 8 * m + 8, :], dp) * (gate * (1.0 + v * (1.0 - gate)))
    for copy in copies:
        copy.wait()


def per_device_kernels(latents, conditioning, w_mod, b_mod, w_qkv, b_qv, w_out, b_out, w_up, b_up, w_down, b_down, cotangent):
    cond = conditioning[:, 0]
    output, grad_lat, g_qkv, g_out, g_up, g_down, g_mod, gb_mod, gb_all, g_cond = run_block(
        latents[:, 0], cotangent[:, 0], cond, b_mod, b_qv, b_out, b_up, b_down, w_mod[0], w_qkv[0], w_out[0], w_up[0], w_down[0]
    )
    S = jax.ShapeDtypeStruct
    shapes = [
        S((2, 256, 1024), BF), S((2, 256, 1024), F32), S((2, 1024), F32), S((32, 6144), F32), S((1, 192), F32), S((32, 3072), F32), S((1, 64), F32),
        S((32, 1024), F32), S((1, 32), F32), S((32, 4096), F32), S((1, 128), F32), S((128, 1024), F32), S((1, 32), F32),
    ]
    (out, gl, gc, mod, bmod, qkv, bqv, wo, bo, up, bu, dn, bd) = pl.pallas_call(
        finish_kernel,
        out_shape=shapes,
        in_specs=[ANY] * 7 + [VM] * 4,
        out_specs=[ANY, ANY, VM, ANY, VM, ANY, VM, ANY, VM, ANY, VM, ANY, VM],
        scratch_shapes=[pltpu.VMEM(s.shape, s.dtype) for s in (output, grad_lat, g_qkv, g_out, g_up, g_down, g_mod)]
        + [pltpu.SemaphoreType.DMA((7,)), pltpu.SemaphoreType.DMA((7,))],
        cost_estimate=pl.CostEstimate(flops=10**6, bytes_accessed=10**7, transcendentals=2048),
    )(output, grad_lat, g_qkv, g_out, g_up, g_down, g_mod, gb_mod, gb_all, g_cond.reshape(8, 16, 128), cond)
    return (out[:, None], gl[:, None], gc[:, None], mod[None], bmod, qkv[None], bqv, wo[None], bo, up[None], bu, dn[None], bd)


def solution(mesh):
    placed = (
        P(None, "dp", "seq", None),
        P(None, "dp", None),
        P(None, ("dp", "seq"), None),
        P(None, ("dp", "seq")),
        P(None, ("dp", "seq"), None),
        P(None, ("dp", "seq")),
        P(None, ("dp", "seq"), None),
        P(None, ("dp", "seq")),
        P(None, ("dp", "seq"), None),
        P(None, ("dp", "seq")),
        P(None, ("dp", "seq"), None),
        P(None, ("dp", "seq")),
        P(None, "dp", "seq", None),
    )
    return jax.shard_map(
        per_device_kernels if dict(mesh.shape) == {"dp": 8, "seq": 4} else per_device,
        mesh=mesh,
        in_specs=placed,
        out_specs=(
            P(None, "dp", "seq", None),
            P(None, "dp", "seq", None),
            P(None, "dp", None),
            P(None, ("dp", "seq"), None),
            P(None, ("dp", "seq")),
            P(None, ("dp", "seq"), None),
            P(None, ("dp", "seq")),
            P(None, ("dp", "seq"), None),
            P(None, ("dp", "seq")),
            P(None, ("dp", "seq"), None),
            P(None, ("dp", "seq")),
            P(None, ("dp", "seq"), None),
            P(None, ("dp", "seq")),
        ),
        check_vma=False,
    )
```
